32 devices in a mesh: doc: 2 (over y), seg: 16 (over z, x, core).
Axes of the slice: x: 2, y: 2, z: 4, core: 2. Of those that a mesh axis runs over, the one named last changes fastest.
Arguments:
- tokens: bfloat16 [12, 2048, 768], P('doc', 'seg'), may hold values from -6 to 6
- token_mask: int32 [12, 2048], P('doc', 'seg'), may hold values from 0 to 1, as said below
- doc_lengths: int32 [2, 7], P('doc'), may hold values from 1 to 48, 96 in all within a row
- seg_qkv: bfloat16 [3, 768, 768], replicated, may hold values from -0.21875 to 0.21875
- seg_proj: bfloat16 [768, 768], replicated, may hold values from -1.25 to 1.25
- seg_up: bfloat16 [768, 3072], replicated, may hold values from -0.21875 to 0.21875
- seg_down: bfloat16 [3072, 768], replicated, may hold values from -0.109375 to 0.109375
- seg_bias: bfloat16 [3072], replicated, may hold values from -3 to 3
- seg_gains: bfloat16 [2, 768], replicated, may hold values from 0.5 to 1.5
- seg_shifts: bfloat16 [6, 768], replicated, may hold values from -3 to 3
- cross_qkv: bfloat16 [3, 768, 768], replicated, may hold values from -0.21875 to 0.21875
- cross_proj: bfloat16 [768, 768], replicated, may hold values from -1.25 to 1.25
- cross_up: bfloat16 [768, 3072], replicated, may hold values from -0.21875 to 0.21875
- cross_down: bfloat16 [3072, 768], replicated, may hold values from -0.109375 to 0.109375
- cross_bias: bfloat16 [3072], replicated, may hold values from -3 to 3
- cross_gains: bfloat16 [2, 768], replicated, may hold values from 0.5 to 1.5
- cross_shifts: bfloat16 [6, 768], replicated, may hold values from -3 to 3
- positions: bfloat16 [64, 768], replicated, may hold values from -3 to 3
- cotangent: bfloat16 [12, 2048, 768], P('doc', 'seg'), may hold values from -6 to 6
Outputs:
- mixed: bfloat16 [12, 2048, 768], P('doc', 'seg')
- input_grad: bfloat16 [12, 2048, 768], P('doc', 'seg')
- seg_qkv_grad: float32 [3, 768, 768], P(None, 'seg')
- seg_proj_grad: float32 [768, 768], P('seg')
- seg_up_grad: float32 [768, 3072], P('seg')
- seg_down_grad: float32 [3072, 768], P('seg')
- seg_bias_grad: float32 [3072], P('seg')
- seg_gains_grad: float32 [2, 768], P(None, 'seg')
- seg_shifts_grad: float32 [6, 768], P(None, 'seg')
- cross_qkv_grad: float32 [3, 768, 768], P(None, 'seg')
- cross_proj_grad: float32 [768, 768], P('seg')
- cross_up_grad: float32 [768, 3072], P('seg')
- cross_down_grad: float32 [3072, 768], P('seg')
- cross_bias_grad: float32 [3072], P('seg')
- cross_gains_grad: float32 [2, 768], P(None, 'seg')
- cross_shifts_grad: float32 [6, 768], P(None, 'seg')
- positions_grad: float32 [64, 768], P(None, 'seg')
The draws below stay inside these ranges and needn't reach their ends.
Inputs may be any that keep to these rules, and one draw needn't show every extreme that they name: `doc_lengths`: each row of a group sums to 96; one document of each group has exactly 48 segments. `token_mask`: in every segment the live tokens are a prefix of 32 tokens or more; the first token is always live.
All inputs are finite; a program needn't handle non-finite values.
Results may differ from the reference program's by a relative error of at most 0.023.
Values may be sent and summed in bfloat16 or wider, within the bound.
No kernel may reach another device: no remote copies, remote signals or barrier semaphores. Data moves between devices by JAX's collectives and lax.ppermute only.
A program may use at most 192 MiB of HBM per device.

```python
import math
import jax
import jax.numpy as jnp
import numpy as np
from jax import lax

D = 768
HEADS = 12
HD = 64
FF = 3072
SEGLEN = 128
MAXPOS = 64
SEG_DEV = 6
SEGS = 96
MAXSEG = 48
DOCS_G = 7
N_DOC = 2
N_SEG = 16


def draw_token_mask(key, part):
    key_whole, key_partial = jax.random.split(key)
    whole_seg = jax.random.randint(key_whole, (N_DOC * SEG_DEV, N_SEG), 0, 2)
    partial_value = jax.random.randint(key_partial, (N_DOC * SEG_DEV, N_SEG), SEGLEN // 4, SEGLEN + 1)
    live_len = jnp.where(whole_seg == 1, SEGLEN, partial_value)
    place_index = jnp.arange(SEGLEN, dtype=jnp.int32)
    live_tokens = (place_index[None, None, :] < live_len[:, :, None]).astype(jnp.int32)
    return live_tokens.reshape(N_DOC * SEG_DEV, N_SEG * SEGLEN)


def block_scale(rng, shape, shards, least, top_value):
    loudness, own = 1.0, jax.random.fold_in(rng, 6)
    for position, parts in shards:
        steps = jnp.exp(jax.random.uniform(jax.random.fold_in(own, position), (parts,), jnp.float32, least / len(shards), top_value / len(shards)))
        loudness = loudness * jnp.repeat(steps, shape[position] // parts).reshape([-1 if axis == position else 1 for axis in range(len(shape))])
    return loudness


def split_up(amount, total, most, slope):
    loads = [(1 << 20) // math.isqrt(grade ** slope) + 1 for grade in range(2, amount + 1)]
    spare, holding = total - most - (amount - 1), [1] * (amount - 1)
    while spare > 0:
        candidates = [i for i in range(amount - 1) if holding[i] < most]
        mass, left = sum([loads[i] for i in candidates]), spare
        for i in candidates:
            more = min(most - holding[i], max(1, left * loads[i] // mass), spare)
            holding[i] = holding[i] + more
            spare = spare - more
    return np.array([most] + holding)


def ragged(key, number_of, total, bound, skew):
    if number_of == 2:
        one = jax.random.randint(key, (), max(1, total - bound), min(bound, total - 1) + 1)
        return jnp.stack([one, total - one])
    sizes = jnp.asarray(split_up(number_of, total, bound, skew), jnp.int32)
    twos = (number_of - 1) // 2
    donor, sink = sizes[1:1 + 2 * twos:2], sizes[2:2 + 2 * twos:2]
    margin = jnp.minimum(donor - 1, bound - sink)
    passed = jax.random.randint(jax.random.fold_in(key, 1), (twos,), 0, 1 << 20) % (margin + 1)
    sizes = sizes.at[1:1 + 2 * twos:2].set(donor - passed).at[2:2 + 2 * twos:2].set(sink + passed)
    return sizes[jax.random.permutation(jax.random.fold_in(key, 2), number_of)]


def gaussian(own_key, dims, spread, most, shards=(), held_as=jnp.bfloat16):
    drawn = spread * jax.random.normal(own_key, dims, jnp.float32)
    if shards:
        drawn = drawn * block_scale(own_key, dims, shards, -0.22, 0.18)
    return jnp.clip(drawn, -most, most).astype(held_as)


def setup_inputs(seed: int = 0) -> dict:
    streams_of = jax.random.split(jax.random.key(seed), 20)
    tokens = gaussian(streams_of[0], (N_DOC * SEG_DEV, N_SEG * SEGLEN, D), 1.0, 6.0, ((0, 2), (1, 16)))
    token_mask = draw_token_mask(jax.random.fold_in(streams_of[19], 71), 0)
    doc_lengths = jax.vmap(lambda own: ragged(own, DOCS_G, SEGS, MAXSEG, 2))(jax.random.split(streams_of[2], N_DOC)).reshape((N_DOC, DOCS_G)).astype(jnp.int32)
    seg_qkv = gaussian(streams_of[3], (3, D, D), D ** -0.5, 0.21875)
    seg_proj = gaussian(streams_of[4], (D, D), (D // 32) ** -0.5, 1.25)
    seg_up = gaussian(streams_of[5], (D, FF), D ** -0.5, 0.21875)
    seg_down = gaussian(streams_of[6], (FF, D), FF ** -0.5, 0.109375)
    seg_bias = gaussian(streams_of[7], (FF,), 0.3, 3.0)
    seg_gains = jnp.clip(1.0 + 0.1 * jax.random.normal(streams_of[8], (2, D), jnp.float32), 0.5, 1.5).astype(jnp.bfloat16)
    seg_shifts = gaussian(streams_of[9], (6, D), 0.3, 3.0)
    cross_qkv = gaussian(streams_of[10], (3, D, D), D ** -0.5, 0.21875)
    cross_proj = gaussian(streams_of[11], (D, D), (D // 32) ** -0.5, 1.25)
    cross_up = gaussian(streams_of[12], (D, FF), D ** -0.5, 0.21875)
    cross_down = gaussian(streams_of[13], (FF, D), FF ** -0.5, 0.109375)
    cross_bias = gaussian(streams_of[14], (FF,), 0.3, 3.0)
    cross_gains = jnp.clip(1.0 + 0.1 * jax.random.normal(streams_of[15], (2, D), jnp.float32), 0.5, 1.5).astype(jnp.bfloat16)
    cross_shifts = gaussian(streams_of[16], (6, D), 0.3, 3.0)
    positions = gaussian(streams_of[17], (MAXPOS, D), 0.5, 3.0)
    cotangent = gaussian(streams_of[18], (N_DOC * SEG_DEV, N_SEG * SEGLEN, D), 1.0, 6.0, ((0, 2), (1, 16)))
    return dict(tokens=tokens, token_mask=token_mask, doc_lengths=doc_lengths, seg_qkv=seg_qkv, seg_proj=seg_proj, seg_up=seg_up, seg_down=seg_down, seg_bias=seg_bias, seg_gains=seg_gains, seg_shifts=seg_shifts, cross_qkv=cross_qkv, cross_proj=cross_proj, cross_up=cross_up, cross_down=cross_down, cross_bias=cross_bias, cross_gains=cross_gains, cross_shifts=cross_shifts, positions=positions, cotangent=cotangent)


precise = lax.Precision.HIGHEST

@jax.custom_vjp
def low(v):
    return lax.optimization_barrier(v.astype(jnp.bfloat16)).astype(jnp.float32)

@jax.custom_vjp
def low_back(v):
    return v

def low_keep(v):
    return (low(v), None)

def low_pass(kept, grad):
    return (grad,)

def back_keep(v):
    return (v, None)

def back_low(kept, grad):
    return (low(grad),)
low.defvjp(low_keep, low_pass)
low_back.defvjp(back_keep, back_low)

def product(left_op, right_op):
    return jnp.dot(left_op, right_op, precision=precise, preferred_element_type=jnp.float32)

def norm_rows(residual, gain_row, shift_row):
    center = residual - lax.optimization_barrier(jnp.mean(residual, axis=-1, keepdims=True))
    scaled = center * lax.rsqrt(lax.optimization_barrier(jnp.mean(center * center, axis=-1, keepdims=True)) + 1e-06)
    return scaled * gain_row + shift_row

def doc_layout(seg_lengths, seg_total):
    doc_ends = jnp.cumsum(seg_lengths).astype(jnp.int32)
    seg_index = jnp.arange(seg_total, dtype=jnp.int32)
    doc_of = lax.optimization_barrier(jnp.sum((seg_index[:, None] >= doc_ends[None, :]).astype(jnp.int32), axis=1))
    doc_starts = doc_ends - seg_lengths
    chosen = doc_of[:, None] == jnp.arange(seg_lengths.shape[0], dtype=jnp.int32)[None, :]
    seg_pos = seg_index - lax.optimization_barrier(jnp.sum(jnp.where(chosen, doc_starts[None, :], 0), axis=1))
    return (doc_of, seg_pos.astype(jnp.int32))

def attend(queries, keys_in, values, allowed):
    scores = jnp.einsum('brhd,bchd->bhrc', queries, keys_in, precision=precise)
    scores = low_back(jnp.where(allowed[:, None], scores, -1e+30))
    weights = low(jax.nn.softmax(scores, axis=-1))
    return jnp.einsum('bhrc,bchd->brhd', weights, values, precision=precise)

def block(rows_in, params, batches, allowed):
    w_qkv, w_proj, w_up, w_down, b_up, gains, shifts = params
    hidden_b = low(rows_in)
    queries = low(low_back((product(hidden_b, w_qkv[0]) + shifts[0]) * 0.125))
    keys_in = low(low_back(product(hidden_b, w_qkv[1])))
    values = low(low_back(product(hidden_b, w_qkv[2]) + shifts[1]))

    def heads_of(matrix):
        return matrix.reshape(batches, -1, HEADS, HD)
    attended = attend(heads_of(queries), heads_of(keys_in), heads_of(values), allowed).reshape(-1, D)
    attended_b = low(low_back(attended))
    branch = low_back(product(attended_b, w_proj) + shifts[2])
    first_out = norm_rows(rows_in + branch, gains[0], shifts[3])
    inner_pre = low_back(product(low(first_out), w_up) + b_up)
    activated = low(jax.nn.gelu(inner_pre, approximate=False))
    second = low_back(product(activated, w_down) + shifts[4])
    return norm_rows(first_out + second, gains[1], shifts[5])

def reference(tokens, token_mask, doc_lengths, seg_qkv, seg_proj, seg_up, seg_down, seg_bias, seg_gains, seg_shifts, cross_qkv, cross_proj, cross_up, cross_down, cross_bias, cross_gains, cross_shifts, positions, cotangent):
    seg_params = tuple((weight.astype(jnp.float32) for weight in (seg_qkv, seg_proj, seg_up, seg_down, seg_bias, seg_gains, seg_shifts)))
    cross_params = tuple((weight.astype(jnp.float32) for weight in (cross_qkv, cross_proj, cross_up, cross_down, cross_bias, cross_gains, cross_shifts)))
    table_f = positions.astype(jnp.float32)
    tok_groups = tokens.astype(jnp.float32).reshape(N_DOC, SEGS, SEGLEN, D)
    mask_groups = token_mask.reshape(N_DOC, SEGS, SEGLEN)
    cot_groups = cotangent.astype(jnp.float32).reshape(N_DOC, SEGS, SEGLEN, D)

    def one_group(running, group_in):
        tok_group, mask_group, len_group, cot_group = group_in
        doc_of, seg_pos = doc_layout(len_group, SEGS)
        allowed_seg = (mask_group > 0)[:, None, :]
        allowed_cross = (doc_of[:, None] == doc_of[None, :])[None]

        def forward(tok_in, seg_in, cross_in, table_in):
            seg_out = block(tok_in.reshape(-1, D), seg_in, SEGS, allowed_seg).reshape(SEGS, SEGLEN, D)
            cls_in = seg_out[:, 0, :] + table_in[seg_pos]
            cls_out = block(cls_in, cross_in, 1, allowed_cross)
            return seg_out.at[:, 0, :].set(cls_out)
        result, pullback = jax.vjp(forward, tok_group, seg_params, cross_params, table_f)
        grad_tok, grad_seg, grad_cross, grad_table = pullback(cot_group)
        running = jax.tree.map(jnp.add, running, (grad_seg, grad_cross, grad_table))
        return (running, (result.astype(jnp.bfloat16), grad_tok.astype(jnp.bfloat16)))
    start = jax.tree.map(jnp.zeros_like, (seg_params, cross_params, table_f))
    totals, outputs = lax.scan(one_group, start, (tok_groups, mask_groups, doc_lengths, cot_groups))
    seg_sum, cross_sum, table_sum = totals
    mixed = outputs[0].reshape(N_DOC * SEG_DEV, N_SEG * SEGLEN, D)
    input_grad = outputs[1].reshape(N_DOC * SEG_DEV, N_SEG * SEGLEN, D)
    return (mixed, input_grad, seg_sum[0], seg_sum[1], seg_sum[2], seg_sum[3], seg_sum[4], seg_sum[5], seg_sum[6], cross_sum[0], cross_sum[1], cross_sum[2], cross_sum[3], cross_sum[4], cross_sum[5], cross_sum[6], table_sum)
```

```python
import functools

import jax
import jax.numpy as jnp
from jax import lax
from jax.experimental import pallas as pl
from jax.experimental.pallas import tpu as pltpu
from jax.sharding import PartitionSpec as P

f32, bf16 = jnp.float32, jnp.bfloat16
VMEM_BYTES = 60 * 2**20
EPS = 1e-6
PAIR = 128
HD = 64


def nn(a, b):
    return lax.dot_general(a, b, (((1,), (0,)), ((), ())), preferred_element_type=f32)


def nt(a, b):
    return lax.dot_general(a, b, (((1,), (1,)), ((), ())), preferred_element_type=f32)


def tn(a, b):
    return lax.dot_general(a, b, (((0,), (0,)), ((), ())), preferred_element_type=f32)


def gelu_both(u):
    e = jnp.exp(u * u * -0.5)
    t = 1.0 / (jnp.abs(u) * (0.3275911 * 0.70710678118654752) + 1.0)
    poly = ((((0.5 * 1.061405429 * t + 0.5 * -1.453152027) * t + 0.5 * 1.421413741) * t + 0.5 * -0.284496736) * t
            + 0.5 * 0.254829592) * t
    tail = poly * e
    phi = jnp.where(u >= 0, 1.0 - tail, tail)
    return u * phi, phi + u * e * 0.39894228040143268


def norm(r):
    c = r - jnp.mean(r, axis=-1, keepdims=True)
    inv = lax.rsqrt(jnp.mean(c * c, axis=-1, keepdims=True) + EPS)
    return c * inv, inv


def norm_back(g, n, inv, gain):
    t = g * gain
    return inv * (t - jnp.mean(t, axis=-1, keepdims=True) - n * jnp.mean(t * n, axis=-1, keepdims=True))


def row_sum(x):
    return jnp.sum(x, axis=0, keepdims=True)


def halves(x):
    low = lax.broadcasted_iota(jnp.int32, x.shape, 1) < HD
    zero = jnp.zeros_like(x)
    return jnp.where(low, x, zero), jnp.where(low, zero, x)


def attn_fwd_kernel(tok, mask, wqkv, wo, gains, shifts, q_o, k_o, v_o, p_o, ob_o, n_o, inv_o):
    hb = tok[...]
    sh = shifts[...].astype(f32)
    q_o[...] = ((nn(hb, wqkv[0]) + sh[0:1]) * 0.125).astype(bf16)
    k_o[...] = nn(hb, wqkv[1]).astype(bf16)
    v_o[...] = (nn(hb, wqkv[2]) + sh[1:2]).astype(bf16)
    segs, pairs = p_o.shape[0], p_o.shape[1]
    L = tok.shape[0] // segs
    for s in range(segs):
        bias = jnp.where(mask[s] > 0, 0.0, -1e30).astype(f32)
        rows = slice(s * L, (s + 1) * L)
        for j in range(pairs):
            cols = slice(j * PAIR, (j + 1) * PAIR)
            k2 = jnp.concatenate(halves(k_o[rows, cols]), axis=0)
            v2 = jnp.concatenate(halves(v_o[rows, cols]), axis=0)
            sc = nt(q_o[rows, cols], k2)
            ps = []
            for e in range(2):
                t = sc[:, e * L:(e + 1) * L] + bias
                t = jnp.exp(t - jnp.max(t, axis=-1, keepdims=True))
                ps.append((t * (1.0 / jnp.sum(t, axis=-1, keepdims=True))).astype(bf16))
            pb = jnp.concatenate(ps, axis=1)
            p_o[s, j] = pb
            ob_o[rows, cols] = nn(pb, v2).astype(bf16)
    r1 = hb.astype(f32) + nn(ob_o[...], wo[...]) + sh[2:3]
    n, inv = norm(r1)
    n_o[...] = n
    inv_o[...] = inv


def attn_fwd(tok, mask, wqkv, wo, gains, shifts, segs_dev, step):
    T, D = tok.shape
    L = T // segs_dev
    pairs = D // PAIR
    B = L * step
    whole = lambda a: pl.BlockSpec(a.shape, lambda i, n=a.ndim: (0,) * n)
    rowblk = pl.BlockSpec((B, D), lambda i: (i, 0))
    return pl.pallas_call(
        attn_fwd_kernel,
        grid=(segs_dev // step,),
        in_specs=[rowblk, pl.BlockSpec((step, 1, L), lambda i: (i, 0, 0)), whole(wqkv), whole(wo), whole(gains), whole(shifts)],
        out_specs=[rowblk] * 3 + [pl.BlockSpec((step, pairs, L, 2 * L), lambda i: (i, 0, 0, 0)), rowblk, rowblk,
                   pl.BlockSpec((B, 1), lambda i: (i, 0))],
        out_shape=[jax.ShapeDtypeStruct((T, D), bf16)] * 3 + [jax.ShapeDtypeStruct((segs_dev, pairs, L, 2 * L), bf16),
                   jax.ShapeDtypeStruct((T, D), bf16), jax.ShapeDtypeStruct((T, D), f32), jax.ShapeDtypeStruct((T, 1), f32)],
        compiler_params=pltpu.CompilerParams(vmem_limit_bytes=VMEM_BYTES),
        name="seg_attention",
    )(tok, mask, wqkv, wo, gains, shifts)


def ffn_kernel(L, steps, n1, inv1, cot, wu, wd, bias, gains, shifts,
               mixed_o, gr1_o, gwu_o, gwd_o, gbias_o, small_o,
               y1b_s, acc_s, gb_s, dg_s, gm_s):
    i = pl.program_id(0)
    ga = gains[...].astype(f32)
    sh = shifts[...].astype(f32)

    @pl.when(i == 0)
    def _():
        y1 = n1[...] * ga[0:1] + sh[3:4]
        acc_s[...] = y1 + sh[4:5]
        y1b_s[...] = y1.astype(bf16)

    @pl.when(i < steps)
    def _():
        u = nn(y1b_s[...], wu[...]) + bias[...].astype(f32)
        g, d = gelu_both(u)
        gb = g.astype(bf16)
        gb_s[i] = gb
        dg_s[i] = d.astype(bf16)
        acc_s[...] += nn(gb, wd[...])

    @pl.when(i == steps - 1)
    def _():
        n2, inv2 = norm(acc_s[...])
        mixed_o[...] = (n2 * ga[1:2] + sh[5:6]).astype(bf16)
        row = lax.broadcasted_iota(jnp.int32, n2.shape, 0)
        gz = jnp.where(row % L == 0, 0.0, cot[...].astype(f32))
        small_o[0:1, :] = row_sum(gz * n2)
        small_o[1:2, :] = row_sum(gz)
        gr2 = norm_back(gz, n2, inv2, ga[1:2])
        gm = gr2.astype(bf16)
        gm_s[...] = gm
        small_o[2:3, :] = row_sum(gm.astype(f32))
        acc_s[...] = gr2

    @pl.when(i >= steps)
    def _():
        j = i - steps
        gm = gm_s[...]
        gwd_o[...] = tn(gb_s[j], gm).astype(bf16)
        gu = (nt(gm, wd[...]) * dg_s[j].astype(f32)).astype(bf16)
        gbias_o[...] = row_sum(gu.astype(f32))
        gwu_o[...] = tn(y1b_s[...], gu).astype(bf16)
        acc_s[...] += nt(gu, wu[...])

    @pl.when(i == 2 * steps - 1)
    def _():
        gy1 = acc_s[...]
        n = n1[...]
        small_o[3:4, :] = row_sum(gy1 * n)
        small_o[4:5, :] = row_sum(gy1)
        gr1_o[...] = norm_back(gy1, n, inv1[...], ga[0:1])


def ffn(n1, inv1, cot, wu, wd, bias, gains, shifts, L, chunk=384):
    T, D = n1.shape
    F = wu.shape[1]
    steps = F // chunk
    whole = lambda a: pl.BlockSpec(a.shape, lambda i, n=a.ndim: (0,) * n)
    wsh = lambda sh: pl.BlockSpec(sh, lambda i, n=len(sh): (0,) * n)
    late = lambda i: jnp.maximum(i - steps, 0)
    return pl.pallas_call(
        functools.partial(ffn_kernel, L, steps),
        grid=(2 * steps,),
        in_specs=[whole(n1), whole(inv1), whole(cot),
                  pl.BlockSpec((D, chunk), lambda i: (0, i % steps)), pl.BlockSpec((chunk, D), lambda i: (i % steps, 0)),
                  pl.BlockSpec((1, chunk), lambda i: (0, i % steps)), whole(gains), whole(shifts)],
        out_specs=[wsh((T, D)), wsh((T, D)), pl.BlockSpec((D, chunk), lambda i: (0, late(i))),
                   pl.BlockSpec((chunk, D), lambda i: (late(i), 0)), pl.BlockSpec((1, chunk), lambda i: (0, late(i))), wsh((8, D))],
        out_shape=[jax.ShapeDtypeStruct((T, D), bf16), jax.ShapeDtypeStruct((T, D), f32), jax.ShapeDtypeStruct((D, F), bf16),
                   jax.ShapeDtypeStruct((F, D), bf16), jax.ShapeDtypeStruct((1, F), f32), jax.ShapeDtypeStruct((8, D), f32)],
        scratch_shapes=[pltpu.VMEM((T, D), bf16), pltpu.VMEM((T, D), f32), pltpu.VMEM((steps, T, chunk), bf16),
                        pltpu.VMEM((steps, T, chunk), bf16), pltpu.VMEM((T, D), bf16)],
        compiler_params=pltpu.CompilerParams(vmem_limit_bytes=VMEM_BYTES),
        name="seg_ffn",
    )(n1, inv1, cot, wu, wd, bias, gains, shifts)


def attn_bwd_kernel(last, gr1, gr1c, p, q, k, v, ob, tok, wqkv, wo, gh_o, gw_o, small_o, gq_s, gk_s, gv_s, ga_s, go_s, ob_s, hb_s):
    i = pl.program_id(0)
    segs, pairs = p.shape[0], p.shape[1]
    B = gr1.shape[0]
    L = B // segs
    row = lax.broadcasted_iota(jnp.int32, (B, 1), 0)
    g1 = gr1[...]
    for s in range(segs):
        g1 = jnp.where(row == s * L, gr1c[s], g1)
    ga = g1.astype(bf16)
    base = pl.ds(i * B, B)
    ga_s[base, :] = ga
    ob_s[base, :] = ob[...]
    hb_s[base, :] = tok[...]
    go_s[...] = nt(ga, wo[...]).astype(bf16)
    for s in range(segs):
        rows = slice(s * L, (s + 1) * L)
        out = pl.ds(i * B + s * L, L)
        for j in range(pairs):
            cols = slice(j * PAIR, (j + 1) * PAIR)
            pb = p[s, j]
            pf = pb.astype(f32)
            g = go_s[rows, cols]
            v2 = jnp.concatenate(halves(v[rows, cols]), axis=0)
            k2 = jnp.concatenate(halves(k[rows, cols]), axis=0)
            q2 = jnp.concatenate(halves(q[rows, cols]), axis=0)
            g2 = jnp.concatenate(halves(g), axis=0)
            gp = nt(g, v2)
            gs = []
            for e in range(2):
                pe, ge = pf[:, e * L:(e + 1) * L], gp[:, e * L:(e + 1) * L]
                gs.append((pe * (ge - jnp.sum(pe * ge, axis=-1, keepdims=True))).astype(bf16))
            gq_s[out, cols] = nn(jnp.concatenate(gs, axis=1), k2).astype(bf16) * jnp.asarray(0.125, bf16)
            gk_s[out, cols] = tn(jnp.concatenate(gs, axis=0), q2).astype(bf16)
            gv_s[out, cols] = tn(jnp.concatenate([pb[:, :L], pb[:, L:]], axis=0), g2).astype(bf16)
    gq, gk, gv = gq_s[base, :], gk_s[base, :], gv_s[base, :]
    gh_o[...] = (g1 + nt(gq, wqkv[0]) + nt(gk, wqkv[1]) + nt(gv, wqkv[2])).astype(bf16)

    @pl.when(i == last)
    def _():
        for n, (a, b) in enumerate(((hb_s, gq_s), (hb_s, gk_s), (hb_s, gv_s), (ob_s, ga_s))):
            gw_o[n] = tn(a[...], b[...]).astype(bf16)
        for n, b in enumerate((gq_s, gv_s, ga_s)):
            small_o[n:n + 1, :] = row_sum(b[...].astype(f32))


def attn_bwd(gr1, gr1c, p, q, k, v, ob, tok, wqkv, wo, segs_dev, step):
    T, D = tok.shape
    L = T // segs_dev
    pairs = D // PAIR
    B = L * step
    n = segs_dev // step
    whole = lambda a: pl.BlockSpec(a.shape, lambda i, n=a.ndim: (0,) * n)
    wsh = lambda sh: pl.BlockSpec(sh, lambda i, n=len(sh): (0,) * n)
    rowblk = pl.BlockSpec((B, D), lambda i: (i, 0))
    return pl.pallas_call(
        functools.partial(attn_bwd_kernel, n - 1),
        grid=(n,),
        in_specs=[rowblk, pl.BlockSpec((step, 1, D), lambda i: (i, 0, 0)), pl.BlockSpec((step, pairs, L, 2 * L), lambda i: (i, 0, 0, 0)),
                  rowblk, rowblk, rowblk, rowblk, rowblk, whole(wqkv), whole(wo)],
        out_specs=[rowblk, wsh((4, D, D)), wsh((8, D))],
        out_shape=[jax.ShapeDtypeStruct((T, D), bf16), jax.ShapeDtypeStruct((4, D, D), bf16), jax.ShapeDtypeStruct((8, D), f32)],
        scratch_shapes=[pltpu.VMEM((T, D), bf16)] * 4 + [pltpu.VMEM((B, D), bf16)] + [pltpu.VMEM((T, D), bf16)] * 2,
        compiler_params=pltpu.CompilerParams(vmem_limit_bytes=VMEM_BYTES),
        name="seg_attention_back",
    )(gr1, gr1c, p, q, k, v, ob, tok, wqkv, wo)


def cross_kernel(r, member, rows_in, swu_h, swd_h, xqkv_h, xo_h, xu_h, xd_h, sbias, sgains, sshifts, xbias, xgains, xshifts, pos,
                 cls_o, gr1_o, gqkv_o, go_o, gu_o, gd_o, sgu_o, sgd_o, sbias_o, xbias_o, ssmall_o, xsmall_o, gpos_o,
                 swu, swd, xqkv, xo, xu, xd, sgb, sdg, xgb, xdg, sgu, xgu, q_s, k_s, v_s, p_s, o_s, go_s, gq_s, gk_s, gv_s, sems):
    srcs = (swu_h, swd_h, xqkv_h, xo_h, xu_h, xd_h)
    dsts = (swu, swd, xqkv, xo, xu, xd)
    copies = [pltpu.make_async_copy(a, b, sems.at[n]) for n, (a, b) in enumerate(zip(srcs, dsts))]
    for c in copies:
        c.start()
    D = swu.shape[0]
    F = swu.shape[1]
    R = rows_in.shape[0]
    chunks = [slice(c, c + D) for c in range(0, F, D)]
    pairs = [slice(c, c + PAIR) for c in range(0, D, PAIR)]
    sg, ss = sgains[...].astype(f32), sshifts[...].astype(f32)
    xg, xs = xgains[...].astype(f32), xshifts[...].astype(f32)
    eighth = jnp.asarray(0.125, bf16)

    def ffn_f(yb, wu, wd, bias, gb_s, dg_s):
        acc = 0.0
        for c in chunks:
            g, d = gelu_both(nn(yb, wu[:, c]) + bias[:, c].astype(f32))
            gb = g.astype(bf16)
            gb_s[:, c] = gb
            dg_s[:, c] = d.astype(bf16)
            acc = acc + nn(gb, wd[c, :])
        return acc

    def ffn_b(gm, wu, wd, dg_s, gu_s, bias_o):
        acc = 0.0
        for c in chunks:
            gu = (nt(gm, wd[c, :]) * dg_s[:, c].astype(f32)).astype(bf16)
            gu_s[:, c] = gu
            bias_o[0:1, c] = row_sum(gu.astype(f32))
            acc = acc + nt(gu, wu[:, c])
        return acc

    n1 = rows_in[:, :D]
    extra = rows_in[:, 2 * D:]
    did = extra[:, 0:1]
    spos = extra[:, 1:2].astype(jnp.int32)
    inv1 = extra[:, 2:3]
    lane = lax.broadcasted_iota(jnp.int32, (8, extra.shape[1]), 1)
    did_row = nt((lane == 0).astype(bf16), extra.astype(bf16))[0:1]
    allowed = did == did_row
    onehot = (lax.broadcasted_iota(jnp.int32, (R, pos.shape[0]), 1) == spos).astype(bf16)

    y1 = n1 * sg[0:1] + ss[3:4]
    y1b = y1.astype(bf16)
    copies[0].wait()
    copies[1].wait()
    n2, inv2 = norm(y1 + ffn_f(y1b, swu, swd, sbias, sgb, sdg) + ss[4:5])
    h = n2 * sg[1:2] + ss[5:6] + nn(onehot, pos[...])

    hb = h.astype(bf16)
    copies[2].wait()
    q_s[...] = ((nn(hb, xqkv[0]) + xs[0:1]) * 0.125).astype(bf16)
    k_s[...] = nn(hb, xqkv[1]).astype(bf16)
    v_s[...] = (nn(hb, xqkv[2]) + xs[1:2]).astype(bf16)
    for j, c in enumerate(pairs):
        q2, v2 = halves(q_s[:, c]), halves(v_s[:, c])
        out = 0.0
        for e in range(2):
            t = jnp.where(allowed, nt(q2[e], k_s[:, c]), -1e30)
            t = jnp.exp(t - jnp.max(t, axis=-1, keepdims=True))
            pb = (t * (1.0 / jnp.sum(t, axis=-1, keepdims=True))).astype(bf16)
            p_s[2 * j + e] = pb
            out = out + nn(pb, v2[e])
        o_s[:, c] = out.astype(bf16)
    copies[3].wait()
    m1, minv1 = norm(h + nn(o_s[...], xo[...]) + xs[2:3])
    z1 = m1 * xg[0:1] + xs[3:4]
    z1b = z1.astype(bf16)
    copies[4].wait()
    copies[5].wait()
    m2, minv2 = norm(z1 + ffn_f(z1b, xu, xd, xbias, xgb, xdg) + xs[4:5])
    cls_o[...] = m2 * xg[1:2] + xs[5:6]

    gz = rows_in[:, D:2 * D]
    xsmall_o[1:2, :] = row_sum(gz * m2)
    xsmall_o[7:8, :] = row_sum(gz)
    gr2 = norm_back(gz, m2, minv2, xg[1:2])
    xgm = gr2.astype(bf16)
    xsmall_o[6:7, :] = row_sum(xgm.astype(f32))
    gy1 = gr2 + ffn_b(xgm, xu, xd, xdg, xgu, xbias_o)
    xsmall_o[0:1, :] = row_sum(gy1 * m1)
    xsmall_o[5:6, :] = row_sum(gy1)
    gr1 = norm_back(gy1, m1, minv1, xg[0:1])
    xga = gr1.astype(bf16)
    xsmall_o[4:5, :] = row_sum(xga.astype(f32))
    go_s[...] = nt(xga, xo[...]).astype(bf16)
    for j, c in enumerate(pairs):
        q2, k2, v2, g2 = halves(q_s[:, c]), halves(k_s[:, c]), halves(v_s[:, c]), halves(go_s[:, c])
        gq = gk = gv = 0.0
        for e in range(2):
            pb = p_s[2 * j + e]
            pf = pb.astype(f32)
            gp = nt(g2[e], v_s[:, c])
            gs = (pf * (gp - jnp.sum(pf * gp, axis=-1, keepdims=True))).astype(bf16)
            gq = gq + nn(gs, k2[e])
            gk = gk + tn(gs, q2[e])
            gv = gv + tn(pb, g2[e])
        gq_s[:, c] = gq.astype(bf16) * eighth
        gk_s[:, c] = gk.astype(bf16)
        gv_s[:, c] = gv.astype(bf16)
    xsmall_o[2:3, :] = row_sum(gq_s[...].astype(f32))
    xsmall_o[3:4, :] = row_sum(gv_s[...].astype(f32))
    gcls = gr1 + nt(gq_s[...], xqkv[0]) + nt(gk_s[...], xqkv[1]) + nt(gv_s[...], xqkv[2])

    high = gcls.astype(bf16)
    gpos_o[...] = tn(onehot, high) + tn(onehot, (gcls - high.astype(f32)).astype(bf16))

    ssmall_o[...] = jnp.zeros_like(ssmall_o)
    ssmall_o[1:2, :] = row_sum(gcls * n2)
    ssmall_o[7:8, :] = row_sum(gcls)
    gr2 = norm_back(gcls, n2, inv2, sg[1:2])
    sgm = gr2.astype(bf16)
    ssmall_o[6:7, :] = row_sum(sgm.astype(f32))
    gy1 = gr2 + ffn_b(sgm, swu, swd, sdg, sgu, sbias_o)
    ssmall_o[0:1, :] = row_sum(gy1 * n1)
    ssmall_o[5:6, :] = row_sum(gy1)
    gr1_o[...] = norm_back(gy1, n1, inv1, sg[0:1])

    def own(x, n):
        pick = lax.broadcasted_iota(jnp.int32, (n, x.shape[1]), 0) + member[0] * n
        pick = (pick == lax.broadcasted_iota(jnp.int32, (n, x.shape[1]), 1)).astype(bf16)
        return nt(pick, x).astype(bf16)

    hbt = own(hb, r)
    gqkv_o[0] = nn(hbt, gq_s[...])
    gqkv_o[1] = nn(hbt, gk_s[...])
    gqkv_o[2] = nn(hbt, gv_s[...])
    go_o[...] = nn(own(o_s[...], r), xga)
    gu_o[...] = nn(own(z1b, r), xgu[...])
    gd_o[...] = nn(own(xgb[...], r * (F // D)), xgm)
    sgu_o[...] = nn(own(y1b, r), sgu[...])
    sgd_o[...] = nn(own(sgb[...], r * (F // D)), sgm)


def cross(member, rows_in, seg_params, cross_params, pos, r):
    swu, swd, sbias, sgains, sshifts = seg_params
    xqkv, xo, xu, xd, xbias, xgains, xshifts = cross_params
    R = rows_in.shape[0]
    D, F = swu.shape
    vm = pl.BlockSpec(memory_space=pltpu.VMEM)
    hbm = pl.BlockSpec(memory_space=pl.ANY)
    S = jax.ShapeDtypeStruct
    outs = [S((R, D), f32), S((R, D), f32), S((3, r, D), f32), S((r, D), f32), S((r, F), f32), S((r * (F // D), D), f32),
            S((r, F), f32), S((r * (F // D), D), f32), S((8, F), f32), S((8, F), f32), S((8, D), f32), S((8, D), f32),
            S((pos.shape[0], D), f32)]
    V = pltpu.VMEM
    return pl.pallas_call(
        functools.partial(cross_kernel, r),
        in_specs=[pl.BlockSpec(memory_space=pltpu.SMEM), vm] + [hbm] * 6 + [vm] * 7,
        out_specs=[vm] * len(outs),
        out_shape=outs,
        scratch_shapes=[V(swu.shape, bf16), V(swd.shape, bf16), V(xqkv.shape, bf16), V(xo.shape, bf16), V(xu.shape, bf16), V(xd.shape, bf16)]
        + [V((R, F), bf16)] * 6 + [V((R, D), bf16)] * 3 + [V((D // HD, R, R), bf16)] + [V((R, D), bf16)] * 5 + [pltpu.SemaphoreType.DMA((6,))],
        compiler_params=pltpu.CompilerParams(vmem_limit_bytes=VMEM_BYTES),
        name="cross_block",
    )(member, rows_in, swu, swd, xqkv, xo, xu, xd, sbias, sgains, sshifts, xbias, xgains, xshifts, pos)


def add_up(a, b):
    return (a.astype(f32) + b.astype(f32)).astype(bf16)


def at(x, i, axis):
    return lax.dynamic_index_in_dim(x, i, axis, keepdims=False)


def fold(pieces, members, member, order):
    bits = members.bit_length() - 1
    x = pieces.reshape((2,) * bits + pieces.shape[1:])
    left = list(range(bits - 1, -1, -1))
    for bit in order:
        axis = left.index(bit)
        left.pop(axis)
        mine = (member >> bit) & 1
        pairs = [(m, m ^ (1 << bit)) for m in range(members)]
        got = lax.ppermute(at(x, 1 - mine, axis), "seg", pairs)
        x = add_up(at(x, mine, axis), got)
    return x


def over_docs(x):
    docs = lax.axis_size("doc")
    total, part = x.astype(f32), x
    for _ in range(docs - 1):
        part = lax.ppermute(part, "doc", [(d, (d + 1) % docs) for d in range(docs)])
        total = total + part.astype(f32)
    return total


def shards(tokens, token_mask, doc_lengths, seg_qkv, seg_proj, seg_up, seg_down, seg_bias, seg_gains, seg_shifts,
           cross_qkv, cross_proj, cross_up, cross_down, cross_bias, cross_gains, cross_shifts, positions, cotangent):
    segs, L, D = tokens.shape
    F = seg_up.shape[1]
    members, member = lax.axis_size("seg"), lax.axis_index("seg")
    docs, doc = lax.axis_size("doc"), lax.axis_index("doc")
    r, wide = D // members, F // D
    T = segs * L
    tok = tokens.reshape(T, D)
    q, k, v, p, ob, n1, inv1 = attn_fwd(tok, token_mask[:, None, :], seg_qkv, seg_proj, seg_gains, seg_shifts, segs, 2)

    lengths = doc_lengths[0]
    here = jnp.arange(segs, dtype=jnp.int32) * members + member
    n_docs = lengths.shape[0]
    before = jnp.arange(n_docs)[:, None] <= jnp.arange(n_docs)[None, :]
    ends = jnp.sum(jnp.where(before, lengths[:, None], 0), axis=0)
    passed = here[:, None] >= ends[None, :]
    doc_of = jnp.sum(passed.astype(jnp.int32), axis=1)
    seg_pos = here - jnp.sum(jnp.where(passed, lengths[None, :], 0), axis=1)
    all_groups = docs * members * segs <= 256
    axes = ("doc", "seg") if all_groups else ("seg",)
    first = lambda x: x.reshape(segs, L, -1)[:, 0, :].astype(f32)
    extra = jnp.stack([(doc_of + doc * 32).astype(f32), seg_pos.astype(f32), inv1.reshape(segs, L)[:, 0]], axis=1)
    packed = jnp.concatenate([first(n1), first(cotangent), jnp.pad(extra, ((0, 0), (0, 125)))], axis=1)
    rows = lax.all_gather(packed, axes, axis=0, tiled=True)

    mixed, gr1, gwu, gwd, gbias, small = ffn(n1, inv1, cotangent.reshape(T, D), seg_up, seg_down, seg_bias[None], seg_gains, seg_shifts, L)

    got = cross(
        member.reshape(1), rows, (seg_up, seg_down, seg_bias[None], seg_gains, seg_shifts),
        (cross_qkv, cross_proj, cross_up, cross_down, cross_bias[None], cross_gains, cross_shifts), positions, r)
    cls_all, gr1_all, *sums = got
    if not all_groups:
        sums = [over_docs(s.astype(bf16)) for s in sums]
    gxqkv, gxo, gxu, gxd, gsu, gsd, sbias_c, xbias, ssmall_c, xsmall, gpos = sums
    place = (doc * members + member if all_groups else member) * segs
    own_rows = lambda x: lax.dynamic_slice_in_dim(x, place, segs, 0)
    cls_out, gr1c = own_rows(cls_all), own_rows(gr1_all)

    gh, gw, small_b = attn_bwd(gr1, gr1c[:, None, :], p, q, k, v, ob, tok, seg_qkv, seg_proj, segs, 2)

    piece_u = gwu.reshape(members, r, F)
    piece_d = gwd.reshape(members, r * wide, D)
    vectors = jnp.concatenate([gbias.reshape(wide, D), small[3:4], small[0:1], small_b[0:3], small[4:5], small[2:3], small[1:2],
                               jnp.zeros((16 - wide - 8, D), f32)], axis=0).astype(bf16)
    piece_a = jnp.concatenate([gw.reshape(4, members, r, D).transpose(1, 0, 2, 3).reshape(members, 4 * r, D),
                               jnp.broadcast_to(vectors[None], (members, 16, D))], axis=1)
    bits = members.bit_length() - 1
    up = list(range(bits))
    sum_d = over_docs(fold(piece_d, members, member, up))
    sum_u = over_docs(fold(piece_u, members, member, up))
    sum_a = over_docs(fold(piece_a, members, member, up))
    cut = lambda x, n: lax.dynamic_slice_in_dim(x, member * n, n, x.ndim - 1)
    vec = sum_a[4 * r:]
    vec_bias = vec[:wide].reshape(F) + sbias_c[0]
    vec_rest = vec[wide:wide + 8] + ssmall_c
    abc = sum_a[:4 * r].reshape(4, r, D)
    mixed = mixed.reshape(segs, L, D).at[:, 0, :].set(cls_out.astype(bf16))
    return (
        mixed, gh.reshape(segs, L, D),
        abc[:3], abc[3], sum_u + gsu, sum_d + gsd, cut(vec_bias, F // members), cut(vec_rest[:2], r), cut(vec_rest[2:], r),
        gxqkv, gxo, gxu, gxd, cut(xbias[0], F // members), cut(xsmall[:2], r), cut(xsmall[2:], r), cut(gpos, r),
    )


def solution(mesh):
    rows, seg, copied = P("doc", "seg", None), P("seg", None), P()
    grads = (P(None, "seg", None), seg, seg, seg, P("seg"), P(None, "seg"), P(None, "seg"))
    return jax.shard_map(
        shards,
        mesh=mesh,
        in_specs=(rows, P("doc", "seg"), P("doc", None)) + (copied,) * 15 + (rows,),
        out_specs=(rows, rows) + grads + grads + (P(None, "seg"),),
        check_vma=False,
    )
```

```python
import functools

import jax
import jax.numpy as jnp
from jax import lax
from jax.experimental import pallas as pl
from jax.experimental.pallas import tpu as pltpu
from jax.sharding import PartitionSpec as P

f32, bf16 = jnp.float32, jnp.bfloat16
VMEM_BYTES = 60 * 2**20
EPS = 1e-6
PAIR = 128
HD = 64
CHUNK = 768
TILE = 384
NEG = -1e30
SMALL_ROWS = 16

S = jax.ShapeDtypeStruct
V = pltpu.VMEM
VM = pl.BlockSpec(memory_space=pltpu.VMEM)
SM = pl.BlockSpec(memory_space=pltpu.SMEM)
ANY = pl.BlockSpec(memory_space=pl.ANY)
PARAMS = pltpu.CompilerParams(vmem_limit_bytes=VMEM_BYTES)


def cost(micros):
    return pl.CostEstimate(flops=int(micros * 1e9), bytes_accessed=int(micros * 3e6), transcendentals=0)


def nn(a, b):
    return lax.dot_general(a, b, (((1,), (0,)), ((), ())), preferred_element_type=f32)


def nt(a, b):
    return lax.dot_general(a, b, (((1,), (1,)), ((), ())), preferred_element_type=f32)


def tn(a, b):
    return lax.dot_general(a, b, (((0,), (0,)), ((), ())), preferred_element_type=f32)


def gelu_both(u):
    phi = lax.erf(u * 0.70710678118654752) * 0.5 + 0.5
    return u * phi, phi + u * (jnp.exp(u * u * -0.5) * 0.39894228040143268)


def norm(r):
    c = r - jnp.mean(r, axis=-1, keepdims=True)
    inv = lax.rsqrt(jnp.mean(c * c, axis=-1, keepdims=True) + EPS)
    return c * inv, inv


def norm_back(g, n, inv, gain):
    t = g * gain
    return inv * (t - jnp.mean(t, axis=-1, keepdims=True) - n * jnp.mean(t * n, axis=-1, keepdims=True))


def row_sum(x):
    return jnp.sum(x, axis=0, keepdims=True)


def halves(x):
    low = lax.broadcasted_iota(jnp.int32, x.shape, 1) < HD
    zero = jnp.zeros_like(x)
    return jnp.where(low, x, zero), jnp.where(low, zero, x)


def two(x):
    return jnp.concatenate(halves(x), axis=0)


def softmax(t):
    t = jnp.exp(t - jnp.max(t, axis=-1, keepdims=True))
    return (t * (1.0 / jnp.sum(t, axis=-1, keepdims=True))).astype(bf16)


def start_all(sems, *pairs):
    copies = [pltpu.make_async_copy(a, b, sems.at[n]) for n, (a, b) in enumerate(pairs)]
    for c in copies:
        c.start()
    return copies


def whole(a):
    return pl.BlockSpec(a.shape, lambda i, n=len(a.shape): (0,) * n)


def split_of(members, n, spread, D):
    per = n * D // members if spread else D // members
    return None if per % 16 or TILE % (2 * per) else (per, D // (2 * per) if spread else 0)


def grad_outs(members, n, spread, D, extra=0):
    split = split_of(members, n, spread, D)
    if not split:
        return [S((n, D, D), bf16)], [V((n, D, D), bf16), pltpu.SemaphoreType.DMA((n, 2))]
    per, step = split
    rows = per if spread else n * per
    return [S((members // 2, rows + extra, D), bf16)] * 2, [V((n, D // (2 * per), 2, per, D), bf16), pltpu.SemaphoreType.DMA((n, 2))]


def turned(m, bits):
    return m if bits < 2 else (m & ~3) | ((m & 1) << 1) | ((m >> 1) & 1)


def emit_grads(split, core, left, right, outs, stage, sems):
    n, D = stage.shape[0], stage.shape[-1]
    bits = outs[0].shape[0].bit_length() - 1

    def copies(j):
        if not split:
            return [pltpu.make_async_copy(stage.at[j], outs[0].at[j], sems.at[j, 0])]
        per, step = split
        res = []
        for k in range(stage.shape[1]):
            m = j * step + k if step else k
            theirs, ours = jnp.where(core == 1, m, turned(m, bits)), jnp.where(core == 0, m, turned(m, bits))
            rows = pl.ds(0, per) if step else pl.ds(j * per, per)
            res += [pltpu.make_async_copy(stage.at[j, k, 1 - core], outs[0].at[theirs, rows], sems.at[j, 0]),
                    pltpu.make_async_copy(stage.at[j, k, core], outs[1].at[ours, rows], sems.at[j, 1])]
        return res

    for j in range(n):
        for t in range(D // TILE):
            res = tn(left(j, slice(t * TILE, (t + 1) * TILE)), right(j)).astype(bf16)
            if split:
                k = TILE // (2 * split[0])
                stage[j, t * k:(t + 1) * k] = res.reshape((k, 2, split[0], D))
            else:
                stage[j, t * TILE:(t + 1) * TILE, :] = res
        for x in copies(j):
            x.start()

    def end():
        for j in range(n):
            for x in copies(j):
                x.wait()

    return end


def forward_kernel(n_docs, split, n_grads, meta, lengths, tok, cot, mask, wqkv_h, wo_h, wu_h, wd_h, bias, gains, shifts, *rest):
    (q_o, k_o, v_o, p_o, ob_o, n_o, inv_o, y1b_o, dg_o, gm_o, gr2_o, mixed_o, pack_o, small_o), rest = rest[:14], rest[14:]
    grads, (wqkv, wo, wu, wd, gb_s, gm_s, sems, stage, gsems) = rest[:n_grads], rest[n_grads:]
    i = pl.program_id(0)
    segs, pairs = p_o.shape[0], p_o.shape[1]
    B, D = tok.shape
    L = B // segs
    n = wu.shape[0]
    ga, sh = gains[...].astype(f32), shifts[...].astype(f32)
    cs = [slice(c * CHUNK, (c + 1) * CHUNK) for c in range(n)]
    load = lambda a, b, m: pltpu.make_async_copy(a, b, sems.at[m])
    first = [load(wqkv_h, wqkv, 0), load(wo_h, wo, 1)]
    ups = [load(wu_h.at[:, c], wu.at[j], 2 + j) for j, c in enumerate(cs)]
    downs = [load(wd_h.at[c, :], wd.at[j], 2 + n + j) for j, c in enumerate(cs)]

    @pl.when(i == 0)
    def _():
        for c in first + ups + downs:
            c.start()
        small_o[...] = jnp.zeros_like(small_o)
        first[0].wait()

    hb = tok[...]
    q_o[...] = ((nn(hb, wqkv[0]) + sh[0:1]) * 0.125).astype(bf16)
    k_o[...] = nn(hb, wqkv[1]).astype(bf16)
    v_o[...] = (nn(hb, wqkv[2]) + sh[1:2]).astype(bf16)
    col = [slice(j * PAIR, (j + 1) * PAIR) for j in range(pairs)]
    for s in range(segs):
        rows = slice(s * L, (s + 1) * L)
        live = jnp.where(mask[pl.ds(i * segs + s, 1), :] > 0, 0.0, NEG).astype(f32)
        scores = [nt(q_o[rows, c], two(k_o[rows, c])) for c in col]
        probs = [jnp.concatenate([softmax(t[:, e:e + L] + live) for e in (0, L)], axis=1) for t in scores]
        for j, c in enumerate(col):
            p_o[s, j] = probs[j]
            ob_o[rows, c] = nn(probs[j], two(v_o[rows, c])).astype(bf16)

    @pl.when(i == 0)
    def _():
        for c in first[1:] + ups + downs:
            c.wait()

    n1, inv1 = norm(hb.astype(f32) + nn(ob_o[...], wo[...]) + sh[2:3])
    n_o[...] = n1
    inv_o[...] = inv1
    y1 = n1 * ga[0:1] + sh[3:4]
    y1b_o[...] = y1.astype(bf16)
    up = lambda j: nn(y1b_o[...], wu[j]) + bias[:, cs[j]].astype(f32)
    here = pl.ds(pl.multiple_of(i * B, B), B)
    u, acc = up(0), y1 + sh[4:5]
    for j in range(n):
        after = up(j + 1) if j + 1 < n else None
        g, d = gelu_both(u)
        gb = g.astype(bf16)
        gb_s[j, here, :] = gb
        dg_o[j] = d.astype(bf16)
        acc = acc + nn(gb, wd[j])
        u = after
    n2, inv2 = norm(acc)
    mixed_o[...] = (n2 * ga[1:2] + sh[5:6]).astype(bf16)
    row = lax.broadcasted_iota(jnp.int32, n2.shape, 0)
    gz = jnp.where(row % L == 0, 0.0, cot[...].astype(f32))
    small_o[0:1, :] += row_sum(gz * n2)
    small_o[1:2, :] += row_sum(gz)
    gr2 = norm_back(gz, n2, inv2, ga[1:2])
    gr2_o[...] = gr2
    gm = gr2.astype(bf16)
    gm_o[...] = gm
    gm_s[here, :] = gm
    small_o[2:3, :] += row_sum(gm.astype(f32))

    lane = lax.broadcasted_iota(jnp.int32, (1, 128), 1)
    for s in range(segs):
        g = (i * segs + s) * meta[2] + meta[0]
        before, doc, pos = jnp.int32(0), meta[1] * 32, g
        for d in range(n_docs):
            before = before + lengths[0, d]
            passed = g >= before
            doc = doc + passed.astype(jnp.int32)
            pos = jnp.where(passed, g - before, pos)
        extra = jnp.where(lane == 0, doc, jnp.where(lane == 1, pos, 0)).astype(f32)
        top = slice(s * L, s * L + 1)
        high = inv1[top].astype(bf16).astype(f32)
        extra = jnp.where(lane == 2, high, jnp.where(lane == 3, inv1[top] - high, extra))
        pack_o[s, :, :D] = n1[top].astype(bf16)
        pack_o[s, :, D:2 * D] = cot[s * L:s * L + 16, :][0:1]
        pack_o[s, :, 2 * D:] = extra.astype(bf16)

    @pl.when(i == pl.num_programs(0) - 1)
    def _():
        emit_grads(split, meta[3], lambda j, c: gb_s[j, :, c], lambda j: gm_s[...], grads, stage, gsems)()


def forward(meta, lengths, tok, cot, mask, wqkv, wo, wu, wd, bias, gains, shifts, members, step=2):
    T, D = tok.shape
    segs_dev, L = mask.shape
    pairs, B, n = D // PAIR, L * step, wu.shape[1] // CHUNK
    rowblk = pl.BlockSpec((B, D), lambda i: (i, 0))
    wide = pl.BlockSpec((n, B, CHUNK), lambda i: (0, i, 0))
    row = lambda dt: (S((T, D), dt), rowblk)
    outs = [row(bf16), row(bf16), row(bf16),
            (S((segs_dev, pairs, L, 2 * L), bf16), pl.BlockSpec((step, pairs, L, 2 * L), lambda i: (i, 0, 0, 0))),
            row(bf16), row(f32), (S((T, 1), f32), pl.BlockSpec((B, 1), lambda i: (i, 0))), row(bf16), (S((n, T, CHUNK), bf16), wide),
            row(bf16), row(f32), row(bf16),
            (S((segs_dev, 1, 2 * D + 128), bf16), pl.BlockSpec((step, 1, 2 * D + 128), lambda i: (i, 0, 0))),
            (S((8, D), f32), whole(S((8, D), f32)))]
    grads, scratch = grad_outs(members, n, True, D)
    return pl.pallas_call(
        functools.partial(forward_kernel, lengths.shape[1], split_of(members, n, True, D), len(grads)),
        grid=(segs_dev // step,),
        in_specs=[SM, SM, rowblk, rowblk, whole(mask), ANY, ANY, ANY, ANY, whole(bias), whole(gains), whole(shifts)],
        out_specs=[o[1] for o in outs] + [ANY] * len(grads),
        out_shape=[o[0] for o in outs] + grads,
        scratch_shapes=[V(wqkv.shape, bf16), V(wo.shape, bf16), V((n, D, CHUNK), bf16), V((n, CHUNK, D), bf16), V((n, T, CHUNK), bf16),
                        V((T, D), bf16), pltpu.SemaphoreType.DMA((2 + 2 * n,))] + scratch,
        compiler_params=PARAMS,
        name="seg_forward", cost_estimate=cost(30),
    )(meta, lengths, tok, cot, mask, wqkv, wo, wu, wd, bias, gains, shifts)


def ffn_back_kernel(split, n_grads, meta, n1, inv1, y1b, dg, gm, gr2, wu_h, wd_h, gains, gr1_o, gbias_o, small_o, *rest):
    grads, (wu, wd, y1b_s, gu_s, sems, stage, gsems) = rest[:n_grads], rest[n_grads:]
    i = pl.program_id(0)
    n = wu.shape[0]
    B = n1.shape[0]
    cs = [slice(c * CHUNK, (c + 1) * CHUNK) for c in range(n)]
    ups = [pltpu.make_async_copy(wu_h.at[:, c], wu.at[j], sems.at[0, j]) for j, c in enumerate(cs)]
    downs = [pltpu.make_async_copy(wd_h.at[c, :], wd.at[j], sems.at[1, j]) for j, c in enumerate(cs)]

    @pl.when(i == 0)
    def _():
        for j in range(n):
            downs[j].start()
            ups[j].start()
        small_o[...] = jnp.zeros_like(small_o)
        gbias_o[...] = jnp.zeros_like(gbias_o)

    def await_first(*copies):
        @pl.when(i == 0)
        def _():
            for c in copies:
                c.wait()

    here = pl.ds(pl.multiple_of(i * B, B), B)
    y1b_s[here, :] = y1b[...]
    await_first(downs[0])
    t, acc = nt(gm[...], wd[0]), gr2[...]
    for j in range(n):
        await_first(ups[j], *downs[j + 1:j + 2])
        after = nt(gm[...], wd[j + 1]) if j + 1 < n else None
        gu = (t * dg[j].astype(f32)).astype(bf16)
        gu_s[j, here, :] = gu
        gbias_o[j:j + 1, :] += row_sum(gu.astype(f32))
        acc = acc + nt(gu, wu[j])
        t = after
    n1v = n1[...]
    small_o[0:1, :] += row_sum(acc * n1v)
    small_o[1:2, :] += row_sum(acc)
    gr1_o[...] = norm_back(acc, n1v, inv1[...], gains[...].astype(f32)[0:1])

    @pl.when(i == pl.num_programs(0) - 1)
    def _():
        emit_grads(split, meta[3], lambda j, c: y1b_s[:, c], lambda j: gu_s[j], grads, stage, gsems)()


def ffn_back(meta, n1, inv1, y1b, dg, gm, gr2, wu, wd, gains, members, B=256):
    T, D = n1.shape
    n = wu.shape[1] // CHUNK
    rowblk = pl.BlockSpec((B, D), lambda i: (i, 0))
    grads, scratch = grad_outs(members, n, False, D)
    shapes = [S((T, D), f32), S((8, CHUNK), f32), S((8, D), f32)]
    return pl.pallas_call(
        functools.partial(ffn_back_kernel, split_of(members, n, False, D), len(grads)),
        grid=(T // B,),
        in_specs=[SM, rowblk, pl.BlockSpec((B, 1), lambda i: (i, 0)), rowblk, pl.BlockSpec((n, B, CHUNK), lambda i: (0, i, 0)), rowblk, rowblk,
                  ANY, ANY, whole(gains)],
        out_specs=[rowblk, whole(shapes[1]), whole(shapes[2])] + [ANY] * len(grads),
        out_shape=shapes + grads,
        scratch_shapes=[V((n, D, CHUNK), bf16), V((n, CHUNK, D), bf16), V((T, D), bf16), V((n, T, CHUNK), bf16),
                        pltpu.SemaphoreType.DMA((2, n))] + scratch,
        compiler_params=PARAMS,
        name="seg_ffn_back", cost_estimate=cost(20),
    )(meta, n1, inv1, y1b, dg, gm, gr2, wu, wd, gains)


def attn_back_kernel(split, n_grads, is_last, meta, *rest):
    if is_last:
        (base_gh, first_v, small_f, small_b, sums_a, gbias, ga_in), rest = rest[:7], rest[7:]
    else:
        (gr1, gr1c, ob), rest = rest[:3], rest[3:]
    (p, q, k, v, tok, wqkv, wo), rest = rest[:7], rest[7:]
    if is_last:
        (gh_o, vec_o), rest = rest[:2], rest[2:]
    else:
        (gh_o, ga_o, first_v_o, sums_o), rest = rest[:4], rest[4:]
    grads, rest = rest[:n_grads], rest[n_grads:]
    go_s, g_s, left_s, sums, rest = *rest[:4], rest[4:]
    if is_last:
        vec_s, wsems, rest = *rest[:2], rest[2:]
    stage, gsems = rest
    i = pl.program_id(0)
    segs, pairs = p.shape[0], p.shape[1]
    B, D = tok.shape
    L, H = B // segs, pairs * PAIR
    here = pl.ds(pl.multiple_of(i * B, B), B)

    @pl.when(i == 0)
    def _():
        sums[...] = jnp.zeros_like(sums)

    left_s[0, here, :] = tok[...]
    if is_last:
        acc, ga = base_gh[...], ga_in[...]
    else:
        row = lax.broadcasted_iota(jnp.int32, (B, 1), 0)
        acc = gr1[...]
        for s in range(segs):
            acc = jnp.where(row == s * L, gr1c[s], acc)
        ga = acc.astype(bf16)
        ga_o[...] = ga
        g_s[1, here, :] = ga
        left_s[1, here, :] = ob[...]
    go_s[...] = nt(ga, wo[...]).astype(bf16)
    col = [slice(j * PAIR, (j + 1) * PAIR) for j in range(pairs)]
    beside = lambda c: slice(H + c.start, H + c.stop)
    eighth = jnp.asarray(0.125, bf16)
    for s in range(segs):
        rows = slice(s * L, (s + 1) * L)
        out = pl.ds(pl.multiple_of(i * B, B) + s * L, L)
        gps = [nt(go_s[rows, c], two(v[rows, c])) for c in col]
        for j, c in enumerate(col):
            pb = p[s, j]
            gv = tn(jnp.concatenate([pb[:, :L], pb[:, L:]], axis=0), two(go_s[rows, c])).astype(bf16)
            if is_last:
                g_s[1, out, beside(c)] = gv
            else:
                first_v_o[rows, c] = gv
        gss = []
        for j, gp in enumerate(gps):
            pf = p[s, j].astype(f32)
            gs = []
            for e in (0, L):
                pe, ge = pf[:, e:e + L], gp[:, e:e + L]
                gs.append((pe * (ge - jnp.sum(pe * ge, axis=-1, keepdims=True))).astype(bf16))
            gss.append(gs)
        for c, gs in zip(col, gss):
            g_s[0, out, c] = nn(jnp.concatenate(gs, axis=1), two(k[rows, c])).astype(bf16) * eighth
            g_s[0, out, beside(c)] = tn(jnp.concatenate(gs, axis=0), two(q[rows, c])).astype(bf16)
    if is_last:
        g_s[1, here, :H] = first_v[...]
        gv = g_s[1, here, H:]
    else:
        gv = first_v_o[...]
    gq, gk = g_s[0, here, :H], g_s[0, here, H:]
    gh_o[...] = (acc + nt(gq, wqkv[0]) + nt(gk, wqkv[1]) + nt(gv, wqkv[2])).astype(gh_o.dtype)
    for m in range(2):
        sums[m:m + 1, :] += row_sum(g_s[m, here, :].astype(f32))

    @pl.when(i == pl.num_programs(0) - 1)
    def _():
        tail = []
        if is_last:
            vec = jnp.concatenate([
                gbias[0:4, :], small_b[0:1, :], small_f[0:1, :], jnp.concatenate([sums_a[0:1, :H], sums[0:1, :H]], axis=1), sums[1:2, :],
                sums_a[1:2, :], small_b[1:2, :], small_f[2:3, :], small_f[1:2, :], jnp.zeros((4, D), f32)], axis=0)
            vec_o[...] = vec
            if split:
                for m in range(vec_s.shape[0]):
                    vec_s[m] = vec.astype(bf16)
                tail = [pltpu.make_async_copy(vec_s, h.at[:, pl.ds(h.shape[1] - SMALL_ROWS, SMALL_ROWS)], wsems.at[m]) for m, h in enumerate(grads)]
        else:
            sums_o[...] = sums[...]
        for x in tail:
            x.start()
        emit_grads(split, meta[3], lambda j, c: left_s[0 if is_last else j, :, c], lambda j: g_s[j], grads, stage, gsems)()
        for x in tail:
            x.wait()


def attn_back(meta, before_it, p, q, k, v, tok, wqkv, wo, members, is_last, step=2):
    T, D = tok.shape
    segs_dev, all_pairs, L = p.shape[:3]
    pairs, H, half = all_pairs // 2, D // 2, int(is_last)
    B = L * step
    rowblk = pl.BlockSpec((B, D), lambda i: (i, 0))
    halfblk = pl.BlockSpec((B, H), lambda i: (i, half))
    firstblk = pl.BlockSpec((B, H), lambda i: (i, 0))
    split = split_of(members, 2, False, D)
    grads, scratch = grad_outs(members, 2, False, D, SMALL_ROWS if is_last else 0)
    small = S((8, D), f32)
    if is_last:
        vec = S((SMALL_ROWS, D), f32)
        specs = [rowblk, firstblk] + [whole(x) for x in before_it[2:6]] + [rowblk]
        outs = [(S((T, D), bf16), rowblk), (vec, whole(vec))]
        more = [V((members // 2, SMALL_ROWS, D), bf16), pltpu.SemaphoreType.DMA((2,))]
    else:
        specs = [rowblk, pl.BlockSpec((step, 1, D), lambda i: (i, 0, 0)), rowblk]
        outs = [(S((T, D), f32), rowblk), (S((T, D), bf16), rowblk), (S((T, H), bf16), firstblk), (small, whole(small))]
        more = []
    return pl.pallas_call(
        functools.partial(attn_back_kernel, split, len(grads), is_last),
        grid=(segs_dev // step,),
        in_specs=[SM] + specs + [pl.BlockSpec((step, pairs, L, 2 * L), lambda i: (i, half, 0, 0)), halfblk, halfblk, halfblk, rowblk,
                                 pl.BlockSpec((3, D, H), lambda i: (0, 0, half)), pl.BlockSpec((H, D), lambda i: (half, 0))],
        out_specs=[o[1] for o in outs] + [ANY] * len(grads),
        out_shape=[o[0] for o in outs] + grads,
        scratch_shapes=[V((B, H), bf16), V((2, T, D), bf16), V((2, T, D), bf16), V((8, D), f32)] + more + scratch,
        compiler_params=PARAMS,
        name="seg_attention_back", cost_estimate=cost(12),
    )(meta, *before_it, p, q, k, v, tok, wqkv, wo)


def onehot(rows, width, start):
    at = lax.broadcasted_iota(jnp.int32, (rows, width), 0) + start
    return (at == lax.broadcasted_iota(jnp.int32, (rows, width), 1)).astype(bf16)


def nt_exact(x, pick):
    a = x.astype(bf16)
    rest = x - a.astype(f32)
    b = rest.astype(bf16)
    return nt(a, pick) + nt(b, pick) + nt((rest - b.astype(f32)).astype(bf16), pick)


def own_vectors(vec, member, r, F):
    D = vec.shape[1]
    wide = F // D
    per = r * wide
    fits = D // per
    parts = nt_exact(vec, onehot(per, D, lax.rem(member, fits) * per))
    line = lax.broadcasted_iota(jnp.int32, parts.shape, 0)
    bias = row_sum(jnp.where(line == lax.div(member, fits), parts, 0.0))
    rest = nt_exact(vec, onehot(r, D, member * r))
    return bias, rest[wide:wide + 2], rest[wide + 2:wide + 8]


def cross_kernel(r, meta, rows_in, mixed_h, swu_h, swd_h, xqkv_h, xo_h, xu_h, xd_h, sbias, sgains, sshifts, xbias, xgains, xshifts, pos,
                 mixed_o, gr1_o, svec_o, gqkv_o, go_o, gu_o, gd_o, gbias_o, ggains_o, gshifts_o, gpos_o, sgu_o, sgd_o,
                 swu, swd, xqkv, xo, xu, xd, sgb, sdg, xgb, xdg, sgu, xgu, q_s, k_s, v_s, p_s, o_s, go_s, gq_s, gk_s, gv_s,
                 cls_s, gr1_s, vec_s, svec_s, patch, sems, psems):
    n, D = swu.shape[0], swu.shape[1]
    R = rows_in.shape[0]
    cs = [slice(c * CHUNK, (c + 1) * CHUNK) for c in range(n)]
    col = [slice(c, c + PAIR) for c in range(0, D, PAIR)]
    queue = []
    for wu_h, wd_h, wu, wd in ((swu_h, swd_h, swu, swd), (xu_h, xd_h, xu, xd)):
        for j, c in enumerate(cs):
            queue += [(wu_h.at[:, c], wu.at[j]), (wd_h.at[c, :], wd.at[j])]
    queue[2 * n:2 * n] = [(xqkv_h.at[m], xqkv.at[m]) for m in range(3)] + [(xo_h, xo)]
    copies = [pltpu.make_async_copy(a, b, sems.at[m]) for m, (a, b) in enumerate(queue)]
    ahead, waited = 6, [0]
    for x in copies[:ahead]:
        x.start()

    def need(count):
        for _ in range(count):
            m = waited[0]
            copies[m].wait()
            if m + ahead < len(copies):
                copies[m + ahead].start()
            waited[0] = m + 1

    segs, L = patch.shape[0], mixed_h.shape[0] // patch.shape[0]
    fetch = [pltpu.make_async_copy(mixed_h.at[pl.ds(s * L, 16), :], patch.at[s], psems.at[s]) for s in range(segs)]
    for x in fetch:
        x.start()
    sg, ss = sgains[...].astype(f32), sshifts[...].astype(f32)
    xg, xs = xgains[...].astype(f32), xshifts[...].astype(f32)
    eighth = jnp.asarray(0.125, bf16)

    def ffn_f(acc, yb, wu, wd, bias, gb_s, dg_s):
        def up(j):
            need(1)
            return nn(yb, wu[j]) + bias[:, cs[j]].astype(f32)

        for j in range(n):
            g, d = gelu_both(up(j))
            gb = g.astype(bf16)
            gb_s[:, cs[j]] = gb
            dg_s[:, cs[j]] = d.astype(bf16)
            need(1)
            acc = acc + nn(gb, wd[j])
        return acc

    def ffn_b(acc, gm, wu, wd, dg_s, gu_s, vec):
        t = nt(gm, wd[0])
        for j in range(n):
            after = nt(gm, wd[j + 1]) if j + 1 < n else None
            gu = (t * dg_s[:, cs[j]].astype(f32)).astype(bf16)
            gu_s[:, cs[j]] = gu
            vec[j:j + 1, :] = row_sum(gu.astype(f32))
            acc = acc + nt(gu, wu[j])
            t = after
        return acc

    vec_s[...] = jnp.zeros_like(vec_s)
    svec_s[...] = jnp.zeros_like(svec_s)
    n1 = rows_in[:, :D].astype(f32)
    extra = rows_in[:, 2 * D:].astype(f32)
    spos = extra[:, 1:2].astype(jnp.int32)
    inv1 = extra[:, 2:3] + extra[:, 3:4]
    lane = lax.broadcasted_iota(jnp.int32, (8, extra.shape[1]), 1)
    did_row = nt((lane == 0).astype(bf16), extra.astype(bf16))[0:1]
    allowed = extra[:, 0:1] == did_row
    placed = (lax.broadcasted_iota(jnp.int32, (R, pos.shape[0]), 1) == spos).astype(bf16)

    y1 = n1 * sg[0:1] + ss[3:4]
    y1b = y1.astype(bf16)
    n2, inv2 = norm(ffn_f(y1 + ss[4:5], y1b, swu, swd, sbias, sgb, sdg))
    h = n2 * sg[1:2] + ss[5:6] + nn(placed, pos[...])

    hb = h.astype(bf16)
    need(1)
    q_s[...] = ((nn(hb, xqkv[0]) + xs[0:1]) * 0.125).astype(bf16)
    need(1)
    k_s[...] = nn(hb, xqkv[1]).astype(bf16)
    need(1)
    v_s[...] = (nn(hb, xqkv[2]) + xs[1:2]).astype(bf16)
    early = R <= 256
    pair_scores = lambda c: [nt(x, k_s[:, c]) for x in halves(q_s[:, c])]
    scores = [pair_scores(c) for c in col] if early else None
    for j, c in enumerate(col):
        out, v2 = 0.0, halves(v_s[:, c])
        sc = scores[j] if early else pair_scores(c)
        for e in range(2):
            pb = softmax(jnp.where(allowed, sc[e], NEG))
            p_s[2 * j + e] = pb
            out = out + nn(pb, v2[e])
        o_s[:, c] = out.astype(bf16)
    need(1)
    m1, minv1 = norm(h + nn(o_s[...], xo[...]) + xs[2:3])
    z1 = m1 * xg[0:1] + xs[3:4]
    z1b = z1.astype(bf16)
    m2, minv2 = norm(ffn_f(z1 + xs[4:5], z1b, xu, xd, xbias, xgb, xdg))
    cls_s[...] = m2 * xg[1:2] + xs[5:6]

    gz = rows_in[:, D:2 * D].astype(f32)
    vec_s[n + 1:n + 2, :] = row_sum(gz * m2)
    vec_s[n + 7:n + 8, :] = row_sum(gz)
    gr2 = norm_back(gz, m2, minv2, xg[1:2])
    xgm = gr2.astype(bf16)
    vec_s[n + 6:n + 7, :] = row_sum(xgm.astype(f32))
    gy1 = ffn_b(gr2, xgm, xu, xd, xdg, xgu, vec_s)
    vec_s[n:n + 1, :] = row_sum(gy1 * m1)
    vec_s[n + 5:n + 6, :] = row_sum(gy1)
    gr1 = norm_back(gy1, m1, minv1, xg[0:1])
    xga = gr1.astype(bf16)
    vec_s[n + 4:n + 5, :] = row_sum(xga.astype(f32))
    go_s[...] = nt(xga, xo[...]).astype(bf16)
    pair_gps = lambda c: [nt(x, v_s[:, c]) for x in halves(go_s[:, c])]
    gps = [pair_gps(c) for c in col] if early else None
    for j, c in enumerate(col):
        gpj = gps[j] if early else pair_gps(c)
        q2, k2, g2 = halves(q_s[:, c]), halves(k_s[:, c]), halves(go_s[:, c])
        gq = gk = gv = 0.0
        for e in range(2):
            pb = p_s[2 * j + e]
            pf = pb.astype(f32)
            gp = gpj[e]
            gs = (pf * (gp - jnp.sum(pf * gp, axis=-1, keepdims=True))).astype(bf16)
            gq = gq + nn(gs, k2[e])
            gk = gk + tn(gs, q2[e])
            gv = gv + tn(pb, g2[e])
        gq_s[:, c] = gq.astype(bf16) * eighth
        gk_s[:, c] = gk.astype(bf16)
        gv_s[:, c] = gv.astype(bf16)
    vec_s[n + 2:n + 3, :] = row_sum(gq_s[...].astype(f32))
    vec_s[n + 3:n + 4, :] = row_sum(gv_s[...].astype(f32))
    gcls = gr1 + nt(gq_s[...], xqkv[0]) + nt(gk_s[...], xqkv[1]) + nt(gv_s[...], xqkv[2])

    svec_s[n + 1:n + 2, :] = row_sum(gcls * n2)
    svec_s[n + 7:n + 8, :] = row_sum(gcls)
    gr2 = norm_back(gcls, n2, inv2, sg[1:2])
    sgm = gr2.astype(bf16)
    svec_s[n + 6:n + 7, :] = row_sum(sgm.astype(f32))
    gy1 = ffn_b(gr2, sgm, swu, swd, sdg, sgu, svec_s)
    svec_s[n:n + 1, :] = row_sum(gy1 * n1)
    svec_s[n + 5:n + 6, :] = row_sum(gy1)
    gr1_s[...] = norm_back(gy1, n1, inv1, sg[0:1])
    svec_o[...] = svec_s[...]

    for x in fetch:
        x.wait()
    top = lax.broadcasted_iota(jnp.int32, (16, 1), 0) == 0
    for s in range(segs):
        line = pl.ds(meta[4] + s, 1)
        gr1_o[s] = gr1_s[line, :]
        patch[s] = jnp.where(top, cls_s[line, :], patch[s].astype(f32)).astype(bf16)
    store = [pltpu.make_async_copy(patch.at[s], mixed_o.at[pl.ds(s * L, 16), :], psems.at[s]) for s in range(segs)]
    for x in store:
        x.start()

    member = meta[0]
    pick = onehot(r, D, member * r)
    own = lambda x: nt(pick, x).astype(bf16)
    pick_wide = onehot(r * n, n * D, member * r * n)
    own_wide = lambda x: nt(pick_wide, x).astype(bf16)
    hbt = own(hb)
    for m, g in enumerate((gq_s, gk_s, gv_s)):
        gqkv_o[m] = nn(hbt, g[...])
    go_o[...] = nn(own(o_s[...]), xga)
    gd_o[...] = nn(own_wide(xgb[...]), xgm)
    sgd_o[...] = nn(own_wide(sgb[...]), sgm)
    z1t, y1t = own(z1b), own(y1b)
    for c in cs:
        gu_o[:, c] = nn(z1t, xgu[:, c])
        sgu_o[:, c] = nn(y1t, sgu[:, c])
    bias, gains, shifts = own_vectors(vec_s[...], member, r, n * D)
    gbias_o[...] = bias
    ggains_o[...] = gains
    gshifts_o[...] = shifts
    gown = nt_exact(gcls, pick)
    high = gown.astype(bf16)
    gpos_o[...] = tn(placed, high) + tn(placed, (gown - high.astype(f32)).astype(bf16))
    for x in store:
        x.wait()


def cross(meta, rows_in, mixed, seg_params, cross_params, pos, segs, r):
    swu, swd, sbias, sgains, sshifts = seg_params
    xqkv, xo, xu, xd, xbias, xgains, xshifts = cross_params
    R = rows_in.shape[0]
    D, F = swu.shape
    n = F // CHUNK
    outs = [S(mixed.shape, bf16), S((segs, 1, D), f32), S((SMALL_ROWS, D), f32), S((3, r, D), f32), S((r, D), f32), S((r, F), f32),
            S((r * n, D), f32), S((1, r * n), f32), S((2, r), f32), S((6, r), f32), S((pos.shape[0], r), f32), S((r, F), f32), S((r * n, D), f32)]
    up, down, row = V((n, D, CHUNK), bf16), V((n, CHUNK, D), bf16), V((R, D), bf16)
    return pl.pallas_call(
        functools.partial(cross_kernel, r),
        in_specs=[SM, VM] + [ANY] * 7 + [VM] * 7,
        out_specs=[ANY] + [VM] * (len(outs) - 1),
        out_shape=outs,
        scratch_shapes=[up, down, V(xqkv.shape, bf16), V(xo.shape, bf16), up, down] + [V((R, F), bf16)] * 6 + [row] * 3
        + [V((D // HD, R, R), bf16)] + [row] * 5 + [V((R, D), f32)] * 2 + [V((SMALL_ROWS, D), f32)] * 2
        + [V((segs, 16, D), bf16), pltpu.SemaphoreType.DMA((4 * n + 4,)), pltpu.SemaphoreType.DMA((segs,))],
        input_output_aliases={2: 0},
        compiler_params=PARAMS,
        name="cross_block", cost_estimate=cost(28),
    )(meta, rows_in, mixed, swu, swd, xqkv, xo, xu, xd, sbias, sgains, sshifts, xbias, xgains, xshifts, pos)


def finish_kernel(r, F, routed, meta, *rest):
    ins, (w_o, o_o, bias_o, gains_o, shifts_o) = rest[:-5], rest[-5:]
    if routed:
        lower = meta[1] == 0
        totals = []
        for x, other in (ins[0:2], ins[2:4]):
            a, b = x[...].astype(f32), other[...].astype(f32)
            totals.append(jnp.concatenate([jnp.where(lower, a, b), jnp.where(lower, b, a)], axis=0))
    else:
        totals = [ins[0][...], ins[1][...]]
    a, b = totals
    H = a.shape[1] // 2
    for m in range(2):
        w_o[m] = jnp.concatenate([a[:r, m * H:(m + 1) * H], b[:r, m * H:(m + 1) * H]], axis=1)
    w_o[2] = b[r:2 * r]
    o_o[...] = a[r:2 * r]
    bias, gains, shifts = own_vectors(b[2 * r:] + ins[-1][...], meta[0], r, F)
    bias_o[...] = bias
    gains_o[...] = gains
    shifts_o[...] = shifts


def finish(meta, parts, vec_c, r, F, routed):
    D = vec_c.shape[1]
    outs = [S((3, r, D), f32), S((r, D), f32), S((1, r * (F // D)), f32), S((2, r), f32), S((6, r), f32)]
    return pl.pallas_call(
        functools.partial(finish_kernel, r, F, routed), in_specs=[SM] + [VM] * (len(parts) + 1), out_specs=[VM] * len(outs), out_shape=outs,
        compiler_params=PARAMS, name="finish", cost_estimate=cost(2),
    )(meta, *parts, vec_c)


def add_up(a, b):
    return (a.astype(f32) + b.astype(f32)).astype(bf16)


def at(x, i, axis):
    return lax.dynamic_index_in_dim(x, i, axis, keepdims=False)


def fold(pieces, members, member):
    bits = members.bit_length() - 1
    x = pieces.reshape((2,) * bits + pieces.shape[1:])
    for bit in range(bits):
        axis = bits - 1 - bit
        mine = (member >> bit) & 1
        got = lax.ppermute(at(x, 1 - mine, axis), "seg", [(m, m ^ (1 << bit)) for m in range(members)])
        x = add_up(at(x, mine, axis), got)
    return x


def over_docs(x):
    docs = lax.axis_size("doc")
    total, part = x.astype(f32), x
    for _ in range(docs - 1):
        part = lax.ppermute(part, "doc", [(d, (d + 1) % docs) for d in range(docs)])
        total = total + part.astype(f32)
    return total


class Routed:
    def __init__(self, send, keep):
        self.members, member = lax.axis_size("seg"), lax.axis_index("seg")
        self.core, self.number = member & 1, lax.axis_index("doc") * self.members + member
        self.x, self.rows, self.steps = keep, send.shape[1], 0
        self.send = send

    def exchange(self, x, by_core):
        return lax.ppermute(x, ("doc", "seg"), [(m, m ^ by_core[m & 1]) for m in range(2 * self.members)])

    def bit_of(self, mask):
        return ((self.number & mask) != 0).astype(jnp.int32)

    def halve(self, axis, by_core):
        bit = jnp.where(self.core == 0, self.bit_of(by_core[0]), self.bit_of(by_core[1]))
        got = self.exchange(at(self.x, 1 - bit, axis), by_core)
        self.x = add_up(at(self.x, bit, axis), got)

    def step(self, count=1):
        X, Z0, Z1, Y = 2, 4, 8, self.members
        for _ in range(count):
            if self.steps == 0:
                x = add_up(self.x, self.exchange(self.send, (1, 1)))
                self.x = x.reshape(2, 2, 2, 2, self.rows // 2, -1)
            elif self.steps == 1:
                self.halve(2, (X, Z0))
            elif self.steps == 2:
                b = jnp.where(self.core == 0, self.bit_of(Z0), self.bit_of(X))
                y = self.bit_of(Y)
                part = lambda i, h: at(at(self.x, i, 1), h, 1)
                got = [self.exchange(part(1 - b, y), (Z0, X)), self.exchange(part(b, 1 - y), (Y, Y)),
                       self.exchange(part(1 - b, 1 - y), (Z0 + Y, X + Y))]
                total = part(b, y).astype(f32)
                for g in got:
                    total = total + g.astype(f32)
                self.x = total.astype(bf16)
            elif self.steps == 3:
                self.halve(0, (Z1, Z1))
            else:
                self.x = (self.x, self.exchange(self.x, (Y, Y)))
            self.steps += 1
        return self.x


def before(x, *others):
    vals = [f.x if isinstance(f, Routed) else f for f in others]
    res = lax.optimization_barrier((x, *vals))
    for f, v in zip(others, res[1:]):
        if isinstance(f, Routed):
            f.x = v
    return res[0]


def meet(*folds):
    for f, v in zip(folds, lax.optimization_barrier(tuple(f.x for f in folds))):
        f.x = v


def join(x, other):
    a, b = x.astype(f32), other.astype(f32)
    lower = lax.axis_index("doc") == 0
    return jnp.concatenate([jnp.where(lower, a, b), jnp.where(lower, b, a)], axis=0)


def trade(x, mask):
    members = lax.axis_size("seg")
    return lax.ppermute(x, ("doc", "seg"), [(m, m ^ mask) for m in range(2 * members)])


def gather_start(x):
    Z1, Y = 8, lax.axis_size("seg")
    near, far, both = trade(x, Z1), trade(x, Y), trade(x, Y + Z1)
    mine, theirs = jnp.stack([x, near]), jnp.stack([far, both])
    lower = lax.axis_index("doc") == 0
    return jnp.stack([jnp.where(lower, mine, theirs), jnp.where(lower, theirs, mine)])


def gather_middle(x):
    X, Z0 = 2, 4
    return jnp.concatenate([x, trade(x, X), trade(x, Z0), trade(x, X + Z0)], axis=1)


def gather_end(x):
    return jnp.concatenate([x, trade(x, 1)], axis=1)


def shards(tokens, token_mask, doc_lengths, seg_qkv, seg_proj, seg_up, seg_down, seg_bias, seg_gains, seg_shifts,
           cross_qkv, cross_proj, cross_up, cross_down, cross_bias, cross_gains, cross_shifts, positions, cotangent):
    segs, L, D = tokens.shape
    F = seg_up.shape[1]
    members, member = lax.axis_size("seg"), lax.axis_index("seg")
    docs, doc = lax.axis_size("doc"), lax.axis_index("doc")
    r, wide, T = D // members, F // D, segs * L
    all_groups = docs * members * segs <= 256
    few = members == 16 and docs == 2
    place = (doc * members if few else doc * members + member if all_groups else member) * segs
    meta = jnp.stack([member, doc, jnp.int32(members), member & 1, place]).astype(jnp.int32)
    tok, cot = tokens.reshape(T, D), cotangent.reshape(T, D)
    bias, xbias = seg_bias[None], cross_bias[None]

    q, k, v, p, ob, n1, inv1, y1b, dg, gm, gr2, mixed, pack, small_f, *gw_d = forward(
        meta, doc_lengths, tok, cot, token_mask, seg_qkv, seg_proj, seg_up, seg_down, bias, seg_gains, seg_shifts, members)
    routed = few and len(gw_d) == 2
    pack = pack.reshape(segs, -1)
    if few:
        pack = gather_start(pack)
    if routed:
        gm = before(gm, pack)
    gr1, gbias, small_b, *gw_u = ffn_back(meta, n1, inv1, y1b, dg, gm, gr2, seg_up, seg_down, seg_gains, members)
    if few:
        rows = gather_middle(pack)
    if routed:
        fold_d = Routed(*gw_d)
        fold_d.step()
        gw_u[0], rows = before(gw_u[0], fold_d, rows), rows
        fold_u = Routed(*gw_u)
    if few:
        rows = gather_end(rows).reshape(docs * members * segs, -1)
    else:
        rows = lax.all_gather(pack, ("doc", "seg") if all_groups else ("seg",), axis=0, tiled=True)
    if routed:
        rows = before(rows, fold_d)
    mixed, gr1c, svec, *sums = cross(
        meta, rows, mixed, (seg_up, seg_down, bias, seg_gains, seg_shifts),
        (cross_qkv, cross_proj, cross_up, cross_down, xbias, cross_gains, cross_shifts), positions, segs, r)
    if routed:
        fold_d.step()
        fold_u.step()
        gr1c = before(gr1c, fold_d, fold_u)
    gh, ga, first_v, sums_a, *gw_a = attn_back(meta, (gr1, gr1c, ob), p, q, k, v, tok, seg_qkv, seg_proj, members, False)
    if routed:
        fold_d.step()
        fold_u.step()
        gw_a[0] = before(gw_a[0], fold_d, fold_u)
        fold_a = Routed(*gw_a)
        ga = before(ga, fold_d, fold_u)
    gh, vec, *gw_b = attn_back(meta, (gh, first_v, small_f, small_b, sums_a, gbias, ga), p, q, k, v, tok, seg_qkv, seg_proj, members, True)
    if routed:
        fold_a.step()
        fold_d.step()
        fold_u.step()
        gw_b[0] = before(gw_b[0], fold_a, fold_d, fold_u)
        fold_b = Routed(*gw_b)

    if not all_groups:
        sums, svec = [over_docs(s.astype(bf16)) for s in sums], over_docs(svec.astype(bf16))
    gxqkv, gxo, gxu, gxd, gxbias, gxgains, gxshifts, gpos, gsu, gsd = sums

    if routed:
        fold_b.step()
        fold_a.step()
        meet(fold_a, fold_b)
        fold_b.step()
        fold_a.step()
        fold_u.step()
        fold_d.step()
        meet(fold_a, fold_b, fold_u)
        fold_b.step()
        fold_a.step()
        meet(fold_a, fold_b)
        fold_b.step()
        fold_a.step()
        fold_u.step()
        meet(fold_a, fold_b)
        fold_b.step()
        sum_d, sum_u = join(*fold_d.x), join(*fold_u.x)
        parts = fold_a.x + fold_b.x
    else:
        def whole_pieces(g, tall=False):
            if len(g) == 1:
                return g[0].reshape(members, -1, D) if tall else g[0].reshape(-1, members, r, D).swapaxes(0, 1).reshape(members, -1, D)
            send, keep = g
            c = member & 1
            first, second = jnp.where(c == 0, keep, send), jnp.where(c == 0, send, keep)
            if members > 4:
                second = second.reshape((-1, 2, 2) + second.shape[1:]).swapaxes(1, 2).reshape(second.shape)
            both = jnp.stack([first, second], axis=1)
            return both.reshape(members, -1, D)

        pieces = [whole_pieces(gw_d, True)] + [whole_pieces(g) for g in (gw_u, gw_a, gw_b)]
        if len(gw_b) == 1:
            tail = jnp.broadcast_to(vec.astype(bf16)[None], (members, SMALL_ROWS, D))
            pieces[3] = jnp.concatenate([pieces[3], tail], axis=1)
        sum_d, sum_u, *parts = [over_docs(fold(x, members, member)) for x in pieces]
    gqkv, go, gb, gg, gs = finish(meta, parts, svec, r, F, routed)
    up = sum_u.reshape(wide, r, D).swapaxes(0, 1).reshape(r, F) + gsu
    return (
        mixed.reshape(segs, L, D), gh.reshape(segs, L, D),
        gqkv, go, up, sum_d + gsd, gb.reshape(-1), gg, gs,
        gxqkv, gxo, gxu, gxd, gxbias.reshape(-1), gxgains, gxshifts, gpos,
    )


def solution(mesh):
    rows, seg, copied = P("doc", "seg", None), P("seg", None), P()
    grads = (P(None, "seg", None), seg, seg, seg, P("seg"), P(None, "seg"), P(None, "seg"))
    return jax.shard_map(
        shards,
        mesh=mesh,
        in_specs=(rows, P("doc", "seg"), P("doc", None)) + (copied,) * 15 + (rows,),
        out_specs=(rows, rows) + grads + grads + (P(None, "seg"),),
        check_vma=False,
    )
```

```python
import functools

import jax
import jax.numpy as jnp
from jax import lax
from jax.experimental import pallas as pl
from jax.experimental.pallas import tpu as pltpu
from jax.sharding import PartitionSpec as P

f32, bf16 = jnp.float32, jnp.bfloat16
VMEM_BYTES = 60 * 2**20
EPS = 1e-6
PAIR = 128
HD = 64
CHUNK = 768
TILE = 384
NEG = -1e30
SMALL_ROWS = 16

S = jax.ShapeDtypeStruct
V = pltpu.VMEM
VM = pl.BlockSpec(memory_space=pltpu.VMEM)
SM = pl.BlockSpec(memory_space=pltpu.SMEM)
ANY = pl.BlockSpec(memory_space=pl.ANY)
PARAMS = pltpu.CompilerParams(vmem_limit_bytes=VMEM_BYTES)


def cost(micros):
    return pl.CostEstimate(flops=int(micros * 1e9), bytes_accessed=int(micros * 3e6), transcendentals=0)


def nn(a, b):
    return lax.dot_general(a, b, (((1,), (0,)), ((), ())), preferred_element_type=f32)


def nt(a, b):
    return lax.dot_general(a, b, (((1,), (1,)), ((), ())), preferred_element_type=f32)


def tn(a, b):
    return lax.dot_general(a, b, (((0,), (0,)), ((), ())), preferred_element_type=f32)


def gelu_both(u):
    phi = lax.erf(u * 0.70710678118654752) * 0.5 + 0.5
    return u * phi, phi + u * (jnp.exp(u * u * -0.5) * 0.39894228040143268)


def norm(r):
    c = r - jnp.mean(r, axis=-1, keepdims=True)
    inv = lax.rsqrt(jnp.mean(c * c, axis=-1, keepdims=True) + EPS)
    return c * inv, inv


def norm_back(g, n, inv, gain):
    t = g * gain
    return inv * (t - jnp.mean(t, axis=-1, keepdims=True) - n * jnp.mean(t * n, axis=-1, keepdims=True))


def row_sum(x):
    return jnp.sum(x, axis=0, keepdims=True)


def halves(x):
    low = lax.broadcasted_iota(jnp.int32, x.shape, 1) < HD
    zero = jnp.zeros_like(x)
    return jnp.where(low, x, zero), jnp.where(low, zero, x)


def two(x):
    return jnp.concatenate(halves(x), axis=0)


def softmax(t):
    t = jnp.exp(t - jnp.max(t, axis=-1, keepdims=True))
    return (t * (1.0 / jnp.sum(t, axis=-1, keepdims=True))).astype(bf16)


def start_all(sems, *pairs):
    copies = [pltpu.make_async_copy(a, b, sems.at[n]) for n, (a, b) in enumerate(pairs)]
    for c in copies:
        c.start()
    return copies


def bias_row(bias, j):
    k = CHUNK // 128
    rows = bias[...].astype(f32)
    return jnp.concatenate([rows[j * k + m:j * k + m + 1] for m in range(k)], axis=1)


def whole(a):
    return pl.BlockSpec(a.shape, lambda i, n=len(a.shape): (0,) * n)


def split_of(members, n, spread, D):
    per = n * D // members if spread else D // members
    return None if per % 16 or TILE % (2 * per) else (per, D // (2 * per) if spread else 0)


def grad_outs(members, n, spread, D, extra=0):
    split = split_of(members, n, spread, D)
    if not split:
        return [S((n, D, D), bf16)], [V((n, D, D), bf16), pltpu.SemaphoreType.DMA((n, 2))]
    per, step = split
    rows = per if spread else n * per
    return [S((members // 2, rows + extra, D), bf16)] * 2, [V((n, D // (2 * per), 2, per, D), bf16), pltpu.SemaphoreType.DMA((n, 2))]


def placed_at(m, bits, core):
    if bits < 2:
        return m
    low, next_, high = m & 1, (m >> 1) & 1, m >> 2
    first = (low << (bits - 1)) | (high << 1) | next_
    second = (next_ << (bits - 1)) | (high << 1) | low
    return jnp.where(core == 0, first, second)


def emit_grads(split, core, left, right, outs, stage, sems):
    n, D = stage.shape[0], stage.shape[-1]
    bits = outs[0].shape[0].bit_length() - 1

    def copies(j):
        if not split:
            return [pltpu.make_async_copy(stage.at[j], outs[0].at[j], sems.at[j, 0])]
        per, step = split
        res = []
        for k in range(stage.shape[1]):
            m = j * step + k if step else k
            theirs, ours = placed_at(m, bits, 1 - core), placed_at(m, bits, core)
            rows = pl.ds(0, per) if step else pl.ds(j * per, per)
            res += [pltpu.make_async_copy(stage.at[j, k, 1 - core], outs[0].at[theirs, rows], sems.at[j, 0]),
                    pltpu.make_async_copy(stage.at[j, k, core], outs[1].at[ours, rows], sems.at[j, 1])]
        return res

    for j in range(n):
        for t in range(D // TILE):
            res = tn(left(j, slice(t * TILE, (t + 1) * TILE)), right(j)).astype(bf16)
            if split:
                k = TILE // (2 * split[0])
                stage[j, t * k:(t + 1) * k] = res.reshape((k, 2, split[0], D))
            else:
                stage[j, t * TILE:(t + 1) * TILE, :] = res
        for x in copies(j):
            x.start()

    def end():
        for j in range(n):
            for x in copies(j):
                x.wait()

    return end


def forward_kernel(n_docs, split, n_grads, meta, lengths, tok, cot, mask, wqkv_h, wo_h, wu_h, wd_h, bias, gains, shifts, *rest):
    (q_o, k_o, v_o, p_o, ob_o, n_o, inv_o, dg_o, gr2_o, mixed_o, pack_o, small_o), rest = rest[:12], rest[12:]
    grads, (wqkv, wo, wu, wd, y1b, gb_s, gm_s, sems, stage, gsems) = rest[:n_grads], rest[n_grads:]
    i = pl.program_id(0)
    segs, pairs = p_o.shape[0], p_o.shape[1]
    B, D = tok.shape
    L = B // segs
    n = wu.shape[0]
    ga, sh = gains[...].astype(f32), shifts[...].astype(f32)
    cs = [slice(c * CHUNK, (c + 1) * CHUNK) for c in range(n)]
    load = lambda a, b, m: pltpu.make_async_copy(a, b, sems.at[m])
    first = [load(wqkv_h, wqkv, 0), load(wo_h, wo, 1)]
    ups = [load(wu_h.at[:, c], wu.at[j], 2 + j) for j, c in enumerate(cs)]
    downs = [load(wd_h.at[c, :], wd.at[j], 2 + n + j) for j, c in enumerate(cs)]

    @pl.when(i == 0)
    def _():
        for c in first + ups + downs:
            c.start()
        small_o[...] = jnp.zeros_like(small_o)
        first[0].wait()

    hb = tok[...]
    q_o[...] = ((nn(hb, wqkv[0]) + sh[0:1]) * 0.125).astype(bf16)
    k_o[...] = nn(hb, wqkv[1]).astype(bf16)
    v_o[...] = (nn(hb, wqkv[2]) + sh[1:2]).astype(bf16)
    col = [slice(j * PAIR, (j + 1) * PAIR) for j in range(pairs)]
    for s in range(segs):
        rows = slice(s * L, (s + 1) * L)
        live = jnp.where(mask[pl.ds(i * segs + s, 1), :] > 0, 0.0, NEG).astype(f32)
        scores = [nt(q_o[rows, c], two(k_o[rows, c])) for c in col]
        probs = [jnp.concatenate([softmax(t[:, e:e + L] + live) for e in (0, L)], axis=1) for t in scores]
        for j, c in enumerate(col):
            p_o[s, j] = probs[j]
            ob_o[rows, c] = nn(probs[j], two(v_o[rows, c])).astype(bf16)

    @pl.when(i == 0)
    def _():
        for c in first[1:] + ups + downs:
            c.wait()

    n1, inv1 = norm(hb.astype(f32) + nn(ob_o[...], wo[...]) + sh[2:3])
    n_o[...] = n1
    inv_o[...] = inv1
    y1 = n1 * ga[0:1] + sh[3:4]
    y1b[...] = y1.astype(bf16)
    up = lambda j: nn(y1b[...], wu[j]) + bias_row(bias, j)
    here = pl.ds(pl.multiple_of(i * B, B), B)
    u, acc = up(0), y1 + sh[4:5]
    for j in range(n):
        after = up(j + 1) if j + 1 < n else None
        g, d = gelu_both(u)
        gb = g.astype(bf16)
        gb_s[j, here, :] = gb
        dg_o[j] = d.astype(bf16)
        acc = acc + nn(gb, wd[j])
        u = after
    n2, inv2 = norm(acc)
    mixed_o[...] = (n2 * ga[1:2] + sh[5:6]).astype(bf16)
    row = lax.broadcasted_iota(jnp.int32, n2.shape, 0)
    gz = jnp.where(row % L == 0, 0.0, cot[...].astype(f32))
    small_o[0:1, :] += row_sum(gz * n2)
    small_o[1:2, :] += row_sum(gz)
    gr2 = norm_back(gz, n2, inv2, ga[1:2])
    gr2_o[...] = gr2
    gm = gr2.astype(bf16)
    gm_s[here, :] = gm
    small_o[2:3, :] += row_sum(gm.astype(f32))

    lane = lax.broadcasted_iota(jnp.int32, (1, 128), 1)
    for s in range(segs):
        g = (i * segs + s) * meta[2] + meta[0]
        before, doc, pos = jnp.int32(0), meta[1] * 32, g
        for d in range(n_docs):
            before = before + lengths[0, d]
            passed = g >= before
            doc = doc + passed.astype(jnp.int32)
            pos = jnp.where(passed, g - before, pos)
        extra = jnp.where(lane == 0, doc, jnp.where(lane == 1, pos, 0)).astype(f32)
        top = slice(s * L, s * L + 1)
        high = inv1[top].astype(bf16).astype(f32)
        extra = jnp.where(lane == 2, high, jnp.where(lane == 3, inv1[top] - high, extra))
        pack_o[s, :, :D] = n1[top].astype(bf16)
        pack_o[s, :, D:2 * D] = cot[s * L:s * L + 16, :][0:1]
        pack_o[s, :, 2 * D:] = extra.astype(bf16)

    @pl.when(i == pl.num_programs(0) - 1)
    def _():
        emit_grads(split, meta[3], lambda j, c: gb_s[j, :, c], lambda j: gm_s[...], grads, stage, gsems)()


def forward(meta, lengths, tok, cot, mask, wqkv, wo, wu, wd, bias, gains, shifts, members, step=2):
    T, D = tok.shape
    segs_dev, L = mask.shape
    pairs, B, n = D // PAIR, L * step, wu.shape[1] // CHUNK
    rowblk = pl.BlockSpec((B, D), lambda i: (i, 0))
    wide = pl.BlockSpec((n, B, CHUNK), lambda i: (0, i, 0))
    row = lambda dt: (S((T, D), dt), rowblk)
    outs = [row(bf16), row(bf16), row(bf16),
            (S((segs_dev, pairs, L, 2 * L), bf16), pl.BlockSpec((step, pairs, L, 2 * L), lambda i: (i, 0, 0, 0))),
            row(bf16), row(f32), (S((T, 1), f32), pl.BlockSpec((B, 1), lambda i: (i, 0))), (S((n, T, CHUNK), bf16), wide),
            row(f32), row(bf16),
            (S((segs_dev, 1, 2 * D + 128), bf16), pl.BlockSpec((step, 1, 2 * D + 128), lambda i: (i, 0, 0))),
            (S((8, D), f32), whole(S((8, D), f32)))]
    grads, scratch = grad_outs(members, n, True, D)
    return pl.pallas_call(
        functools.partial(forward_kernel, lengths.shape[1], split_of(members, n, True, D), len(grads)),
        grid=(segs_dev // step,),
        in_specs=[SM, SM, rowblk, rowblk, whole(mask), ANY, ANY, ANY, ANY, whole(bias), whole(gains), whole(shifts)],
        out_specs=[o[1] for o in outs] + [ANY] * len(grads),
        out_shape=[o[0] for o in outs] + grads,
        scratch_shapes=[V(wqkv.shape, bf16), V(wo.shape, bf16), V((n, D, CHUNK), bf16), V((n, CHUNK, D), bf16), V((B, D), bf16), V((n, T, CHUNK), bf16),
                        V((T, D), bf16), pltpu.SemaphoreType.DMA((2 + 2 * n,))] + scratch,
        compiler_params=PARAMS,
        name="seg_forward", cost_estimate=cost(30),
    )(meta, lengths, tok, cot, mask, wqkv, wo, wu, wd, bias, gains, shifts)


def ffn_back_kernel(split, n_grads, meta, n1, inv1, dg, gr2, wu_h, wd_h, gains, shifts, gr1_o, gbias_o, small_o, *rest):
    grads, (wu, wd, gm, y1b_s, gu_s, sems, stage, gsems) = rest[:n_grads], rest[n_grads:]
    i = pl.program_id(0)
    n = wu.shape[0]
    B = n1.shape[0]
    cs = [slice(c * CHUNK, (c + 1) * CHUNK) for c in range(n)]
    ups = [pltpu.make_async_copy(wu_h.at[:, c], wu.at[j], sems.at[0, j]) for j, c in enumerate(cs)]
    downs = [pltpu.make_async_copy(wd_h.at[c, :], wd.at[j], sems.at[1, j]) for j, c in enumerate(cs)]
    order = [c for pair in zip(downs, ups) for c in pair]

    @pl.when(i == 0)
    def _():
        for c in order[:3]:
            c.start()
        small_o[...] = jnp.zeros_like(small_o)
        gbias_o[...] = jnp.zeros_like(gbias_o)

    def await_first(m, count):
        @pl.when(i == 0)
        def _():
            for k in range(m, min(m + count, 2 * n)):
                order[k].wait()
                if k + 3 < 2 * n:
                    order[k + 3].start()

    here = pl.ds(pl.multiple_of(i * B, B), B)
    n1v, gfirst = n1[...], gains[...].astype(f32)[0:1]
    y1b_s[here, :] = (n1v * gfirst + shifts[...].astype(f32)[3:4]).astype(bf16)
    acc = gr2[...]
    gm[...] = acc.astype(bf16)
    await_first(0, 1)
    t = nt(gm[...], wd[0])
    for j in range(n):
        await_first(2 * j + 1, 2)
        after = nt(gm[...], wd[j + 1]) if j + 1 < n else None
        gu = (t * dg[j].astype(f32)).astype(bf16)
        gu_s[j, here, :] = gu
        gbias_o[j:j + 1, :] += row_sum(gu.astype(f32))
        acc = acc + nt(gu, wu[j])
        t = after
    small_o[0:1, :] += row_sum(acc * n1v)
    small_o[1:2, :] += row_sum(acc)
    gr1_o[...] = norm_back(acc, n1v, inv1[...], gfirst)

    @pl.when(i == pl.num_programs(0) - 1)
    def _():
        emit_grads(split, meta[3], lambda j, c: y1b_s[:, c], lambda j: gu_s[j], grads, stage, gsems)()


def ffn_back(meta, n1, inv1, dg, gr2, wu, wd, gains, shifts, members, B=256):
    T, D = n1.shape
    n = wu.shape[1] // CHUNK
    rowblk = pl.BlockSpec((B, D), lambda i: (i, 0))
    grads, scratch = grad_outs(members, n, False, D)
    shapes = [S((T, D), f32), S((8, CHUNK), f32), S((8, D), f32)]
    return pl.pallas_call(
        functools.partial(ffn_back_kernel, split_of(members, n, False, D), len(grads)),
        grid=(T // B,),
        in_specs=[SM, rowblk, pl.BlockSpec((B, 1), lambda i: (i, 0)), pl.BlockSpec((n, B, CHUNK), lambda i: (0, i, 0)), rowblk,
                  ANY, ANY, whole(gains), whole(shifts)],
        out_specs=[rowblk, whole(shapes[1]), whole(shapes[2])] + [ANY] * len(grads),
        out_shape=shapes + grads,
        scratch_shapes=[V((n, D, CHUNK), bf16), V((n, CHUNK, D), bf16), V((B, D), bf16), V((T, D), bf16), V((n, T, CHUNK), bf16),
                        pltpu.SemaphoreType.DMA((2, n))] + scratch,
        compiler_params=PARAMS,
        name="seg_ffn_back", cost_estimate=cost(20),
    )(meta, n1, inv1, dg, gr2, wu, wd, gains, shifts)


def with_cls(rows, cls):
    row = lax.broadcasted_iota(jnp.int32, (rows.shape[0], 1), 0)
    for s in range(cls.shape[0]):
        rows = jnp.where(row == s * (rows.shape[0] // cls.shape[0]), cls[s], rows)
    return rows


def input_grad_kernel(gr1, gr1c, qk0, qk1, vv, wqkv, o):
    H = qk0.shape[1] // 2
    part = lambda a: jnp.concatenate([qk0[:, a:a + H], qk1[:, a:a + H]], axis=1)
    o[...] = (with_cls(gr1[...], gr1c) + nt(part(0), wqkv[0]) + nt(part(H), wqkv[1]) + nt(vv[...], wqkv[2])).astype(bf16)


def input_grad(gr1, gr1c, qk0, qk1, vv, wqkv, step=2):
    T, D = gr1.shape
    segs = gr1c.shape[0]
    rowblk = pl.BlockSpec((T // segs * step, D), lambda i: (i, 0))
    return pl.pallas_call(
        input_grad_kernel,
        grid=(segs // step,),
        in_specs=[rowblk, pl.BlockSpec((step, 1, D), lambda i: (i, 0, 0)), rowblk, rowblk, rowblk, whole(wqkv)],
        out_specs=rowblk,
        out_shape=S((T, D), bf16),
        compiler_params=PARAMS,
        name="input_grad", cost_estimate=cost(6),
    )(gr1, gr1c, qk0, qk1, vv, wqkv)


def attn_back_kernel(split, n_grads, is_last, meta, *rest):
    if is_last:
        (first_v, small_f, small_b, sums_a, gbias, ga_in), rest = rest[:6], rest[6:]
    else:
        (gr1, gr1c, ob), rest = rest[:3], rest[3:]
    (p, q, k, v, tok, wo), rest = rest[:6], rest[6:]
    if is_last:
        (qk_o, vv_o, vec_o), rest = rest[:3], rest[3:]
    else:
        (qk_o, ga_o, first_v_o, sums_o), rest = rest[:4], rest[4:]
    grads, rest = rest[:n_grads], rest[n_grads:]
    go_s, g_s, left_s, sums, rest = *rest[:4], rest[4:]
    if is_last:
        vec_s, wsems, rest = *rest[:2], rest[2:]
    stage, gsems = rest
    i = pl.program_id(0)
    segs, pairs = p.shape[0], p.shape[1]
    B, D = tok.shape
    L, H = B // segs, pairs * PAIR
    here = pl.ds(pl.multiple_of(i * B, B), B)

    @pl.when(i == 0)
    def _():
        sums[...] = jnp.zeros_like(sums)

    left_s[0, here, :] = tok[...]
    if is_last:
        ga = ga_in[...]
    else:
        ga = with_cls(gr1[...], gr1c).astype(bf16)
        ga_o[...] = ga
        g_s[1, here, :] = ga
        left_s[1, here, :] = ob[...]
    go_s[...] = nt(ga, wo[...]).astype(bf16)
    col = [slice(j * PAIR, (j + 1) * PAIR) for j in range(pairs)]
    beside = lambda c: slice(H + c.start, H + c.stop)
    eighth = jnp.asarray(0.125, bf16)
    for s in range(segs):
        rows = slice(s * L, (s + 1) * L)
        out = pl.ds(pl.multiple_of(i * B, B) + s * L, L)
        gps = [nt(go_s[rows, c], two(v[rows, c])) for c in col]
        for j, c in enumerate(col):
            pb = p[s, j]
            gv = tn(jnp.concatenate([pb[:, :L], pb[:, L:]], axis=0), two(go_s[rows, c])).astype(bf16)
            if is_last:
                g_s[1, out, beside(c)] = gv
            else:
                first_v_o[rows, c] = gv
        gss = []
        for j, gp in enumerate(gps):
            pf = p[s, j].astype(f32)
            gs = []
            for e in (0, L):
                pe, ge = pf[:, e:e + L], gp[:, e:e + L]
                gs.append((pe * (ge - jnp.sum(pe * ge, axis=-1, keepdims=True))).astype(bf16))
            gss.append(gs)
        for c, gs in zip(col, gss):
            g_s[0, out, c] = nn(jnp.concatenate(gs, axis=1), two(k[rows, c])).astype(bf16) * eighth
            g_s[0, out, beside(c)] = tn(jnp.concatenate(gs, axis=0), two(q[rows, c])).astype(bf16)
    if is_last:
        g_s[1, here, :H] = first_v[...]
        vv_o[...] = g_s[1, here, :]
    qk_o[...] = g_s[0, here, :]
    for m in range(2):
        sums[m:m + 1, :] += row_sum(g_s[m, here, :].astype(f32))

    @pl.when(i == pl.num_programs(0) - 1)
    def _():
        tail = []
        if is_last:
            vec = jnp.concatenate([
                gbias[0:4, :], small_b[0:1, :], small_f[0:1, :], jnp.concatenate([sums_a[0:1, :H], sums[0:1, :H]], axis=1), sums[1:2, :],
                sums_a[1:2, :], small_b[1:2, :], small_f[2:3, :], small_f[1:2, :], jnp.zeros((4, D), f32)], axis=0)
            vec_o[...] = vec
            if split:
                for m in range(vec_s.shape[0]):
                    vec_s[m] = vec.astype(bf16)
                tail = [pltpu.make_async_copy(vec_s, h.at[:, pl.ds(h.shape[1] - SMALL_ROWS, SMALL_ROWS)], wsems.at[m]) for m, h in enumerate(grads)]
        else:
            sums_o[...] = sums[...]
        for x in tail:
            x.start()
        emit_grads(split, meta[3], lambda j, c: left_s[0 if is_last else j, :, c], lambda j: g_s[j], grads, stage, gsems)()
        for x in tail:
            x.wait()


def attn_back(meta, before_it, p, q, k, v, tok, wo, members, is_last, step=2):
    T, D = tok.shape
    segs_dev, all_pairs, L = p.shape[:3]
    pairs, H, half = all_pairs // 2, D // 2, int(is_last)
    B = L * step
    rowblk = pl.BlockSpec((B, D), lambda i: (i, 0))
    halfblk = pl.BlockSpec((B, H), lambda i: (i, half))
    firstblk = pl.BlockSpec((B, H), lambda i: (i, 0))
    split = split_of(members, 2, False, D)
    grads, scratch = grad_outs(members, 2, False, D, SMALL_ROWS if is_last else 0)
    small = S((8, D), f32)
    if is_last:
        vec = S((SMALL_ROWS, D), f32)
        specs = [firstblk] + [whole(x) for x in before_it[1:5]] + [rowblk]
        outs = [(S((T, D), bf16), rowblk), (S((T, D), bf16), rowblk), (vec, whole(vec))]
        more = [V((members // 2, SMALL_ROWS, D), bf16), pltpu.SemaphoreType.DMA((2,))]
    else:
        specs = [rowblk, pl.BlockSpec((step, 1, D), lambda i: (i, 0, 0)), rowblk]
        outs = [(S((T, D), bf16), rowblk), (S((T, D), bf16), rowblk), (S((T, H), bf16), firstblk), (small, whole(small))]
        more = []
    return pl.pallas_call(
        functools.partial(attn_back_kernel, split, len(grads), is_last),
        grid=(segs_dev // step,),
        in_specs=[SM] + specs + [pl.BlockSpec((step, pairs, L, 2 * L), lambda i: (i, half, 0, 0)), halfblk, halfblk, halfblk, rowblk,
                                 pl.BlockSpec((H, D), lambda i: (half, 0))],
        out_specs=[o[1] for o in outs] + [ANY] * len(grads),
        out_shape=[o[0] for o in outs] + grads,
        scratch_shapes=[V((B, H), bf16), V((2, T, D), bf16), V((2, T, D), bf16), V((8, D), f32)] + more + scratch,
        compiler_params=PARAMS,
        name="seg_attention_back", cost_estimate=cost(12),
    )(meta, *before_it, p, q, k, v, tok, wo)


def onehot(rows, width, start):
    at = lax.broadcasted_iota(jnp.int32, (rows, width), 0) + start
    return (at == lax.broadcasted_iota(jnp.int32, (rows, width), 1)).astype(bf16)


def nt_exact(x, pick):
    a = x.astype(bf16)
    rest = x - a.astype(f32)
    b = rest.astype(bf16)
    return nt(a, pick) + nt(b, pick) + nt((rest - b.astype(f32)).astype(bf16), pick)


def own_vectors(vec, member, r, F):
    D = vec.shape[1]
    wide = F // D
    per = r * wide
    fits = D // per
    parts = nt_exact(vec, onehot(per, D, lax.rem(member, fits) * per))
    line = lax.broadcasted_iota(jnp.int32, parts.shape, 0)
    bias = row_sum(jnp.where(line == lax.div(member, fits), parts, 0.0))
    rest = nt_exact(vec, onehot(r, D, member * r))
    return bias, rest[wide:wide + 2], rest[wide + 2:wide + 8]


def cross_kernel(r, meta, rows_in, mixed_h, swu_h, swd_h, xqkv_h, xo_h, xu_h, xd_h, sbias, sgains, sshifts, xbias, xgains, xshifts, pos,
                 mixed_o, gr1_o, svec_o, gqkv_o, go_o, gu_o, gd_o, gbias_o, ggains_o, gshifts_o, gpos_o, sgu_o, sgd_o,
                 swu, swd, xqkv, xo, xu, xd, sgb, sdg, xgb, xdg, sgu, xgu, q_s, k_s, v_s, p_s, o_s, go_s, gq_s, gk_s, gv_s,
                 cls_s, gr1_s, vec_s, svec_s, patch, sems, psems):
    n, D = swu.shape[0], swu.shape[1]
    R = rows_in.shape[0]
    cs = [slice(c * CHUNK, (c + 1) * CHUNK) for c in range(n)]
    col = [slice(c, c + PAIR) for c in range(0, D, PAIR)]
    queue = []
    for wu_h, wd_h, wu, wd in ((swu_h, swd_h, swu, swd), (xu_h, xd_h, xu, xd)):
        for j, c in enumerate(cs):
            queue += [(wu_h.at[:, c], wu.at[j]), (wd_h.at[c, :], wd.at[j])]
    queue[2 * n:2 * n] = [(xqkv_h.at[m], xqkv.at[m]) for m in range(3)] + [(xo_h, xo)]
    copies = [pltpu.make_async_copy(a, b, sems.at[m]) for m, (a, b) in enumerate(queue)]
    ahead, waited = 4, [0]
    for x in copies[:ahead]:
        x.start()

    def need(count):
        for _ in range(count):
            m = waited[0]
            copies[m].wait()
            if m + ahead < len(copies):
                copies[m + ahead].start()
            waited[0] = m + 1

    segs, L = patch.shape[0], mixed_h.shape[0] // patch.shape[0]
    fetch = [pltpu.make_async_copy(mixed_h.at[pl.ds(s * L, 16), :], patch.at[s], psems.at[s]) for s in range(segs)]
    for x in fetch:
        x.start()
    sg, ss = sgains[...].astype(f32), sshifts[...].astype(f32)
    xg, xs = xgains[...].astype(f32), xshifts[...].astype(f32)
    eighth = jnp.asarray(0.125, bf16)

    def ffn_f(acc, yb, wu, wd, bias, gb_s, dg_s):
        def up(j):
            need(1)
            return nn(yb, wu[j]) + bias_row(bias, j)

        for j in range(n):
            g, d = gelu_both(up(j))
            gb = g.astype(bf16)
            gb_s[:, cs[j]] = gb
            dg_s[:, cs[j]] = d.astype(bf16)
            need(1)
            acc = acc + nn(gb, wd[j])
        return acc

    def ffn_b(acc, gm, wu, wd, dg_s, gu_s, vec):
        t = nt(gm, wd[0])
        for j in range(n):
            after = nt(gm, wd[j + 1]) if j + 1 < n else None
            gu = (t * dg_s[:, cs[j]].astype(f32)).astype(bf16)
            gu_s[:, cs[j]] = gu
            vec[j:j + 1, :] = row_sum(gu.astype(f32))
            acc = acc + nt(gu, wu[j])
            t = after
        return acc

    vec_s[...] = jnp.zeros_like(vec_s)
    svec_s[...] = jnp.zeros_like(svec_s)
    n1 = rows_in[:, :D].astype(f32)
    extra = rows_in[:, 2 * D:].astype(f32)
    spos = extra[:, 1:2].astype(jnp.int32)
    inv1 = extra[:, 2:3] + extra[:, 3:4]
    lane = lax.broadcasted_iota(jnp.int32, (8, extra.shape[1]), 1)
    did_row = nt((lane == 0).astype(bf16), extra.astype(bf16))[0:1]
    allowed = extra[:, 0:1] == did_row
    placed = (lax.broadcasted_iota(jnp.int32, (R, pos.shape[0]), 1) == spos).astype(bf16)

    y1 = n1 * sg[0:1] + ss[3:4]
    y1b = y1.astype(bf16)
    n2, inv2 = norm(ffn_f(y1 + ss[4:5], y1b, swu, swd, sbias, sgb, sdg))
    h = n2 * sg[1:2] + ss[5:6] + nn(placed, pos[...])

    hb = h.astype(bf16)
    need(1)
    q_s[...] = ((nn(hb, xqkv[0]) + xs[0:1]) * 0.125).astype(bf16)
    need(1)
    k_s[...] = nn(hb, xqkv[1]).astype(bf16)
    need(1)
    v_s[...] = (nn(hb, xqkv[2]) + xs[1:2]).astype(bf16)
    early = R <= 256
    pair_scores = lambda c: [nt(x, k_s[:, c]) for x in halves(q_s[:, c])]
    scores = [pair_scores(c) for c in col] if early else None
    for j, c in enumerate(col):
        out, v2 = 0.0, halves(v_s[:, c])
        sc = scores[j] if early else pair_scores(c)
        for e in range(2):
            pb = softmax(jnp.where(allowed, sc[e], NEG))
            p_s[2 * j + e] = pb
            out = out + nn(pb, v2[e])
        o_s[:, c] = out.astype(bf16)
    need(1)
    m1, minv1 = norm(h + nn(o_s[...], xo[...]) + xs[2:3])
    z1 = m1 * xg[0:1] + xs[3:4]
    z1b = z1.astype(bf16)
    m2, minv2 = norm(ffn_f(z1 + xs[4:5], z1b, xu, xd, xbias, xgb, xdg))
    cls_s[...] = m2 * xg[1:2] + xs[5:6]

    gz = rows_in[:, D:2 * D].astype(f32)
    vec_s[n + 1:n + 2, :] = row_sum(gz * m2)
    vec_s[n + 7:n + 8, :] = row_sum(gz)
    gr2 = norm_back(gz, m2, minv2, xg[1:2])
    xgm = gr2.astype(bf16)
    vec_s[n + 6:n + 7, :] = row_sum(xgm.astype(f32))
    gy1 = ffn_b(gr2, xgm, xu, xd, xdg, xgu, vec_s)
    vec_s[n:n + 1, :] = row_sum(gy1 * m1)
    vec_s[n + 5:n + 6, :] = row_sum(gy1)
    gr1 = norm_back(gy1, m1, minv1, xg[0:1])
    xga = gr1.astype(bf16)
    vec_s[n + 4:n + 5, :] = row_sum(xga.astype(f32))
    go_s[...] = nt(xga, xo[...]).astype(bf16)
    pair_gps = lambda c: [nt(x, v_s[:, c]) for x in halves(go_s[:, c])]
    gps = [pair_gps(c) for c in col] if early else None
    for j, c in enumerate(col):
        gpj = gps[j] if early else pair_gps(c)
        q2, k2, g2 = halves(q_s[:, c]), halves(k_s[:, c]), halves(go_s[:, c])
        gq = gk = gv = 0.0
        for e in range(2):
            pb = p_s[2 * j + e]
            pf = pb.astype(f32)
            gp = gpj[e]
            gs = (pf * (gp - jnp.sum(pf * gp, axis=-1, keepdims=True))).astype(bf16)
            gq = gq + nn(gs, k2[e])
            gk = gk + tn(gs, q2[e])
            gv = gv + tn(pb, g2[e])
        gq_s[:, c] = gq.astype(bf16) * eighth
        gk_s[:, c] = gk.astype(bf16)
        gv_s[:, c] = gv.astype(bf16)
    vec_s[n + 2:n + 3, :] = row_sum(gq_s[...].astype(f32))
    vec_s[n + 3:n + 4, :] = row_sum(gv_s[...].astype(f32))
    gcls = gr1 + nt(gq_s[...], xqkv[0]) + nt(gk_s[...], xqkv[1]) + nt(gv_s[...], xqkv[2])

    svec_s[n + 1:n + 2, :] = row_sum(gcls * n2)
    svec_s[n + 7:n + 8, :] = row_sum(gcls)
    gr2 = norm_back(gcls, n2, inv2, sg[1:2])
    sgm = gr2.astype(bf16)
    svec_s[n + 6:n + 7, :] = row_sum(sgm.astype(f32))
    gy1 = ffn_b(gr2, sgm, swu, swd, sdg, sgu, svec_s)
    svec_s[n:n + 1, :] = row_sum(gy1 * n1)
    svec_s[n + 5:n + 6, :] = row_sum(gy1)
    gr1_s[...] = norm_back(gy1, n1, inv1, sg[0:1])
    svec_o[...] = svec_s[...]

    for x in fetch:
        x.wait()
    top = lax.broadcasted_iota(jnp.int32, (16, 1), 0) == 0
    for s in range(segs):
        line = pl.ds(meta[4] + s, 1)
        gr1_o[s] = gr1_s[line, :]
        patch[s] = jnp.where(top, cls_s[line, :], patch[s].astype(f32)).astype(bf16)
    store = [pltpu.make_async_copy(patch.at[s], mixed_o.at[pl.ds(s * L, 16), :], psems.at[s]) for s in range(segs)]
    for x in store:
        x.start()

    member = meta[0]
    pick = onehot(r, D, member * r)
    own = lambda x: nt(pick, x).astype(bf16)
    pick_wide = onehot(r * n, n * D, member * r * n)
    own_wide = lambda x: nt(pick_wide, x).astype(bf16)
    hbt = own(hb)
    for m, g in enumerate((gq_s, gk_s, gv_s)):
        gqkv_o[m] = nn(hbt, g[...])
    go_o[...] = nn(own(o_s[...]), xga)
    gd_o[...] = nn(own_wide(xgb[...]), xgm)
    sgd_o[...] = nn(own_wide(sgb[...]), sgm)
    z1t, y1t = own(z1b), own(y1b)
    for c in cs:
        gu_o[:, c] = nn(z1t, xgu[:, c])
        sgu_o[:, c] = nn(y1t, sgu[:, c])
    bias, gains, shifts = own_vectors(vec_s[...], member, r, n * D)
    gbias_o[...] = bias
    ggains_o[...] = gains
    gshifts_o[...] = shifts
    gown = nt_exact(gcls, pick)
    high = gown.astype(bf16)
    gpos_o[...] = tn(placed, high) + tn(placed, (gown - high.astype(f32)).astype(bf16))
    for x in store:
        x.wait()


def cross(meta, rows_in, mixed, seg_params, cross_params, pos, segs, r):
    swu, swd, sbias, sgains, sshifts = seg_params
    xqkv, xo, xu, xd, xbias, xgains, xshifts = cross_params
    R = rows_in.shape[0]
    D, F = swu.shape
    n = F // CHUNK
    outs = [S(mixed.shape, bf16), S((segs, 1, D), f32), S((SMALL_ROWS, D), f32), S((3, r, D), f32), S((r, D), f32), S((r, F), f32),
            S((r * n, D), f32), S((1, r * n), f32), S((2, r), f32), S((6, r), f32), S((pos.shape[0], r), f32), S((r, F), f32), S((r * n, D), f32)]
    up, down, row = V((n, D, CHUNK), bf16), V((n, CHUNK, D), bf16), V((R, D), bf16)
    return pl.pallas_call(
        functools.partial(cross_kernel, r),
        in_specs=[SM, VM] + [ANY] * 7 + [VM] * 7,
        out_specs=[ANY] + [VM] * (len(outs) - 1),
        out_shape=outs,
        scratch_shapes=[up, down, V(xqkv.shape, bf16), V(xo.shape, bf16), up, down] + [V((R, F), bf16)] * 6 + [row] * 3
        + [V((D // HD, R, R), bf16)] + [row] * 5 + [V((R, D), f32)] * 2 + [V((SMALL_ROWS, D), f32)] * 2
        + [V((segs, 16, D), bf16), pltpu.SemaphoreType.DMA((4 * n + 4,)), pltpu.SemaphoreType.DMA((segs,))],
        input_output_aliases={2: 0},
        compiler_params=PARAMS,
        name="cross_block", cost_estimate=cost(28),
    )(meta, rows_in, mixed, swu, swd, xqkv, xo, xu, xd, sbias, sgains, sshifts, xbias, xgains, xshifts, pos)


def finish_kernel(r, F, routed, meta, *rest):
    ins, (w_o, o_o, bias_o, gains_o, shifts_o) = rest[:-5], rest[-5:]
    if routed:
        lower = meta[1] == 0
        totals = []
        for x, other in (ins[0:2], ins[2:4]):
            a, b = x[...].astype(f32), other[...].astype(f32)
            totals.append(jnp.concatenate([jnp.where(lower, a, b), jnp.where(lower, b, a)], axis=0))
    else:
        totals = [ins[0][...], ins[1][...]]
    a, b = totals
    H = a.shape[1] // 2
    for m in range(2):
        w_o[m] = jnp.concatenate([a[:r, m * H:(m + 1) * H], b[:r, m * H:(m + 1) * H]], axis=1)
    w_o[2] = b[r:2 * r]
    o_o[...] = a[r:2 * r]
    bias, gains, shifts = own_vectors(b[2 * r:] + ins[-1][...], meta[0], r, F)
    bias_o[...] = bias
    gains_o[...] = gains
    shifts_o[...] = shifts


def finish(meta, parts, vec_c, r, F, routed):
    D = vec_c.shape[1]
    outs = [S((3, r, D), f32), S((r, D), f32), S((1, r * (F // D)), f32), S((2, r), f32), S((6, r), f32)]
    return pl.pallas_call(
        functools.partial(finish_kernel, r, F, routed), in_specs=[SM] + [VM] * (len(parts) + 1), out_specs=[VM] * len(outs), out_shape=outs,
        compiler_params=PARAMS, name="finish", cost_estimate=cost(2),
    )(meta, *parts, vec_c)


def add_up(a, b):
    return (a.astype(f32) + b.astype(f32)).astype(bf16)


def at(x, i, axis):
    return lax.dynamic_index_in_dim(x, i, axis, keepdims=False)


def fold(pieces, members, member):
    bits = members.bit_length() - 1
    x = pieces.reshape((2,) * bits + pieces.shape[1:])
    for bit in range(bits):
        axis = bits - 1 - bit
        mine = (member >> bit) & 1
        got = lax.ppermute(at(x, 1 - mine, axis), "seg", [(m, m ^ (1 << bit)) for m in range(members)])
        x = add_up(at(x, mine, axis), got)
    return x


def over_docs(x):
    docs = lax.axis_size("doc")
    total, part = x.astype(f32), x
    for _ in range(docs - 1):
        part = lax.ppermute(part, "doc", [(d, (d + 1) % docs) for d in range(docs)])
        total = total + part.astype(f32)
    return total


class Routed:
    def __init__(self, send, keep):
        self.members, member = lax.axis_size("seg"), lax.axis_index("seg")
        self.core, self.number = member & 1, lax.axis_index("doc") * self.members + member
        self.step, self.out = 0, [send]
        self.shape = (2, 2, 2, 2, send.shape[1] // 2, send.shape[2])
        self.terms, self.fresh = [(keep, ())], 0

    def bit(self, first, second):
        return jnp.where(self.core == 0, (self.number & first) != 0, (self.number & second) != 0).astype(jnp.int32)

    def sum(self, *choices):
        total = 0.0
        for x, path in self.terms:
            for axis, i in path + choices:
                x = at(x, i, axis)
            total = total + x.astype(f32)
        return total.astype(bf16)

    def ready(self):
        X, Z0, Z1, Y = 2, 4, 8, self.members
        if self.step == 1:
            self.terms = [(x.reshape(self.shape), path) for x, path in self.terms]
            b = self.bit(X, Z0)
            self.masks, self.out, self.choice = [(X, Z0)], [self.sum((0, 1 - b))], ((0, b),)
        elif self.step == 2:
            b, y = self.bit(Z0, X), self.bit(Y, Y)
            self.masks = [(Z0, X), (Y, Y), (Z0 + Y, X + Y)]
            self.out = [self.sum((1, i), (1, h)) for i, h in ((1 - b, y), (b, 1 - y), (1 - b, 1 - y))]
            self.choice = ((1, b), (1, y))
        elif self.step == 3:
            b = self.bit(Z1, Z1)
            self.terms, self.fresh = [(lax.optimization_barrier(self.sum()), ())], 0
            self.masks, self.out, self.choice = [(Z1, Z1)], [self.sum((0, 1 - b))], ((0, b),)
        else:
            self.masks, self.out = [(Y, Y)], [self.sum()]
        return self

    def go(self):
        masks = self.masks if self.step else [(1, 1)]
        got = [lax.ppermute(x, ("doc", "seg"), [(m, m ^ by[m & 1]) for m in range(2 * self.members)]) for x, by in zip(self.out, masks)]
        if self.step == 4:
            self.x = (self.out[0], got[0])
        elif self.step:
            self.terms = [(x, path + self.choice) for x, path in self.terms] + [(x, ()) for x in got]
        else:
            self.terms.append((got[0], ()))
        self.fresh = len(got)
        self.step += 1
        return self

    def hold(self, *arrays):
        old = self.terms[:len(self.terms) - self.fresh]
        vals = lax.optimization_barrier(tuple(x for x, _ in old) + arrays)
        self.terms = [(v, path) for v, (_, path) in zip(vals, old)] + self.terms[len(old):]
        return self

    def after(self, *others):
        return self.hold(*(x for f in others for x in f.out))


def before(x, *others):
    vals = [v for f in others for v in (f.out if isinstance(f, Routed) else [f])]
    res = lax.optimization_barrier((x, *vals))
    rest = list(res[1:])
    for f in others:
        if isinstance(f, Routed):
            f.out = [rest.pop(0) for _ in f.out]
        else:
            rest.pop(0)
    return res[0]


def join(x, other):
    a, b = x.astype(f32), other.astype(f32)
    lower = lax.axis_index("doc") == 0
    return jnp.concatenate([jnp.where(lower, a, b), jnp.where(lower, b, a)], axis=0)


def trade(x, mask):
    members = lax.axis_size("seg")
    return lax.ppermute(x, ("doc", "seg"), [(m, m ^ mask) for m in range(2 * members)])


def gather_start(x):
    Z1, Y = 8, lax.axis_size("seg")
    near, far, both = trade(x, Z1), trade(x, Y), trade(x, Y + Z1)
    mine, theirs = jnp.stack([x, near]), jnp.stack([far, both])
    lower = lax.axis_index("doc") == 0
    return jnp.stack([jnp.where(lower, mine, theirs), jnp.where(lower, theirs, mine)])


def gather_middle(x):
    X, Z0 = 2, 4
    return jnp.concatenate([x, trade(x, X), trade(x, Z0), trade(x, X + Z0)], axis=1)


def gather_end(x):
    return jnp.concatenate([x, trade(x, 1)], axis=1)


def shards(tokens, token_mask, doc_lengths, seg_qkv, seg_proj, seg_up, seg_down, seg_bias, seg_gains, seg_shifts,
           cross_qkv, cross_proj, cross_up, cross_down, cross_bias, cross_gains, cross_shifts, positions, cotangent):
    segs, L, D = tokens.shape
    F = seg_up.shape[1]
    members, member = lax.axis_size("seg"), lax.axis_index("seg")
    docs, doc = lax.axis_size("doc"), lax.axis_index("doc")
    r, wide, T = D // members, F // D, segs * L
    all_groups = docs * members * segs <= 256
    few = members == 16 and docs == 2
    place = (doc * members if few else doc * members + member if all_groups else member) * segs
    meta = jnp.stack([member, doc, jnp.int32(members), member & 1, place]).astype(jnp.int32)
    tok, cot = tokens.reshape(T, D), cotangent.reshape(T, D)
    bias, xbias = seg_bias.reshape(-1, 128), cross_bias.reshape(-1, 128)

    q, k, v, p, ob, n1, inv1, dg, gr2, mixed, pack, small_f, *gw_d = forward(
        meta, doc_lengths, tok, cot, token_mask, seg_qkv, seg_proj, seg_up, seg_down, bias, seg_gains, seg_shifts, members)
    routed = few and len(gw_d) == 2
    pack = pack.reshape(segs, -1)
    if few:
        pack = gather_start(pack)
    if routed:
        fold_d = Routed(*gw_d).go()
        inv1 = before(inv1, pack)
    gr1, gbias, small_b, *gw_u = ffn_back(meta, n1, inv1, dg, gr2, seg_up, seg_down, seg_gains, seg_shifts, members)
    if few:
        rows = gather_middle(pack)
    if routed:
        gw_u[0] = before(gw_u[0], fold_d.ready(), rows)
        fold_u = Routed(*gw_u).go()
    if few:
        rows = gather_end(rows).reshape(docs * members * segs, -1)
    else:
        rows = lax.all_gather(pack, ("doc", "seg") if all_groups else ("seg",), axis=0, tiled=True)
    if routed:
        rows = before(rows, fold_d)
        fold_d.go()
    mixed, gr1c, svec, *sums = cross(
        meta, rows, mixed, (seg_up, seg_down, bias, seg_gains, seg_shifts),
        (cross_qkv, cross_proj, cross_up, cross_down, xbias, cross_gains, cross_shifts), positions, segs, r)
    if routed:
        gr1c = before(gr1c, fold_d.ready(), fold_u.ready())
        fold_d.go()
        fold_u.go()
    qk0, ga, first_v, sums_a, *gw_a = attn_back(meta, (gr1, gr1c, ob), p, q, k, v, tok, seg_proj, members, False)
    if routed:
        gw_a[0] = before(gw_a[0], fold_d.ready(), fold_u.ready())
        ga = before(ga, fold_d, fold_u)
        fold_a = Routed(*gw_a).go()
        fold_d.go()
        fold_u.go()
    qk1, vv, vec, *gw_b = attn_back(meta, (first_v, small_f, small_b, sums_a, gbias, ga), p, q, k, v, tok, seg_proj, members, True)
    if routed:
        gw_b[0] = before(gw_b[0], fold_a.ready(), fold_d.ready(), fold_u.ready())
        fold_b = Routed(*gw_b).go()
        for f in (fold_a, fold_d, fold_u):
            f.go()

    if not all_groups:
        sums, svec = [over_docs(s.astype(bf16)) for s in sums], over_docs(svec.astype(bf16))
    gxqkv, gxo, gxu, gxd, gxbias, gxgains, gxshifts, gpos, gsu, gsd = sums

    if routed:
        gh = input_grad(gr1, gr1c, qk0, qk1, vv, seg_qkv)
        fold_b.hold(gh)
        for m in range(3):
            fold_b.ready()
            fold_a.after(fold_b)
            fold_b.go()
            fold_a.ready()
            fold_b.after(fold_a)
            fold_a.go()
        fold_b.ready().go()
        fold_u.ready().go()
        sum_d, sum_u = join(*fold_d.x), join(*fold_u.x)
        parts = fold_a.x + fold_b.x
    else:
        def whole_pieces(g, tall=False):
            if len(g) == 1:
                return g[0].reshape(members, -1, D) if tall else g[0].reshape(-1, members, r, D).swapaxes(0, 1).reshape(members, -1, D)
            send, keep = g
            c = member & 1
            first, second = jnp.where(c == 0, keep, send), jnp.where(c == 0, send, keep)
            if members > 4:
                apart = lambda x: x.reshape((2, -1, 2) + x.shape[1:])
                first = jnp.moveaxis(apart(first), 0, 2).reshape(first.shape)
                second = apart(second).swapaxes(0, 1).reshape(second.shape)
            both = jnp.stack([first, second], axis=1)
            return both.reshape(members, -1, D)

        pieces = [whole_pieces(gw_d, True)] + [whole_pieces(g) for g in (gw_u, gw_a, gw_b)]
        if len(gw_b) == 1:
            tail = jnp.broadcast_to(vec.astype(bf16)[None], (members, SMALL_ROWS, D))
            pieces[3] = jnp.concatenate([pieces[3], tail], axis=1)
        sum_d, sum_u, *parts = [over_docs(fold(x, members, member)) for x in pieces]
    if not routed:
        gh = input_grad(gr1, gr1c, qk0, qk1, vv, seg_qkv)
    gqkv, go, gb, gg, gs = finish(meta, parts, svec, r, F, routed)
    up = sum_u.reshape(wide, r, D).swapaxes(0, 1).reshape(r, F) + gsu
    return (
        mixed.reshape(segs, L, D), gh.reshape(segs, L, D),
        gqkv, go, up, sum_d + gsd, gb.reshape(-1), gg, gs,
        gxqkv, gxo, gxu, gxd, gxbias.reshape(-1), gxgains, gxshifts, gpos,
    )


def solution(mesh):
    rows, seg, copied = P("doc", "seg", None), P("seg", None), P()
    grads = (P(None, "seg", None), seg, seg, seg, P("seg"), P(None, "seg"), P(None, "seg"))
    return jax.shard_map(
        shards,
        mesh=mesh,
        in_specs=(rows, P("doc", "seg"), P("doc", None)) + (copied,) * 15 + (rows,),
        out_specs=(rows, rows) + grads + grads + (P(None, "seg"),),
        check_vma=False,
    )
```

```python
import functools

import jax
import jax.numpy as jnp
from jax import lax
from jax.experimental import pallas as pl
from jax.experimental.pallas import tpu as pltpu
from jax.sharding import PartitionSpec as P

f32, bf16 = jnp.float32, jnp.bfloat16
VMEM_BYTES = 60 * 2**20
EPS = 1e-6
PAIR = 128
HD = 64
CHUNK = 768
TILE = 384
NEG = -1e30
SMALL_ROWS = 16

S = jax.ShapeDtypeStruct
V = pltpu.VMEM
VM = pl.BlockSpec(memory_space=pltpu.VMEM)
SM = pl.BlockSpec(memory_space=pltpu.SMEM)
ANY = pl.BlockSpec(memory_space=pl.ANY)
PARAMS = pltpu.CompilerParams(vmem_limit_bytes=VMEM_BYTES)


def cost(micros):
    return pl.CostEstimate(flops=int(micros * 1e9), bytes_accessed=int(micros * 3e6), transcendentals=0)


def nn(a, b):
    return lax.dot_general(a, b, (((1,), (0,)), ((), ())), preferred_element_type=f32)


def nt(a, b):
    return lax.dot_general(a, b, (((1,), (1,)), ((), ())), preferred_element_type=f32)


def tn(a, b):
    return lax.dot_general(a, b, (((0,), (0,)), ((), ())), preferred_element_type=f32)


def gelu_both(u):
    phi = lax.erf(u * 0.70710678118654752) * 0.5 + 0.5
    return u * phi, phi + u * (jnp.exp(u * u * -0.5) * 0.39894228040143268)


def norm(r):
    c = r - jnp.mean(r, axis=-1, keepdims=True)
    inv = lax.rsqrt(jnp.mean(c * c, axis=-1, keepdims=True) + EPS)
    return c * inv, inv


def norm_back(g, n, inv, gain):
    t = g * gain
    return inv * (t - jnp.mean(t, axis=-1, keepdims=True) - n * jnp.mean(t * n, axis=-1, keepdims=True))


def row_sum(x):
    return jnp.sum(x, axis=0, keepdims=True)


def halves(x):
    low = lax.broadcasted_iota(jnp.int32, x.shape, 1) < HD
    zero = jnp.zeros_like(x)
    return jnp.where(low, x, zero), jnp.where(low, zero, x)


def two(x):
    return jnp.concatenate(halves(x), axis=0)


def softmax(t):
    t = jnp.exp(t - jnp.max(t, axis=-1, keepdims=True))
    return (t * (1.0 / jnp.sum(t, axis=-1, keepdims=True))).astype(bf16)


def start_all(sems, *pairs):
    copies = [pltpu.make_async_copy(a, b, sems.at[n]) for n, (a, b) in enumerate(pairs)]
    for c in copies:
        c.start()
    return copies


def bias_row(bias, j):
    k = CHUNK // 128
    rows = bias[...].astype(f32)
    return jnp.concatenate([rows[j * k + m:j * k + m + 1] for m in range(k)], axis=1)


def whole(a):
    return pl.BlockSpec(a.shape, lambda i, n=len(a.shape): (0,) * n)


def split_of(members, n, spread, D):
    per = n * D // members if spread else D // members
    return None if per % 16 or TILE % (2 * per) else (per, D // (2 * per) if spread else 0)


def grad_outs(members, n, spread, D, extra=0):
    split = split_of(members, n, spread, D)
    if not split:
        return [S((n, D, D), bf16)], [V((n, D, D), bf16), pltpu.SemaphoreType.DMA((n, 2))]
    per, step = split
    rows = per if spread else n * per
    return [S((members // 2, rows + extra, D), bf16)] * 2, [V((n, D // (2 * per), 2, per, D), bf16), pltpu.SemaphoreType.DMA((n, 2))]


def placed_at(m, bits, core):
    if bits < 2:
        return m
    low, next_, high = m & 1, (m >> 1) & 1, m >> 2
    first = (low << (bits - 1)) | (high << 1) | next_
    second = (next_ << (bits - 1)) | (high << 1) | low
    return jnp.where(core == 0, first, second)


def emit_grads(split, core, left, right, outs, stage, sems):
    n, D = stage.shape[0], stage.shape[-1]
    bits = outs[0].shape[0].bit_length() - 1

    def copies(j):
        if not split:
            return [pltpu.make_async_copy(stage.at[j], outs[0].at[j], sems.at[j, 0])]
        per, step = split
        res = []
        for k in range(stage.shape[1]):
            m = j * step + k if step else k
            theirs, ours = placed_at(m, bits, 1 - core), placed_at(m, bits, core)
            rows = pl.ds(0, per) if step else pl.ds(j * per, per)
            res += [pltpu.make_async_copy(stage.at[j, k, 1 - core], outs[0].at[theirs, rows], sems.at[j, 0]),
                    pltpu.make_async_copy(stage.at[j, k, core], outs[1].at[ours, rows], sems.at[j, 1])]
        return res

    for j in range(n):
        for t in range(D // TILE):
            res = tn(left(j, slice(t * TILE, (t + 1) * TILE)), right(j)).astype(bf16)
            if split:
                k = TILE // (2 * split[0])
                stage[j, t * k:(t + 1) * k] = res.reshape((k, 2, split[0], D))
            else:
                stage[j, t * TILE:(t + 1) * TILE, :] = res
        for x in copies(j):
            x.start()

    def end():
        for j in range(n):
            for x in copies(j):
                x.wait()

    return end


def forward_kernel(n_docs, split, n_grads, meta, lengths, tok, cot, mask, wqkv_h, wo_h, wu_h, wd_h, bias, gains, shifts, *rest):
    (q_o, k_o, v_o, p_o, ob_o, n_o, inv_o, dg_o, gr2_o, mixed_o, pack_o, small_o), rest = rest[:12], rest[12:]
    grads, (wqkv, wo, wu, wd, y1b, gb_s, gm_s, sems, stage, gsems) = rest[:n_grads], rest[n_grads:]
    i = pl.program_id(0)
    segs, pairs = p_o.shape[0], p_o.shape[1]
    B, D = tok.shape
    L = B // segs
    n = wu.shape[0]
    ga, sh = gains[...].astype(f32), shifts[...].astype(f32)
    cs = [slice(c * CHUNK, (c + 1) * CHUNK) for c in range(n)]
    load = lambda a, b, m: pltpu.make_async_copy(a, b, sems.at[m])
    first = [load(wqkv_h, wqkv, 0), load(wo_h, wo, 1)]
    ups = [load(wu_h.at[:, c], wu.at[j], 2 + j) for j, c in enumerate(cs)]
    downs = [load(wd_h.at[c, :], wd.at[j], 2 + n + j) for j, c in enumerate(cs)]

    @pl.when(i == 0)
    def _():
        for c in first + ups + downs:
            c.start()
        small_o[...] = jnp.zeros_like(small_o)
        first[0].wait()

    hb = tok[...]
    q_o[...] = ((nn(hb, wqkv[0]) + sh[0:1]) * 0.125).astype(bf16)
    k_o[...] = nn(hb, wqkv[1]).astype(bf16)
    v_o[...] = (nn(hb, wqkv[2]) + sh[1:2]).astype(bf16)
    col = [slice(j * PAIR, (j + 1) * PAIR) for j in range(pairs)]
    for s in range(segs):
        rows = slice(s * L, (s + 1) * L)
        live = jnp.where(mask[pl.ds(i * segs + s, 1), :] > 0, 0.0, NEG).astype(f32)
        scores = [nt(q_o[rows, c], two(k_o[rows, c])) for c in col]
        probs = [jnp.concatenate([softmax(t[:, e:e + L] + live) for e in (0, L)], axis=1) for t in scores]
        for j, c in enumerate(col):
            p_o[s, j] = probs[j]
            ob_o[rows, c] = nn(probs[j], two(v_o[rows, c])).astype(bf16)

    @pl.when(i == 0)
    def _():
        for c in first[1:] + ups + downs:
            c.wait()

    n1, inv1 = norm(hb.astype(f32) + nn(ob_o[...], wo[...]) + sh[2:3])
    n_o[...] = n1
    inv_o[...] = inv1
    y1 = n1 * ga[0:1] + sh[3:4]
    y1b[...] = y1.astype(bf16)
    up = lambda j: nn(y1b[...], wu[j]) + bias_row(bias, j)
    here = pl.ds(pl.multiple_of(i * B, B), B)
    u, acc = up(0), y1 + sh[4:5]
    for j in range(n):
        after = up(j + 1) if j + 1 < n else None
        g, d = gelu_both(u)
        gb = g.astype(bf16)
        gb_s[j, here, :] = gb
        dg_o[j] = d.astype(bf16)
        acc = acc + nn(gb, wd[j])
        u = after
    n2, inv2 = norm(acc)
    mixed_o[...] = (n2 * ga[1:2] + sh[5:6]).astype(bf16)
    row = lax.broadcasted_iota(jnp.int32, n2.shape, 0)
    gz = jnp.where(row % L == 0, 0.0, cot[...].astype(f32))
    small_o[0:1, :] += row_sum(gz * n2)
    small_o[1:2, :] += row_sum(gz)
    gr2 = norm_back(gz, n2, inv2, ga[1:2])
    gr2_o[...] = gr2
    gm = gr2.astype(bf16)
    gm_s[here, :] = gm
    small_o[2:3, :] += row_sum(gm.astype(f32))

    lane = lax.broadcasted_iota(jnp.int32, (1, 128), 1)
    for s in range(segs):
        g = (i * segs + s) * meta[2] + meta[0]
        before, doc, pos = jnp.int32(0), meta[1] * 32, g
        for d in range(n_docs):
            before = before + lengths[0, d]
            passed = g >= before
            doc = doc + passed.astype(jnp.int32)
            pos = jnp.where(passed, g - before, pos)
        extra = jnp.where(lane == 0, doc, jnp.where(lane == 1, pos, 0)).astype(f32)
        top = slice(s * L, s * L + 1)
        high = inv1[top].astype(bf16).astype(f32)
        extra = jnp.where(lane == 2, high, jnp.where(lane == 3, inv1[top] - high, extra))
        pack_o[s, :, :D] = n1[top].astype(bf16)
        pack_o[s, :, D:2 * D] = cot[s * L:s * L + 16, :][0:1]
        pack_o[s, :, 2 * D:] = extra.astype(bf16)

    @pl.when(i == pl.num_programs(0) - 1)
    def _():
        emit_grads(split, meta[3], lambda j, c: gb_s[j, :, c], lambda j: gm_s[...], grads, stage, gsems)()


def forward(meta, lengths, tok, cot, mask, wqkv, wo, wu, wd, bias, gains, shifts, members, step=2):
    T, D = tok.shape
    segs_dev, L = mask.shape
    pairs, B, n = D // PAIR, L * step, wu.shape[1] // CHUNK
    rowblk = pl.BlockSpec((B, D), lambda i: (i, 0))
    wide = pl.BlockSpec((n, B, CHUNK), lambda i: (0, i, 0))
    row = lambda dt: (S((T, D), dt), rowblk)
    outs = [row(bf16), row(bf16), row(bf16),
            (S((segs_dev, pairs, L, 2 * L), bf16), pl.BlockSpec((step, pairs, L, 2 * L), lambda i: (i, 0, 0, 0))),
            row(bf16), row(f32), (S((T, 1), f32), pl.BlockSpec((B, 1), lambda i: (i, 0))), (S((n, T, CHUNK), bf16), wide),
            row(f32), row(bf16),
            (S((segs_dev, 1, 2 * D + 128), bf16), pl.BlockSpec((step, 1, 2 * D + 128), lambda i: (i, 0, 0))),
            (S((8, D), f32), whole(S((8, D), f32)))]
    grads, scratch = grad_outs(members, n, True, D)
    return pl.pallas_call(
        functools.partial(forward_kernel, lengths.shape[1], split_of(members, n, True, D), len(grads)),
        grid=(segs_dev // step,),
        in_specs=[SM, SM, rowblk, rowblk, whole(mask), ANY, ANY, ANY, ANY, whole(bias), whole(gains), whole(shifts)],
        out_specs=[o[1] for o in outs] + [ANY] * len(grads),
        out_shape=[o[0] for o in outs] + grads,
        scratch_shapes=[V(wqkv.shape, bf16), V(wo.shape, bf16), V((n, D, CHUNK), bf16), V((n, CHUNK, D), bf16), V((B, D), bf16), V((n, T, CHUNK), bf16),
                        V((T, D), bf16), pltpu.SemaphoreType.DMA((2 + 2 * n,))] + scratch,
        compiler_params=PARAMS,
        name="seg_forward", cost_estimate=cost(30),
    )(meta, lengths, tok, cot, mask, wqkv, wo, wu, wd, bias, gains, shifts)


def ffn_back_kernel(split, n_grads, meta, n1, inv1, dg, gr2, wu_h, wd_h, gains, shifts, gr1_o, gbias_o, small_o, *rest):
    grads, (wu, wd, gm, y1b_s, gu_s, sems, stage, gsems) = rest[:n_grads], rest[n_grads:]
    i = pl.program_id(0)
    n = wu.shape[0]
    B = n1.shape[0]
    cs = [slice(c * CHUNK, (c + 1) * CHUNK) for c in range(n)]
    ups = [pltpu.make_async_copy(wu_h.at[:, c], wu.at[j], sems.at[0, j]) for j, c in enumerate(cs)]
    downs = [pltpu.make_async_copy(wd_h.at[c, :], wd.at[j], sems.at[1, j]) for j, c in enumerate(cs)]
    order = [c for pair in zip(downs, ups) for c in pair]

    @pl.when(i == 0)
    def _():
        for c in order[:3]:
            c.start()
        small_o[...] = jnp.zeros_like(small_o)
        gbias_o[...] = jnp.zeros_like(gbias_o)

    def await_first(m, count):
        @pl.when(i == 0)
        def _():
            for k in range(m, min(m + count, 2 * n)):
                order[k].wait()
                if k + 3 < 2 * n:
                    order[k + 3].start()

    here = pl.ds(pl.multiple_of(i * B, B), B)
    n1v, gfirst = n1[...], gains[...].astype(f32)[0:1]
    y1b_s[here, :] = (n1v * gfirst + shifts[...].astype(f32)[3:4]).astype(bf16)
    acc = gr2[...]
    gm[...] = acc.astype(bf16)
    await_first(0, 1)
    t = nt(gm[...], wd[0])
    for j in range(n):
        await_first(2 * j + 1, 2)
        after = nt(gm[...], wd[j + 1]) if j + 1 < n else None
        gu = (t * dg[j].astype(f32)).astype(bf16)
        gu_s[j, here, :] = gu
        gbias_o[j:j + 1, :] += row_sum(gu.astype(f32))
        acc = acc + nt(gu, wu[j])
        t = after
    small_o[0:1, :] += row_sum(acc * n1v)
    small_o[1:2, :] += row_sum(acc)
    gr1_o[...] = norm_back(acc, n1v, inv1[...], gfirst)

    @pl.when(i == pl.num_programs(0) - 1)
    def _():
        emit_grads(split, meta[3], lambda j, c: y1b_s[:, c], lambda j: gu_s[j], grads, stage, gsems)()


def ffn_back(meta, n1, inv1, dg, gr2, wu, wd, gains, shifts, members, B=256):
    T, D = n1.shape
    n = wu.shape[1] // CHUNK
    rowblk = pl.BlockSpec((B, D), lambda i: (i, 0))
    grads, scratch = grad_outs(members, n, False, D)
    shapes = [S((T, D), f32), S((8, CHUNK), f32), S((8, D), f32)]
    return pl.pallas_call(
        functools.partial(ffn_back_kernel, split_of(members, n, False, D), len(grads)),
        grid=(T // B,),
        in_specs=[SM, rowblk, pl.BlockSpec((B, 1), lambda i: (i, 0)), pl.BlockSpec((n, B, CHUNK), lambda i: (0, i, 0)), rowblk,
                  ANY, ANY, whole(gains), whole(shifts)],
        out_specs=[rowblk, whole(shapes[1]), whole(shapes[2])] + [ANY] * len(grads),
        out_shape=shapes + grads,
        scratch_shapes=[V((n, D, CHUNK), bf16), V((n, CHUNK, D), bf16), V((B, D), bf16), V((T, D), bf16), V((n, T, CHUNK), bf16),
                        pltpu.SemaphoreType.DMA((2, n))] + scratch,
        compiler_params=PARAMS,
        name="seg_ffn_back", cost_estimate=cost(20),
    )(meta, n1, inv1, dg, gr2, wu, wd, gains, shifts)


def with_cls(rows, cls):
    row = lax.broadcasted_iota(jnp.int32, (rows.shape[0], 1), 0)
    for s in range(cls.shape[0]):
        rows = jnp.where(row == s * (rows.shape[0] // cls.shape[0]), cls[s], rows)
    return rows


def input_grad_kernel(gr1, gr1c, qk0, qk1, vv, wqkv, o):
    H = qk0.shape[1] // 2
    part = lambda a: jnp.concatenate([qk0[:, a:a + H], qk1[:, a:a + H]], axis=1)
    o[...] = (with_cls(gr1[...], gr1c) + nt(part(0), wqkv[0]) + nt(part(H), wqkv[1]) + nt(vv[...], wqkv[2])).astype(bf16)


def input_grad(gr1, gr1c, qk0, qk1, vv, wqkv, step=2):
    T, D = gr1.shape
    segs = gr1c.shape[0]
    rowblk = pl.BlockSpec((T // segs * step, D), lambda i: (i, 0))
    return pl.pallas_call(
        input_grad_kernel,
        grid=(segs // step,),
        in_specs=[rowblk, pl.BlockSpec((step, 1, D), lambda i: (i, 0, 0)), rowblk, rowblk, rowblk, whole(wqkv)],
        out_specs=rowblk,
        out_shape=S((T, D), bf16),
        compiler_params=PARAMS,
        name="input_grad", cost_estimate=cost(6),
    )(gr1, gr1c, qk0, qk1, vv, wqkv)


def attn_back_kernel(split, n_grads, is_last, meta, *rest):
    if is_last:
        (first_v, small_f, small_b, sums_a, gbias, ga_in), rest = rest[:6], rest[6:]
    else:
        (gr1, gr1c, ob), rest = rest[:3], rest[3:]
    (p, q, k, v, tok, wo), rest = rest[:6], rest[6:]
    if is_last:
        (qk_o, vv_o, vec_o), rest = rest[:3], rest[3:]
    else:
        (qk_o, ga_o, first_v_o, sums_o), rest = rest[:4], rest[4:]
    grads, rest = rest[:n_grads], rest[n_grads:]
    go_s, g_s, left_s, sums, rest = *rest[:4], rest[4:]
    if is_last:
        vec_s, wsems, rest = *rest[:2], rest[2:]
    stage, gsems = rest
    i = pl.program_id(0)
    segs, pairs = p.shape[0], p.shape[1]
    B, D = tok.shape
    L, H = B // segs, pairs * PAIR
    here = pl.ds(pl.multiple_of(i * B, B), B)

    @pl.when(i == 0)
    def _():
        sums[...] = jnp.zeros_like(sums)

    left_s[0, here, :] = tok[...]
    if is_last:
        ga = ga_in[...]
    else:
        ga = with_cls(gr1[...], gr1c).astype(bf16)
        ga_o[...] = ga
        g_s[1, here, :] = ga
        left_s[1, here, :] = ob[...]
    go_s[...] = nt(ga, wo[...]).astype(bf16)
    col = [slice(j * PAIR, (j + 1) * PAIR) for j in range(pairs)]
    beside = lambda c: slice(H + c.start, H + c.stop)
    eighth = jnp.asarray(0.125, bf16)
    for s in range(segs):
        rows = slice(s * L, (s + 1) * L)
        out = pl.ds(pl.multiple_of(i * B, B) + s * L, L)
        gps = [nt(go_s[rows, c], two(v[rows, c])) for c in col]
        for j, c in enumerate(col):
            pb = p[s, j]
            gv = tn(jnp.concatenate([pb[:, :L], pb[:, L:]], axis=0), two(go_s[rows, c])).astype(bf16)
            if is_last:
                g_s[1, out, beside(c)] = gv
            else:
                first_v_o[rows, c] = gv
        gss = []
        for j, gp in enumerate(gps):
            pf = p[s, j].astype(f32)
            gs = []
            for e in (0, L):
                pe, ge = pf[:, e:e + L], gp[:, e:e + L]
                gs.append((pe * (ge - jnp.sum(pe * ge, axis=-1, keepdims=True))).astype(bf16))
            gss.append(gs)
        for c, gs in zip(col, gss):
            g_s[0, out, c] = nn(jnp.concatenate(gs, axis=1), two(k[rows, c])).astype(bf16) * eighth
            g_s[0, out, beside(c)] = tn(jnp.concatenate(gs, axis=0), two(q[rows, c])).astype(bf16)
    if is_last:
        g_s[1, here, :H] = first_v[...]
        vv_o[...] = g_s[1, here, :]
    qk_o[...] = g_s[0, here, :]
    for m in range(2):
        sums[m:m + 1, :] += row_sum(g_s[m, here, :].astype(f32))

    @pl.when(i == pl.num_programs(0) - 1)
    def _():
        tail = []
        if is_last:
            vec = jnp.concatenate([
                gbias[0:4, :], small_b[0:1, :], small_f[0:1, :], jnp.concatenate([sums_a[0:1, :H], sums[0:1, :H]], axis=1), sums[1:2, :],
                sums_a[1:2, :], small_b[1:2, :], small_f[2:3, :], small_f[1:2, :], jnp.zeros((4, D), f32)], axis=0)
            vec_o[...] = vec
            if split:
                for m in range(vec_s.shape[0]):
                    vec_s[m] = vec.astype(bf16)
                tail = [pltpu.make_async_copy(vec_s, h.at[:, pl.ds(h.shape[1] - SMALL_ROWS, SMALL_ROWS)], wsems.at[m]) for m, h in enumerate(grads)]
        else:
            sums_o[...] = sums[...]
        for x in tail:
            x.start()
        emit_grads(split, meta[3], lambda j, c: left_s[0 if is_last else j, :, c], lambda j: g_s[j], grads, stage, gsems)()
        for x in tail:
            x.wait()


def attn_back(meta, before_it, p, q, k, v, tok, wo, members, is_last, step=2):
    T, D = tok.shape
    segs_dev, all_pairs, L = p.shape[:3]
    pairs, H, half = all_pairs // 2, D // 2, int(is_last)
    B = L * step
    rowblk = pl.BlockSpec((B, D), lambda i: (i, 0))
    halfblk = pl.BlockSpec((B, H), lambda i: (i, half))
    firstblk = pl.BlockSpec((B, H), lambda i: (i, 0))
    split = split_of(members, 2, False, D)
    grads, scratch = grad_outs(members, 2, False, D, SMALL_ROWS if is_last else 0)
    small = S((8, D), f32)
    if is_last:
        vec = S((SMALL_ROWS, D), f32)
        specs = [firstblk] + [whole(x) for x in before_it[1:5]] + [rowblk]
        outs = [(S((T, D), bf16), rowblk), (S((T, D), bf16), rowblk), (vec, whole(vec))]
        more = [V((members // 2, SMALL_ROWS, D), bf16), pltpu.SemaphoreType.DMA((2,))]
    else:
        specs = [rowblk, pl.BlockSpec((step, 1, D), lambda i: (i, 0, 0)), rowblk]
        outs = [(S((T, D), bf16), rowblk), (S((T, D), bf16), rowblk), (S((T, H), bf16), firstblk), (small, whole(small))]
        more = []
    return pl.pallas_call(
        functools.partial(attn_back_kernel, split, len(grads), is_last),
        grid=(segs_dev // step,),
        in_specs=[SM] + specs + [pl.BlockSpec((step, pairs, L, 2 * L), lambda i: (i, half, 0, 0)), halfblk, halfblk, halfblk, rowblk,
                                 pl.BlockSpec((H, D), lambda i: (half, 0))],
        out_specs=[o[1] for o in outs] + [ANY] * len(grads),
        out_shape=[o[0] for o in outs] + grads,
        scratch_shapes=[V((B, H), bf16), V((2, T, D), bf16), V((2, T, D), bf16), V((8, D), f32)] + more + scratch,
        compiler_params=PARAMS,
        name="seg_attention_back", cost_estimate=cost(12),
    )(meta, *before_it, p, q, k, v, tok, wo)


def onehot(rows, width, start):
    at = lax.broadcasted_iota(jnp.int32, (rows, width), 0) + start
    return (at == lax.broadcasted_iota(jnp.int32, (rows, width), 1)).astype(bf16)


def nt_exact(x, pick):
    a = x.astype(bf16)
    rest = x - a.astype(f32)
    b = rest.astype(bf16)
    return nt(a, pick) + nt(b, pick) + nt((rest - b.astype(f32)).astype(bf16), pick)


def own_vectors(vec, member, r, F):
    D = vec.shape[1]
    wide = F // D
    per = r * wide
    fits = D // per
    parts = nt_exact(vec, onehot(per, D, lax.rem(member, fits) * per))
    line = lax.broadcasted_iota(jnp.int32, parts.shape, 0)
    bias = row_sum(jnp.where(line == lax.div(member, fits), parts, 0.0))
    rest = nt_exact(vec, onehot(r, D, member * r))
    return bias, rest[wide:wide + 2], rest[wide + 2:wide + 8]


def cross_kernel(r, meta, rows_in, mixed_h, swu_h, swd_h, xqkv_h, xo_h, xu_h, xd_h, sbias, sgains, sshifts, xbias, xgains, xshifts, pos,
                 mixed_o, gr1_o, svec_o, gqkv_o, go_o, gu_o, gd_o, gbias_o, ggains_o, gshifts_o, gpos_o, sgu_o, sgd_o,
                 swu, swd, xqkv, xo, xu, xd, sgb, sdg, xgb, xdg, sgu, xgu, q_s, k_s, v_s, p_s, o_s, go_s, gq_s, gk_s, gv_s, hb_s, z1_s, y1_s,
                 cls_s, gr1_s, vec_s, svec_s, patch, sems, psems):
    n, D = swu.shape[0], swu.shape[1]
    R = rows_in.shape[0]
    cs = [slice(c * CHUNK, (c + 1) * CHUNK) for c in range(n)]
    col = [slice(c, c + PAIR) for c in range(0, D, PAIR)]
    queue = []
    for wu_h, wd_h, wu, wd in ((swu_h, swd_h, swu, swd), (xu_h, xd_h, xu, xd)):
        for j, c in enumerate(cs):
            queue += [(wu_h.at[:, c], wu.at[j]), (wd_h.at[c, :], wd.at[j])]
    queue[2 * n:2 * n] = [(xqkv_h.at[m], xqkv.at[m]) for m in range(3)] + [(xo_h, xo)]
    copies = [pltpu.make_async_copy(a, b, sems.at[m]) for m, (a, b) in enumerate(queue)]
    ahead, waited = 4, [0]
    for x in copies[:ahead]:
        x.start()

    def need(count):
        for _ in range(count):
            m = waited[0]
            copies[m].wait()
            if m + ahead < len(copies):
                copies[m + ahead].start()
            waited[0] = m + 1

    segs, L = patch.shape[0], mixed_h.shape[0] // patch.shape[0]
    fetch = [pltpu.make_async_copy(mixed_h.at[pl.ds(s * L, 16), :], patch.at[s], psems.at[s]) for s in range(segs)]
    for x in fetch:
        x.start()
    sg, ss = sgains[...].astype(f32), sshifts[...].astype(f32)
    xg, xs = xgains[...].astype(f32), xshifts[...].astype(f32)
    eighth = jnp.asarray(0.125, bf16)

    def ffn_f(acc, yb, wu, wd, bias, gb_s, dg_s):
        def up(j):
            need(1)
            return nn(yb, wu[j]) + bias_row(bias, j)

        for j in range(n):
            g, d = gelu_both(up(j))
            gb = g.astype(bf16)
            gb_s[:, cs[j]] = gb
            dg_s[:, cs[j]] = d.astype(bf16)
            need(1)
            acc = acc + nn(gb, wd[j])
        return acc

    def ffn_b(acc, gm, wu, wd, dg_s, gu_s, vec):
        t = nt(gm, wd[0])
        for j in range(n):
            after = nt(gm, wd[j + 1]) if j + 1 < n else None
            gu = (t * dg_s[:, cs[j]].astype(f32)).astype(bf16)
            gu_s[:, cs[j]] = gu
            vec[j:j + 1, :] = row_sum(gu.astype(f32))
            acc = acc + nt(gu, wu[j])
            t = after
        return acc

    vec_s[...] = jnp.zeros_like(vec_s)
    svec_s[...] = jnp.zeros_like(svec_s)
    n1 = rows_in[:, :D].astype(f32)
    extra = rows_in[:, 2 * D:].astype(f32)
    spos = extra[:, 1:2].astype(jnp.int32)
    inv1 = extra[:, 2:3] + extra[:, 3:4]
    lane = lax.broadcasted_iota(jnp.int32, (8, extra.shape[1]), 1)
    did_row = nt((lane == 0).astype(bf16), extra.astype(bf16))[0:1]
    allowed = extra[:, 0:1] == did_row
    placed = (lax.broadcasted_iota(jnp.int32, (R, pos.shape[0]), 1) == spos).astype(bf16)

    y1 = n1 * sg[0:1] + ss[3:4]
    y1b = y1.astype(bf16)
    n2, inv2 = norm(ffn_f(y1 + ss[4:5], y1b, swu, swd, sbias, sgb, sdg))
    h = n2 * sg[1:2] + ss[5:6] + nn(placed, pos[...])

    hb = h.astype(bf16)
    need(1)
    q_s[...] = ((nn(hb, xqkv[0]) + xs[0:1]) * 0.125).astype(bf16)
    need(1)
    k_s[...] = nn(hb, xqkv[1]).astype(bf16)
    need(1)
    v_s[...] = (nn(hb, xqkv[2]) + xs[1:2]).astype(bf16)
    early = R <= 256
    pair_scores = lambda c: [nt(x, k_s[:, c]) for x in halves(q_s[:, c])]
    scores = [pair_scores(c) for c in col] if early else None
    for j, c in enumerate(col):
        out, v2 = 0.0, halves(v_s[:, c])
        sc = scores[j] if early else pair_scores(c)
        for e in range(2):
            pb = softmax(jnp.where(allowed, sc[e], NEG))
            p_s[2 * j + e] = pb
            out = out + nn(pb, v2[e])
        o_s[:, c] = out.astype(bf16)
    need(1)
    m1, minv1 = norm(h + nn(o_s[...], xo[...]) + xs[2:3])
    z1 = m1 * xg[0:1] + xs[3:4]
    z1b = z1.astype(bf16)
    m2, minv2 = norm(ffn_f(z1 + xs[4:5], z1b, xu, xd, xbias, xgb, xdg))
    cls_s[...] = m2 * xg[1:2] + xs[5:6]

    gz = rows_in[:, D:2 * D].astype(f32)
    vec_s[n + 1:n + 2, :] = row_sum(gz * m2)
    vec_s[n + 7:n + 8, :] = row_sum(gz)
    gr2 = norm_back(gz, m2, minv2, xg[1:2])
    xgm = gr2.astype(bf16)
    vec_s[n + 6:n + 7, :] = row_sum(xgm.astype(f32))
    gy1 = ffn_b(gr2, xgm, xu, xd, xdg, xgu, vec_s)
    vec_s[n:n + 1, :] = row_sum(gy1 * m1)
    vec_s[n + 5:n + 6, :] = row_sum(gy1)
    gr1 = norm_back(gy1, m1, minv1, xg[0:1])
    xga = gr1.astype(bf16)
    vec_s[n + 4:n + 5, :] = row_sum(xga.astype(f32))
    go_s[...] = nt(xga, xo[...]).astype(bf16)
    pair_gps = lambda c: [nt(x, v_s[:, c]) for x in halves(go_s[:, c])]
    gps = [pair_gps(c) for c in col] if early else None
    for j, c in enumerate(col):
        gpj = gps[j] if early else pair_gps(c)
        q2, k2, g2 = halves(q_s[:, c]), halves(k_s[:, c]), halves(go_s[:, c])
        gq = gk = gv = 0.0
        for e in range(2):
            pb = p_s[2 * j + e]
            pf = pb.astype(f32)
            gp = gpj[e]
            gs = (pf * (gp - jnp.sum(pf * gp, axis=-1, keepdims=True))).astype(bf16)
            gq = gq + nn(gs, k2[e])
            gk = gk + tn(gs, q2[e])
            gv = gv + tn(pb, g2[e])
        gq_s[:, c] = gq.astype(bf16) * eighth
        gk_s[:, c] = gk.astype(bf16)
        gv_s[:, c] = gv.astype(bf16)
    vec_s[n + 2:n + 3, :] = row_sum(gq_s[...].astype(f32))
    vec_s[n + 3:n + 4, :] = row_sum(gv_s[...].astype(f32))
    gcls = gr1 + nt(gq_s[...], xqkv[0]) + nt(gk_s[...], xqkv[1]) + nt(gv_s[...], xqkv[2])

    svec_s[n + 1:n + 2, :] = row_sum(gcls * n2)
    svec_s[n + 7:n + 8, :] = row_sum(gcls)
    gr2 = norm_back(gcls, n2, inv2, sg[1:2])
    sgm = gr2.astype(bf16)
    svec_s[n + 6:n + 7, :] = row_sum(sgm.astype(f32))
    gy1 = ffn_b(gr2, sgm, swu, swd, sdg, sgu, svec_s)
    svec_s[n:n + 1, :] = row_sum(gy1 * n1)
    svec_s[n + 5:n + 6, :] = row_sum(gy1)
    gr1_s[...] = norm_back(gy1, n1, inv1, sg[0:1])
    svec_o[...] = svec_s[...]

    for x in fetch:
        x.wait()
    top = lax.broadcasted_iota(jnp.int32, (16, 1), 0) == 0
    for s in range(segs):
        line = pl.ds(meta[4] + s, 1)
        gr1_o[s] = gr1_s[line, :]
        patch[s] = jnp.where(top, cls_s[line, :], patch[s].astype(f32)).astype(bf16)
    store = [pltpu.make_async_copy(patch.at[s], mixed_o.at[pl.ds(s * L, 16), :], psems.at[s]) for s in range(segs)]
    for x in store:
        x.start()

    member = meta[0]
    pick = onehot(r, D, member * r)
    window = 256

    def own(x, count):
        width = x.shape[1]
        at_col = jnp.minimum(lax.div(member * count, 128) * 128, width - window)
        near = x[:, pl.ds(pl.multiple_of(at_col, 128), window)]
        return nt(onehot(count, window, member * count - at_col), near).astype(bf16)

    hb_s[...] = hb
    z1_s[...] = z1b
    y1_s[...] = y1b
    hbt = own(hb_s, r)
    for m, g in enumerate((gq_s, gk_s, gv_s)):
        gqkv_o[m] = nn(hbt, g[...])
    go_o[...] = nn(own(o_s, r), xga)
    gd_o[...] = nn(own(xgb, r * n), xgm)
    sgd_o[...] = nn(own(sgb, r * n), sgm)
    z1t, y1t = own(z1_s, r), own(y1_s, r)
    for c in cs:
        gu_o[:, c] = nn(z1t, xgu[:, c])
        sgu_o[:, c] = nn(y1t, sgu[:, c])
    bias, gains, shifts = own_vectors(vec_s[...], member, r, n * D)
    gbias_o[...] = bias
    ggains_o[...] = gains
    gshifts_o[...] = shifts
    gown = nt_exact(gcls, pick)
    high = gown.astype(bf16)
    gpos_o[...] = tn(placed, high) + tn(placed, (gown - high.astype(f32)).astype(bf16))
    for x in store:
        x.wait()


def cross(meta, rows_in, mixed, seg_params, cross_params, pos, segs, r):
    swu, swd, sbias, sgains, sshifts = seg_params
    xqkv, xo, xu, xd, xbias, xgains, xshifts = cross_params
    R = rows_in.shape[0]
    D, F = swu.shape
    n = F // CHUNK
    outs = [S(mixed.shape, bf16), S((segs, 1, D), f32), S((SMALL_ROWS, D), f32), S((3, r, D), f32), S((r, D), f32), S((r, F), f32),
            S((r * n, D), f32), S((1, r * n), f32), S((2, r), f32), S((6, r), f32), S((pos.shape[0], r), f32), S((r, F), f32), S((r * n, D), f32)]
    up, down, row = V((n, D, CHUNK), bf16), V((n, CHUNK, D), bf16), V((R, D), bf16)
    return pl.pallas_call(
        functools.partial(cross_kernel, r),
        in_specs=[SM, VM] + [ANY] * 7 + [VM] * 7,
        out_specs=[ANY] + [VM] * (len(outs) - 1),
        out_shape=outs,
        scratch_shapes=[up, down, V(xqkv.shape, bf16), V(xo.shape, bf16), up, down] + [V((R, F), bf16)] * 6 + [row] * 3
        + [V((D // HD, R, R), bf16)] + [row] * 8 + [V((R, D), f32)] * 2 + [V((SMALL_ROWS, D), f32)] * 2
        + [V((segs, 16, D), bf16), pltpu.SemaphoreType.DMA((4 * n + 4,)), pltpu.SemaphoreType.DMA((segs,))],
        input_output_aliases={2: 0},
        compiler_params=PARAMS,
        name="cross_block", cost_estimate=cost(28),
    )(meta, rows_in, mixed, swu, swd, xqkv, xo, xu, xd, sbias, sgains, sshifts, xbias, xgains, xshifts, pos)


def finish_kernel(r, F, routed, meta, *rest):
    ins, (w_o, o_o, bias_o, gains_o, shifts_o) = rest[:-5], rest[-5:]
    if routed:
        lower = meta[1] == 0
        totals = []
        for x, other in (ins[0:2], ins[2:4]):
            a, b = x[...].astype(f32), other[...].astype(f32)
            totals.append(jnp.concatenate([jnp.where(lower, a, b), jnp.where(lower, b, a)], axis=0))
    else:
        totals = [ins[0][...], ins[1][...]]
    a, b = totals
    H = a.shape[1] // 2
    for m in range(2):
        w_o[m] = jnp.concatenate([a[:r, m * H:(m + 1) * H], b[:r, m * H:(m + 1) * H]], axis=1)
    w_o[2] = b[r:2 * r]
    o_o[...] = a[r:2 * r]
    bias, gains, shifts = own_vectors(b[2 * r:] + ins[-1][...], meta[0], r, F)
    bias_o[...] = bias
    gains_o[...] = gains
    shifts_o[...] = shifts


def finish(meta, parts, vec_c, r, F, routed):
    D = vec_c.shape[1]
    outs = [S((3, r, D), f32), S((r, D), f32), S((1, r * (F // D)), f32), S((2, r), f32), S((6, r), f32)]
    return pl.pallas_call(
        functools.partial(finish_kernel, r, F, routed), in_specs=[SM] + [VM] * (len(parts) + 1), out_specs=[VM] * len(outs), out_shape=outs,
        compiler_params=PARAMS, name="finish", cost_estimate=cost(2),
    )(meta, *parts, vec_c)


def add_up(a, b):
    return (a.astype(f32) + b.astype(f32)).astype(bf16)


def at(x, i, axis):
    return lax.dynamic_index_in_dim(x, i, axis, keepdims=False)


def fold(pieces, members, member):
    bits = members.bit_length() - 1
    x = pieces.reshape((2,) * bits + pieces.shape[1:])
    for bit in range(bits):
        axis = bits - 1 - bit
        mine = (member >> bit) & 1
        got = lax.ppermute(at(x, 1 - mine, axis), "seg", [(m, m ^ (1 << bit)) for m in range(members)])
        x = add_up(at(x, mine, axis), got)
    return x


def over_docs(x):
    docs = lax.axis_size("doc")
    total, part = x.astype(f32), x
    for _ in range(docs - 1):
        part = lax.ppermute(part, "doc", [(d, (d + 1) % docs) for d in range(docs)])
        total = total + part.astype(f32)
    return total


class Routed:
    def __init__(self, send, keep):
        self.members, member = lax.axis_size("seg"), lax.axis_index("seg")
        self.core, self.number = member & 1, lax.axis_index("doc") * self.members + member
        self.step, self.out = 0, [send]
        self.shape = (2, 2, 2, 2, send.shape[1] // 2, send.shape[2])
        self.terms, self.fresh = [(keep, ())], 0

    def bit(self, first, second):
        return jnp.where(self.core == 0, (self.number & first) != 0, (self.number & second) != 0).astype(jnp.int32)

    def sum(self, *choices):
        total = 0.0
        for x, path in self.terms:
            for axis, i in path + choices:
                x = at(x, i, axis)
            total = total + x.astype(f32)
        return total.astype(bf16)

    def ready(self):
        X, Z0, Z1, Y = 2, 4, 8, self.members
        if self.step == 1:
            self.terms = [(x.reshape(self.shape), path) for x, path in self.terms]
            b = self.bit(X, Z0)
            self.masks, self.out, self.choice = [(X, Z0)], [self.sum((0, 1 - b))], ((0, b),)
        elif self.step == 2:
            b, y = self.bit(Z0, X), self.bit(Y, Y)
            self.masks = [(Z0, X), (Y, Y), (Z0 + Y, X + Y)]
            self.out = [self.sum((1, i), (1, h)) for i, h in ((1 - b, y), (b, 1 - y), (1 - b, 1 - y))]
            self.choice = ((1, b), (1, y))
        elif self.step == 3:
            b = self.bit(Z1, Z1)
            self.terms, self.fresh = [(lax.optimization_barrier(self.sum()), ())], 0
            self.masks, self.out, self.choice = [(Z1, Z1)], [self.sum((0, 1 - b))], ((0, b),)
        else:
            self.masks, self.out = [(Y, Y)], [self.sum()]
        return self

    def go(self):
        masks = self.masks if self.step else [(1, 1)]
        got = [lax.ppermute(x, ("doc", "seg"), [(m, m ^ by[m & 1]) for m in range(2 * self.members)]) for x, by in zip(self.out, masks)]
        if self.step == 4:
            self.x = (self.out[0], got[0])
        elif self.step:
            self.terms = [(x, path + self.choice) for x, path in self.terms] + [(x, ()) for x in got]
        else:
            self.terms.append((got[0], ()))
        self.fresh = len(got)
        self.step += 1
        return self

    def hold(self, *arrays):
        old = self.terms[:len(self.terms) - self.fresh]
        vals = lax.optimization_barrier(tuple(x for x, _ in old) + arrays)
        self.terms = [(v, path) for v, (_, path) in zip(vals, old)] + self.terms[len(old):]
        return self

    def after(self, *others):
        return self.hold(*(x for f in others for x in f.out))


def before(x, *others):
    vals = [v for f in others for v in (f.out if isinstance(f, Routed) else [f])]
    res = lax.optimization_barrier((x, *vals))
    rest = list(res[1:])
    for f in others:
        if isinstance(f, Routed):
            f.out = [rest.pop(0) for _ in f.out]
        else:
            rest.pop(0)
    return res[0]


def join(x, other):
    a, b = x.astype(f32), other.astype(f32)
    lower = lax.axis_index("doc") == 0
    return jnp.concatenate([jnp.where(lower, a, b), jnp.where(lower, b, a)], axis=0)


def trade(x, mask):
    members = lax.axis_size("seg")
    return lax.ppermute(x, ("doc", "seg"), [(m, m ^ mask) for m in range(2 * members)])


def gather_start(x):
    Z1, Y = 8, lax.axis_size("seg")
    near, far, both = trade(x, Z1), trade(x, Y), trade(x, Y + Z1)
    mine, theirs = jnp.stack([x, near]), jnp.stack([far, both])
    lower = lax.axis_index("doc") == 0
    return jnp.stack([jnp.where(lower, mine, theirs), jnp.where(lower, theirs, mine)])


def gather_middle(x):
    X, Z0 = 2, 4
    return jnp.concatenate([x, trade(x, X), trade(x, Z0), trade(x, X + Z0)], axis=1)


def gather_end(x):
    return jnp.concatenate([x, trade(x, 1)], axis=1)


def shards(tokens, token_mask, doc_lengths, seg_qkv, seg_proj, seg_up, seg_down, seg_bias, seg_gains, seg_shifts,
           cross_qkv, cross_proj, cross_up, cross_down, cross_bias, cross_gains, cross_shifts, positions, cotangent):
    segs, L, D = tokens.shape
    F = seg_up.shape[1]
    members, member = lax.axis_size("seg"), lax.axis_index("seg")
    docs, doc = lax.axis_size("doc"), lax.axis_index("doc")
    r, wide, T = D // members, F // D, segs * L
    all_groups = docs * members * segs <= 256
    few = members == 16 and docs == 2
    place = (doc * members if few else doc * members + member if all_groups else member) * segs
    meta = jnp.stack([member, doc, jnp.int32(members), member & 1, place]).astype(jnp.int32)
    tok, cot = tokens.reshape(T, D), cotangent.reshape(T, D)
    bias, xbias = seg_bias.reshape(-1, 128), cross_bias.reshape(-1, 128)

    q, k, v, p, ob, n1, inv1, dg, gr2, mixed, pack, small_f, *gw_d = forward(
        meta, doc_lengths, tok, cot, token_mask, seg_qkv, seg_proj, seg_up, seg_down, bias, seg_gains, seg_shifts, members)
    routed = few and len(gw_d) == 2
    pack = pack.reshape(segs, -1)
    if few:
        pack = gather_start(pack)
    if routed:
        fold_d = Routed(*gw_d).go()
        inv1 = before(inv1, pack)
    gr1, gbias, small_b, *gw_u = ffn_back(meta, n1, inv1, dg, gr2, seg_up, seg_down, seg_gains, seg_shifts, members)
    if few:
        rows = gather_middle(pack)
    if routed:
        gw_u[0] = before(gw_u[0], fold_d.ready(), rows)
        fold_u = Routed(*gw_u).go()
    if few:
        rows = gather_end(rows).reshape(docs * members * segs, -1)
    else:
        rows = lax.all_gather(pack, ("doc", "seg") if all_groups else ("seg",), axis=0, tiled=True)
    if routed:
        rows = before(rows, fold_d)
        fold_d.go()
    mixed, gr1c, svec, *sums = cross(
        meta, rows, mixed, (seg_up, seg_down, bias, seg_gains, seg_shifts),
        (cross_qkv, cross_proj, cross_up, cross_down, xbias, cross_gains, cross_shifts), positions, segs, r)
    if routed:
        gr1c = before(gr1c, fold_d.ready(), fold_u.ready())
        fold_d.go()
        fold_u.go()
    qk0, ga, first_v, sums_a, *gw_a = attn_back(meta, (gr1, gr1c, ob), p, q, k, v, tok, seg_proj, members, False)
    if routed:
        gw_a[0] = before(gw_a[0], fold_d.ready(), fold_u.ready())
        ga = before(ga, fold_d, fold_u)
        fold_a = Routed(*gw_a).go()
        fold_d.go()
        fold_u.go()
    qk1, vv, vec, *gw_b = attn_back(meta, (first_v, small_f, small_b, sums_a, gbias, ga), p, q, k, v, tok, seg_proj, members, True)
    if routed:
        gw_b[0] = before(gw_b[0], fold_a.ready(), fold_d.ready(), fold_u.ready())
        fold_b = Routed(*gw_b).go()
        for f in (fold_a, fold_d, fold_u):
            f.go()

    if not all_groups:
        sums, svec = [over_docs(s.astype(bf16)) for s in sums], over_docs(svec.astype(bf16))
    gxqkv, gxo, gxu, gxd, gxbias, gxgains, gxshifts, gpos, gsu, gsd = sums

    if routed:
        gh = input_grad(gr1, gr1c, qk0, qk1, vv, seg_qkv)
        fold_b.hold(gh)
        for m in range(3):
            fold_b.ready()
            fold_a.after(fold_b)
            fold_b.go()
            fold_a.ready()
            fold_b.after(fold_a)
            fold_a.go()
        fold_b.ready().go()
        fold_u.ready().go()
        sum_d, sum_u = join(*fold_d.x), join(*fold_u.x)
        parts = fold_a.x + fold_b.x
    else:
        def whole_pieces(g, tall=False):
            if len(g) == 1:
                return g[0].reshape(members, -1, D) if tall else g[0].reshape(-1, members, r, D).swapaxes(0, 1).reshape(members, -1, D)
            send, keep = g
            c = member & 1
            first, second = jnp.where(c == 0, keep, send), jnp.where(c == 0, send, keep)
            if members > 4:
                apart = lambda x: x.reshape((2, -1, 2) + x.shape[1:])
                first = jnp.moveaxis(apart(first), 0, 2).reshape(first.shape)
                second = apart(second).swapaxes(0, 1).reshape(second.shape)
            both = jnp.stack([first, second], axis=1)
            return both.reshape(members, -1, D)

        pieces = [whole_pieces(gw_d, True)] + [whole_pieces(g) for g in (gw_u, gw_a, gw_b)]
        if len(gw_b) == 1:
            tail = jnp.broadcast_to(vec.astype(bf16)[None], (members, SMALL_ROWS, D))
            pieces[3] = jnp.concatenate([pieces[3], tail], axis=1)
        sum_d, sum_u, *parts = [over_docs(fold(x, members, member)) for x in pieces]
    if not routed:
        gh = input_grad(gr1, gr1c, qk0, qk1, vv, seg_qkv)
    gqkv, go, gb, gg, gs = finish(meta, parts, svec, r, F, routed)
    up = sum_u.reshape(wide, r, D).swapaxes(0, 1).reshape(r, F) + gsu
    return (
        mixed.reshape(segs, L, D), gh.reshape(segs, L, D),
        gqkv, go, up, sum_d + gsd, gb.reshape(-1), gg, gs,
        gxqkv, gxo, gxu, gxd, gxbias.reshape(-1), gxgains, gxshifts, gpos,
    )


def solution(mesh):
    rows, seg, copied = P("doc", "seg", None), P("seg", None), P()
    grads = (P(None, "seg", None), seg, seg, seg, P("seg"), P(None, "seg"), P(None, "seg"))
    return jax.shard_map(
        shards,
        mesh=mesh,
        in_specs=(rows, P("doc", "seg"), P("doc", None)) + (copied,) * 15 + (rows,),
        out_specs=(rows, rows) + grads + grads + (P(None, "seg"),),
        check_vma=False,
    )
```

```python
import functools

import jax
import jax.numpy as jnp
from jax import lax
from jax.experimental import pallas as pl
from jax.experimental.pallas import tpu as pltpu
from jax.sharding import PartitionSpec as P

f32, bf16 = jnp.float32, jnp.bfloat16
VMEM_BYTES = 60 * 2**20
EPS = 1e-6
PAIR = 128
HD = 64
CHUNK = 768
TILE = 384
NEG = -1e30
SMALL_ROWS = 16

S = jax.ShapeDtypeStruct
V = pltpu.VMEM
VM = pl.BlockSpec(memory_space=pltpu.VMEM)
SM = pl.BlockSpec(memory_space=pltpu.SMEM)
ANY = pl.BlockSpec(memory_space=pl.ANY)
PARAMS = pltpu.CompilerParams(vmem_limit_bytes=VMEM_BYTES)


def cost(micros):
    return pl.CostEstimate(flops=int(micros * 1e9), bytes_accessed=int(micros * 3e6), transcendentals=0)


def nn(a, b):
    return lax.dot_general(a, b, (((1,), (0,)), ((), ())), preferred_element_type=f32)


def nt(a, b):
    return lax.dot_general(a, b, (((1,), (1,)), ((), ())), preferred_element_type=f32)


def tn(a, b):
    return lax.dot_general(a, b, (((0,), (0,)), ((), ())), preferred_element_type=f32)


def gelu_both(u):
    phi = lax.erf(u * 0.70710678118654752) * 0.5 + 0.5
    return u * phi, phi + u * (jnp.exp(u * u * -0.5) * 0.39894228040143268)


def norm(r):
    c = r - jnp.mean(r, axis=-1, keepdims=True)
    inv = lax.rsqrt(jnp.mean(c * c, axis=-1, keepdims=True) + EPS)
    return c * inv, inv


def norm_back(g, n, inv, gain):
    t = g * gain
    return inv * (t - jnp.mean(t, axis=-1, keepdims=True) - n * jnp.mean(t * n, axis=-1, keepdims=True))


def row_sum(x):
    return jnp.sum(x, axis=0, keepdims=True)


def halves(x):
    low = lax.broadcasted_iota(jnp.int32, x.shape, 1) < HD
    zero = jnp.zeros_like(x)
    return jnp.where(low, x, zero), jnp.where(low, zero, x)


def two(x):
    return jnp.concatenate(halves(x), axis=0)


def softmax(t):
    t = jnp.exp(t - jnp.max(t, axis=-1, keepdims=True))
    return (t * (1.0 / jnp.sum(t, axis=-1, keepdims=True))).astype(bf16)


def start_all(sems, *pairs):
    copies = [pltpu.make_async_copy(a, b, sems.at[n]) for n, (a, b) in enumerate(pairs)]
    for c in copies:
        c.start()
    return copies


def bias_row(bias, j):
    k = CHUNK // 128
    rows = bias[...].astype(f32)
    return jnp.concatenate([rows[j * k + m:j * k + m + 1] for m in range(k)], axis=1)


def whole(a):
    return pl.BlockSpec(a.shape, lambda i, n=len(a.shape): (0,) * n)


def split_of(members, n, spread, D):
    per = n * D // members if spread else D // members
    return None if per % 16 or TILE % (2 * per) else (per, D // (2 * per) if spread else 0)


def grad_outs(members, n, spread, D, extra=0):
    split = split_of(members, n, spread, D)
    if not split:
        return [S((n, D, D), bf16)], [V((n, D, D), bf16), pltpu.SemaphoreType.DMA((n, 2))]
    per, step = split
    rows = per if spread else n * per
    return [S((members // 2, rows + extra, D), bf16)] * 2, [V((n, D // (2 * per), 2, per, D), bf16), pltpu.SemaphoreType.DMA((n, 2))]


def placed_at(m, bits, core):
    if bits < 2:
        return m
    low, next_, high = m & 1, (m >> 1) & 1, m >> 2
    first = (low << (bits - 1)) | (high << 1) | next_
    second = (next_ << (bits - 1)) | (high << 1) | low
    return jnp.where(core == 0, first, second)


def emit_grads(split, core, left, right, outs, stage, sems):
    n, D = stage.shape[0], stage.shape[-1]
    bits = outs[0].shape[0].bit_length() - 1

    def copies(j):
        if not split:
            return [pltpu.make_async_copy(stage.at[j], outs[0].at[j], sems.at[j, 0])]
        per, step = split
        res = []
        for k in range(stage.shape[1]):
            m = j * step + k if step else k
            theirs, ours = placed_at(m, bits, 1 - core), placed_at(m, bits, core)
            rows = pl.ds(0, per) if step else pl.ds(j * per, per)
            res += [pltpu.make_async_copy(stage.at[j, k, 1 - core], outs[0].at[theirs, rows], sems.at[j, 0]),
                    pltpu.make_async_copy(stage.at[j, k, core], outs[1].at[ours, rows], sems.at[j, 1])]
        return res

    for j in range(n):
        for t in range(D // TILE):
            res = tn(left(j, slice(t * TILE, (t + 1) * TILE)), right(j)).astype(bf16)
            if split:
                k = TILE // (2 * split[0])
                stage[j, t * k:(t + 1) * k] = res.reshape((k, 2, split[0], D))
            else:
                stage[j, t * TILE:(t + 1) * TILE, :] = res
        for x in copies(j):
            x.start()

    def end():
        for j in range(n):
            for x in copies(j):
                x.wait()

    return end


def forward_kernel(n_docs, split, n_grads, meta, lengths, tok, cot, mask, wqkv_h, wo_h, wu_h, wd_h, bias, gains, shifts, *rest):
    (q_o, k_o, v_o, p_o, ob_o, n_o, inv_o, dg_o, gr2_o, mixed_o, pack_o, small_o), rest = rest[:12], rest[12:]
    grads, (wqkv, wo, wu, wd, y1b, gb_s, gm_s, sems, stage, gsems) = rest[:n_grads], rest[n_grads:]
    i = pl.program_id(0)
    segs, pairs = p_o.shape[0], p_o.shape[1]
    B, D = tok.shape
    L = B // segs
    n = wu.shape[0]
    ga, sh = gains[...].astype(f32), shifts[...].astype(f32)
    cs = [slice(c * CHUNK, (c + 1) * CHUNK) for c in range(n)]
    load = lambda a, b, m: pltpu.make_async_copy(a, b, sems.at[m])
    first = [load(wqkv_h, wqkv, 0), load(wo_h, wo, 1)]
    ups = [load(wu_h.at[:, c], wu.at[j], 2 + j) for j, c in enumerate(cs)]
    downs = [load(wd_h.at[c, :], wd.at[j], 2 + n + j) for j, c in enumerate(cs)]

    @pl.when(i == 0)
    def _():
        for c in first + ups + downs:
            c.start()
        small_o[...] = jnp.zeros_like(small_o)
        first[0].wait()

    hb = tok[...]
    q_o[...] = ((nn(hb, wqkv[0]) + sh[0:1]) * 0.125).astype(bf16)
    k_o[...] = nn(hb, wqkv[1]).astype(bf16)
    v_o[...] = (nn(hb, wqkv[2]) + sh[1:2]).astype(bf16)
    col = [slice(j * PAIR, (j + 1) * PAIR) for j in range(pairs)]
    for s in range(segs):
        rows = slice(s * L, (s + 1) * L)
        live = jnp.where(mask[pl.ds(i * segs + s, 1), :] > 0, 0.0, NEG).astype(f32)
        scores = [nt(q_o[rows, c], two(k_o[rows, c])) for c in col]
        probs = [jnp.concatenate([softmax(t[:, e:e + L] + live) for e in (0, L)], axis=1) for t in scores]
        for j, c in enumerate(col):
            p_o[s, j] = probs[j]
            ob_o[rows, c] = nn(probs[j], two(v_o[rows, c])).astype(bf16)

    @pl.when(i == 0)
    def _():
        for c in first[1:] + ups + downs:
            c.wait()

    n1, inv1 = norm(hb.astype(f32) + nn(ob_o[...], wo[...]) + sh[2:3])
    n_o[...] = n1
    inv_o[...] = inv1
    y1 = n1 * ga[0:1] + sh[3:4]
    y1b[...] = y1.astype(bf16)
    up = lambda j: nn(y1b[...], wu[j]) + bias_row(bias, j)
    here = pl.ds(pl.multiple_of(i * B, B), B)
    u, acc = up(0), y1 + sh[4:5]
    for j in range(n):
        after = up(j + 1) if j + 1 < n else None
        g, d = gelu_both(u)
        gb = g.astype(bf16)
        gb_s[j, here, :] = gb
        dg_o[j] = d.astype(bf16)
        acc = acc + nn(gb, wd[j])
        u = after
    n2, inv2 = norm(acc)
    mixed_o[...] = (n2 * ga[1:2] + sh[5:6]).astype(bf16)
    row = lax.broadcasted_iota(jnp.int32, n2.shape, 0)
    gz = jnp.where(row % L == 0, 0.0, cot[...].astype(f32))
    small_o[0:1, :] += row_sum(gz * n2)
    small_o[1:2, :] += row_sum(gz)
    gr2 = norm_back(gz, n2, inv2, ga[1:2])
    gr2_o[...] = gr2
    gm = gr2.astype(bf16)
    gm_s[here, :] = gm
    small_o[2:3, :] += row_sum(gm.astype(f32))

    lane = lax.broadcasted_iota(jnp.int32, (1, 128), 1)
    for s in range(segs):
        g = (i * segs + s) * meta[2] + meta[0]
        before, doc, pos = jnp.int32(0), meta[1] * 32, g
        for d in range(n_docs):
            before = before + lengths[0, d]
            passed = g >= before
            doc = doc + passed.astype(jnp.int32)
            pos = jnp.where(passed, g - before, pos)
        extra = jnp.where(lane == 0, doc, jnp.where(lane == 1, pos, 0)).astype(f32)
        top = slice(s * L, s * L + 1)
        high = inv1[top].astype(bf16).astype(f32)
        extra = jnp.where(lane == 2, high, jnp.where(lane == 3, inv1[top] - high, extra))
        pack_o[s, :, :D] = n1[top].astype(bf16)
        pack_o[s, :, D:2 * D] = cot[s * L:s * L + 16, :][0:1]
        pack_o[s, :, 2 * D:] = extra.astype(bf16)

    @pl.when(i == pl.num_programs(0) - 1)
    def _():
        emit_grads(split, meta[3], lambda j, c: gb_s[j, :, c], lambda j: gm_s[...], grads, stage, gsems)()


def forward(meta, lengths, tok, cot, mask, wqkv, wo, wu, wd, bias, gains, shifts, members, step=3):
    T, D = tok.shape
    segs_dev, L = mask.shape
    pairs, B, n = D // PAIR, L * step, wu.shape[1] // CHUNK
    rowblk = pl.BlockSpec((B, D), lambda i: (i, 0))
    wide = pl.BlockSpec((n, B, CHUNK), lambda i: (0, i, 0))
    row = lambda dt: (S((T, D), dt), rowblk)
    outs = [row(bf16), row(bf16), row(bf16),
            (S((segs_dev, pairs, L, 2 * L), bf16), pl.BlockSpec((step, pairs, L, 2 * L), lambda i: (i, 0, 0, 0))),
            row(bf16), row(f32), (S((T, 1), f32), pl.BlockSpec((B, 1), lambda i: (i, 0))), (S((n, T, CHUNK), bf16), wide),
            row(f32), row(bf16),
            (S((segs_dev, 1, 2 * D + 128), bf16), pl.BlockSpec((step, 1, 2 * D + 128), lambda i: (i, 0, 0))),
            (S((8, D), f32), whole(S((8, D), f32)))]
    grads, scratch = grad_outs(members, n, True, D)
    return pl.pallas_call(
        functools.partial(forward_kernel, lengths.shape[1], split_of(members, n, True, D), len(grads)),
        grid=(segs_dev // step,),
        in_specs=[SM, SM, rowblk, rowblk, whole(mask), ANY, ANY, ANY, ANY, whole(bias), whole(gains), whole(shifts)],
        out_specs=[o[1] for o in outs] + [ANY] * len(grads),
        out_shape=[o[0] for o in outs] + grads,
        scratch_shapes=[V(wqkv.shape, bf16), V(wo.shape, bf16), V((n, D, CHUNK), bf16), V((n, CHUNK, D), bf16), V((B, D), bf16), V((n, T, CHUNK), bf16),
                        V((T, D), bf16), pltpu.SemaphoreType.DMA((2 + 2 * n,))] + scratch,
        compiler_params=PARAMS,
        name="seg_forward", cost_estimate=cost(30),
    )(meta, lengths, tok, cot, mask, wqkv, wo, wu, wd, bias, gains, shifts)


def ffn_back_kernel(split, n_grads, meta, n1, inv1, dg, gr2, wu_h, wd_h, gains, shifts, gr1_o, gbias_o, small_o, *rest):
    grads, (wu, wd, gm, y1b_s, gu_s, sems, stage, gsems) = rest[:n_grads], rest[n_grads:]
    i = pl.program_id(0)
    n = wu.shape[0]
    B = n1.shape[0]
    cs = [slice(c * CHUNK, (c + 1) * CHUNK) for c in range(n)]
    ups = [pltpu.make_async_copy(wu_h.at[:, c], wu.at[j], sems.at[0, j]) for j, c in enumerate(cs)]
    downs = [pltpu.make_async_copy(wd_h.at[c, :], wd.at[j], sems.at[1, j]) for j, c in enumerate(cs)]
    order = [c for pair in zip(downs, ups) for c in pair]

    @pl.when(i == 0)
    def _():
        for c in order[:3]:
            c.start()
        small_o[...] = jnp.zeros_like(small_o)
        gbias_o[...] = jnp.zeros_like(gbias_o)

    def await_first(m, count):
        @pl.when(i == 0)
        def _():
            for k in range(m, min(m + count, 2 * n)):
                order[k].wait()
                if k + 3 < 2 * n:
                    order[k + 3].start()

    here = pl.ds(pl.multiple_of(i * B, B), B)
    n1v, gfirst = n1[...], gains[...].astype(f32)[0:1]
    y1b_s[here, :] = (n1v * gfirst + shifts[...].astype(f32)[3:4]).astype(bf16)
    acc = gr2[...]
    gm[...] = acc.astype(bf16)
    await_first(0, 1)
    t = nt(gm[...], wd[0])
    for j in range(n):
        await_first(2 * j + 1, 2)
        after = nt(gm[...], wd[j + 1]) if j + 1 < n else None
        gu = (t * dg[j].astype(f32)).astype(bf16)
        gu_s[j, here, :] = gu
        gbias_o[j:j + 1, :] += row_sum(gu.astype(f32))
        acc = acc + nt(gu, wu[j])
        t = after
    small_o[0:1, :] += row_sum(acc * n1v)
    small_o[1:2, :] += row_sum(acc)
    gr1_o[...] = norm_back(acc, n1v, inv1[...], gfirst)

    @pl.when(i == pl.num_programs(0) - 1)
    def _():
        emit_grads(split, meta[3], lambda j, c: y1b_s[:, c], lambda j: gu_s[j], grads, stage, gsems)()


def ffn_back(meta, n1, inv1, dg, gr2, wu, wd, gains, shifts, members, B=768):
    T, D = n1.shape
    n = wu.shape[1] // CHUNK
    rowblk = pl.BlockSpec((B, D), lambda i: (i, 0))
    grads, scratch = grad_outs(members, n, False, D)
    shapes = [S((T, D), f32), S((8, CHUNK), f32), S((8, D), f32)]
    return pl.pallas_call(
        functools.partial(ffn_back_kernel, split_of(members, n, False, D), len(grads)),
        grid=(T // B,),
        in_specs=[SM, rowblk, pl.BlockSpec((B, 1), lambda i: (i, 0)), pl.BlockSpec((n, B, CHUNK), lambda i: (0, i, 0)), rowblk,
                  ANY, ANY, whole(gains), whole(shifts)],
        out_specs=[rowblk, whole(shapes[1]), whole(shapes[2])] + [ANY] * len(grads),
        out_shape=shapes + grads,
        scratch_shapes=[V((n, D, CHUNK), bf16), V((n, CHUNK, D), bf16), V((B, D), bf16), V((T, D), bf16), V((n, T, CHUNK), bf16),
                        pltpu.SemaphoreType.DMA((2, n))] + scratch,
        compiler_params=PARAMS,
        name="seg_ffn_back", cost_estimate=cost(20),
    )(meta, n1, inv1, dg, gr2, wu, wd, gains, shifts)


def with_cls(rows, cls):
    row = lax.broadcasted_iota(jnp.int32, (rows.shape[0], 1), 0)
    for s in range(cls.shape[0]):
        rows = jnp.where(row == s * (rows.shape[0] // cls.shape[0]), cls[s], rows)
    return rows


def input_grad_kernel(gr1, gr1c, qk0, qk1, vv, wqkv, o):
    H = qk0.shape[1] // 2
    part = lambda a: jnp.concatenate([qk0[:, a:a + H], qk1[:, a:a + H]], axis=1)
    o[...] = (with_cls(gr1[...], gr1c) + nt(part(0), wqkv[0]) + nt(part(H), wqkv[1]) + nt(vv[...], wqkv[2])).astype(bf16)


def input_grad(gr1, gr1c, qk0, qk1, vv, wqkv, step=2):
    T, D = gr1.shape
    segs = gr1c.shape[0]
    rowblk = pl.BlockSpec((T // segs * step, D), lambda i: (i, 0))
    return pl.pallas_call(
        input_grad_kernel,
        grid=(segs // step,),
        in_specs=[rowblk, pl.BlockSpec((step, 1, D), lambda i: (i, 0, 0)), rowblk, rowblk, rowblk, whole(wqkv)],
        out_specs=rowblk,
        out_shape=S((T, D), bf16),
        compiler_params=PARAMS,
        name="input_grad", cost_estimate=cost(6),
    )(gr1, gr1c, qk0, qk1, vv, wqkv)


def attn_back_kernel(split, n_grads, is_last, meta, *rest):
    if is_last:
        (first_v, small_f, small_b, sums_a, gbias, ga_in), rest = rest[:6], rest[6:]
    else:
        (gr1, gr1c, ob), rest = rest[:3], rest[3:]
    (p, q, k, v, tok, wo), rest = rest[:6], rest[6:]
    if is_last:
        (qk_o, vv_o, vec_o), rest = rest[:3], rest[3:]
    else:
        (qk_o, ga_o, first_v_o, sums_o), rest = rest[:4], rest[4:]
    grads, rest = rest[:n_grads], rest[n_grads:]
    go_s, g_s, left_s, sums, rest = *rest[:4], rest[4:]
    if is_last:
        vec_s, wsems, rest = *rest[:2], rest[2:]
    stage, gsems = rest
    i = pl.program_id(0)
    segs, pairs = p.shape[0], p.shape[1]
    B, D = tok.shape
    L, H = B // segs, pairs * PAIR
    here = pl.ds(pl.multiple_of(i * B, B), B)

    @pl.when(i == 0)
    def _():
        sums[...] = jnp.zeros_like(sums)

    left_s[0, here, :] = tok[...]
    if is_last:
        ga = ga_in[...]
    else:
        ga = with_cls(gr1[...], gr1c).astype(bf16)
        ga_o[...] = ga
        g_s[1, here, :] = ga
        left_s[1, here, :] = ob[...]
    go_s[...] = nt(ga, wo[...]).astype(bf16)
    col = [slice(j * PAIR, (j + 1) * PAIR) for j in range(pairs)]
    beside = lambda c: slice(H + c.start, H + c.stop)
    eighth = jnp.asarray(0.125, bf16)
    for s in range(segs):
        rows = slice(s * L, (s + 1) * L)
        out = pl.ds(pl.multiple_of(i * B, B) + s * L, L)
        gps = [nt(go_s[rows, c], two(v[rows, c])) for c in col]
        for j, c in enumerate(col):
            pb = p[s, j]
            gv = tn(jnp.concatenate([pb[:, :L], pb[:, L:]], axis=0), two(go_s[rows, c])).astype(bf16)
            if is_last:
                g_s[1, out, beside(c)] = gv
            else:
                first_v_o[rows, c] = gv
        gss = []
        for j, gp in enumerate(gps):
            pf = p[s, j].astype(f32)
            gs = []
            for e in (0, L):
                pe, ge = pf[:, e:e + L], gp[:, e:e + L]
                gs.append((pe * (ge - jnp.sum(pe * ge, axis=-1, keepdims=True))).astype(bf16))
            gss.append(gs)
        for c, gs in zip(col, gss):
            g_s[0, out, c] = nn(jnp.concatenate(gs, axis=1), two(k[rows, c])).astype(bf16) * eighth
            g_s[0, out, beside(c)] = tn(jnp.concatenate(gs, axis=0), two(q[rows, c])).astype(bf16)
    if is_last:
        g_s[1, here, :H] = first_v[...]
        vv_o[...] = g_s[1, here, :]
    qk_o[...] = g_s[0, here, :]
    for m in range(2):
        sums[m:m + 1, :] += row_sum(g_s[m, here, :].astype(f32))

    @pl.when(i == pl.num_programs(0) - 1)
    def _():
        tail = []
        if is_last:
            vec = jnp.concatenate([
                gbias[0:4, :], small_b[0:1, :], small_f[0:1, :], jnp.concatenate([sums_a[0:1, :H], sums[0:1, :H]], axis=1), sums[1:2, :],
                sums_a[1:2, :], small_b[1:2, :], small_f[2:3, :], small_f[1:2, :], jnp.zeros((4, D), f32)], axis=0)
            vec_o[...] = vec
            if split:
                for m in range(vec_s.shape[0]):
                    vec_s[m] = vec.astype(bf16)
                tail = [pltpu.make_async_copy(vec_s, h.at[:, pl.ds(h.shape[1] - SMALL_ROWS, SMALL_ROWS)], wsems.at[m]) for m, h in enumerate(grads)]
        else:
            sums_o[...] = sums[...]
        for x in tail:
            x.start()
        emit_grads(split, meta[3], lambda j, c: left_s[0 if is_last else j, :, c], lambda j: g_s[j], grads, stage, gsems)()
        for x in tail:
            x.wait()


def attn_back(meta, before_it, p, q, k, v, tok, wo, members, is_last, step=2):
    T, D = tok.shape
    segs_dev, all_pairs, L = p.shape[:3]
    pairs, H, half = all_pairs // 2, D // 2, int(is_last)
    B = L * step
    rowblk = pl.BlockSpec((B, D), lambda i: (i, 0))
    halfblk = pl.BlockSpec((B, H), lambda i: (i, half))
    firstblk = pl.BlockSpec((B, H), lambda i: (i, 0))
    split = split_of(members, 2, False, D)
    grads, scratch = grad_outs(members, 2, False, D, SMALL_ROWS if is_last else 0)
    small = S((8, D), f32)
    if is_last:
        vec = S((SMALL_ROWS, D), f32)
        specs = [firstblk] + [whole(x) for x in before_it[1:5]] + [rowblk]
        outs = [(S((T, D), bf16), rowblk), (S((T, D), bf16), rowblk), (vec, whole(vec))]
        more = [V((members // 2, SMALL_ROWS, D), bf16), pltpu.SemaphoreType.DMA((2,))]
    else:
        specs = [rowblk, pl.BlockSpec((step, 1, D), lambda i: (i, 0, 0)), rowblk]
        outs = [(S((T, D), bf16), rowblk), (S((T, D), bf16), rowblk), (S((T, H), bf16), firstblk), (small, whole(small))]
        more = []
    return pl.pallas_call(
        functools.partial(attn_back_kernel, split, len(grads), is_last),
        grid=(segs_dev // step,),
        in_specs=[SM] + specs + [pl.BlockSpec((step, pairs, L, 2 * L), lambda i: (i, half, 0, 0)), halfblk, halfblk, halfblk, rowblk,
                                 pl.BlockSpec((H, D), lambda i: (half, 0))],
        out_specs=[o[1] for o in outs] + [ANY] * len(grads),
        out_shape=[o[0] for o in outs] + grads,
        scratch_shapes=[V((B, H), bf16), V((2, T, D), bf16), V((2, T, D), bf16), V((8, D), f32)] + more + scratch,
        compiler_params=PARAMS,
        name="seg_attention_back", cost_estimate=cost(12),
    )(meta, *before_it, p, q, k, v, tok, wo)


def onehot(rows, width, start):
    at = lax.broadcasted_iota(jnp.int32, (rows, width), 0) + start
    return (at == lax.broadcasted_iota(jnp.int32, (rows, width), 1)).astype(bf16)


def nt_exact(x, pick):
    a = x.astype(bf16)
    rest = x - a.astype(f32)
    b = rest.astype(bf16)
    return nt(a, pick) + nt(b, pick) + nt((rest - b.astype(f32)).astype(bf16), pick)


def own_vectors(vec, member, r, F):
    D = vec.shape[1]
    wide = F // D
    per = r * wide
    fits = D // per
    parts = nt_exact(vec, onehot(per, D, lax.rem(member, fits) * per))
    line = lax.broadcasted_iota(jnp.int32, parts.shape, 0)
    bias = row_sum(jnp.where(line == lax.div(member, fits), parts, 0.0))
    rest = nt_exact(vec, onehot(r, D, member * r))
    return bias, rest[wide:wide + 2], rest[wide + 2:wide + 8]


def cross_kernel(r, meta, rows_in, mixed_h, swu_h, swd_h, xqkv_h, xo_h, xu_h, xd_h, sbias, sgains, sshifts, xbias, xgains, xshifts, pos,
                 mixed_o, gr1_o, svec_o, gqkv_o, go_o, gu_o, gd_o, gbias_o, ggains_o, gshifts_o, gpos_o, sgu_o, sgd_o,
                 swu, swd, xqkv, xo, xu, xd, sgb, sdg, xgb, xdg, sgu, xgu, q_s, k_s, v_s, p_s, o_s, go_s, gq_s, gk_s, gv_s, hb_s, z1_s, y1_s,
                 cls_s, gr1_s, vec_s, svec_s, patch, sems, psems):
    n, D = swu.shape[0], swu.shape[1]
    R = rows_in.shape[0]
    cs = [slice(c * CHUNK, (c + 1) * CHUNK) for c in range(n)]
    col = [slice(c, c + PAIR) for c in range(0, D, PAIR)]
    queue = []
    for wu_h, wd_h, wu, wd in ((swu_h, swd_h, swu, swd), (xu_h, xd_h, xu, xd)):
        for j, c in enumerate(cs):
            queue += [(wu_h.at[:, c], wu.at[j]), (wd_h.at[c, :], wd.at[j])]
    queue[2 * n:2 * n] = [(xqkv_h.at[m], xqkv.at[m]) for m in range(3)] + [(xo_h, xo)]
    copies = [pltpu.make_async_copy(a, b, sems.at[m]) for m, (a, b) in enumerate(queue)]
    ahead, waited = 4, [0]
    for x in copies[:ahead]:
        x.start()

    def need(count):
        for _ in range(count):
            m = waited[0]
            copies[m].wait()
            if m + ahead < len(copies):
                copies[m + ahead].start()
            waited[0] = m + 1

    segs, L = patch.shape[0], mixed_h.shape[0] // patch.shape[0]
    fetch = [pltpu.make_async_copy(mixed_h.at[pl.ds(s * L, 16), :], patch.at[s], psems.at[s]) for s in range(segs)]
    for x in fetch:
        x.start()
    sg, ss = sgains[...].astype(f32), sshifts[...].astype(f32)
    xg, xs = xgains[...].astype(f32), xshifts[...].astype(f32)
    eighth = jnp.asarray(0.125, bf16)

    def ffn_f(acc, yb, wu, wd, bias, gb_s, dg_s):
        def up(j):
            need(1)
            return nn(yb, wu[j]) + bias_row(bias, j)

        for j in range(n):
            g, d = gelu_both(up(j))
            gb = g.astype(bf16)
            gb_s[:, cs[j]] = gb
            dg_s[:, cs[j]] = d.astype(bf16)
            need(1)
            acc = acc + nn(gb, wd[j])
        return acc

    def ffn_b(acc, gm, wu, wd, dg_s, gu_s, vec):
        t = nt(gm, wd[0])
        for j in range(n):
            after = nt(gm, wd[j + 1]) if j + 1 < n else None
            gu = (t * dg_s[:, cs[j]].astype(f32)).astype(bf16)
            gu_s[:, cs[j]] = gu
            vec[j:j + 1, :] = row_sum(gu.astype(f32))
            acc = acc + nt(gu, wu[j])
            t = after
        return acc

    vec_s[...] = jnp.zeros_like(vec_s)
    svec_s[...] = jnp.zeros_like(svec_s)
    n1 = rows_in[:, :D].astype(f32)
    extra = rows_in[:, 2 * D:].astype(f32)
    spos = extra[:, 1:2].astype(jnp.int32)
    inv1 = extra[:, 2:3] + extra[:, 3:4]
    lane = lax.broadcasted_iota(jnp.int32, (8, extra.shape[1]), 1)
    did_row = nt((lane == 0).astype(bf16), extra.astype(bf16))[0:1]
    allowed = extra[:, 0:1] == did_row
    placed = (lax.broadcasted_iota(jnp.int32, (R, pos.shape[0]), 1) == spos).astype(bf16)

    y1 = n1 * sg[0:1] + ss[3:4]
    y1b = y1.astype(bf16)
    n2, inv2 = norm(ffn_f(y1 + ss[4:5], y1b, swu, swd, sbias, sgb, sdg))
    h = n2 * sg[1:2] + ss[5:6] + nn(placed, pos[...])

    hb = h.astype(bf16)
    need(1)
    q_s[...] = ((nn(hb, xqkv[0]) + xs[0:1]) * 0.125).astype(bf16)
    need(1)
    k_s[...] = nn(hb, xqkv[1]).astype(bf16)
    need(1)
    v_s[...] = (nn(hb, xqkv[2]) + xs[1:2]).astype(bf16)
    early = R <= 256
    pair_scores = lambda c: [nt(x, k_s[:, c]) for x in halves(q_s[:, c])]
    scores = [pair_scores(c) for c in col] if early else None
    for j, c in enumerate(col):
        out, v2 = 0.0, halves(v_s[:, c])
        sc = scores[j] if early else pair_scores(c)
        for e in range(2):
            pb = softmax(jnp.where(allowed, sc[e], NEG))
            p_s[2 * j + e] = pb
            out = out + nn(pb, v2[e])
        o_s[:, c] = out.astype(bf16)
    need(1)
    m1, minv1 = norm(h + nn(o_s[...], xo[...]) + xs[2:3])
    z1 = m1 * xg[0:1] + xs[3:4]
    z1b = z1.astype(bf16)
    m2, minv2 = norm(ffn_f(z1 + xs[4:5], z1b, xu, xd, xbias, xgb, xdg))
    cls_s[...] = m2 * xg[1:2] + xs[5:6]

    gz = rows_in[:, D:2 * D].astype(f32)
    vec_s[n + 1:n + 2, :] = row_sum(gz * m2)
    vec_s[n + 7:n + 8, :] = row_sum(gz)
    gr2 = norm_back(gz, m2, minv2, xg[1:2])
    xgm = gr2.astype(bf16)
    vec_s[n + 6:n + 7, :] = row_sum(xgm.astype(f32))
    gy1 = ffn_b(gr2, xgm, xu, xd, xdg, xgu, vec_s)
    vec_s[n:n + 1, :] = row_sum(gy1 * m1)
    vec_s[n + 5:n + 6, :] = row_sum(gy1)
    gr1 = norm_back(gy1, m1, minv1, xg[0:1])
    xga = gr1.astype(bf16)
    vec_s[n + 4:n + 5, :] = row_sum(xga.astype(f32))
    go_s[...] = nt(xga, xo[...]).astype(bf16)
    pair_gps = lambda c: [nt(x, v_s[:, c]) for x in halves(go_s[:, c])]
    gps = [pair_gps(c) for c in col] if early else None
    for j, c in enumerate(col):
        gpj = gps[j] if early else pair_gps(c)
        q2, k2, g2 = halves(q_s[:, c]), halves(k_s[:, c]), halves(go_s[:, c])
        gq = gk = gv = 0.0
        for e in range(2):
            pb = p_s[2 * j + e]
            pf = pb.astype(f32)
            gp = gpj[e]
            gs = (pf * (gp - jnp.sum(pf * gp, axis=-1, keepdims=True))).astype(bf16)
            gq = gq + nn(gs, k2[e])
            gk = gk + tn(gs, q2[e])
            gv = gv + tn(pb, g2[e])
        gq_s[:, c] = gq.astype(bf16) * eighth
        gk_s[:, c] = gk.astype(bf16)
        gv_s[:, c] = gv.astype(bf16)
    vec_s[n + 2:n + 3, :] = row_sum(gq_s[...].astype(f32))
    vec_s[n + 3:n + 4, :] = row_sum(gv_s[...].astype(f32))
    gcls = gr1 + nt(gq_s[...], xqkv[0]) + nt(gk_s[...], xqkv[1]) + nt(gv_s[...], xqkv[2])

    svec_s[n + 1:n + 2, :] = row_sum(gcls * n2)
    svec_s[n + 7:n + 8, :] = row_sum(gcls)
    gr2 = norm_back(gcls, n2, inv2, sg[1:2])
    sgm = gr2.astype(bf16)
    svec_s[n + 6:n + 7, :] = row_sum(sgm.astype(f32))
    gy1 = ffn_b(gr2, sgm, swu, swd, sdg, sgu, svec_s)
    svec_s[n:n + 1, :] = row_sum(gy1 * n1)
    svec_s[n + 5:n + 6, :] = row_sum(gy1)
    gr1_s[...] = norm_back(gy1, n1, inv1, sg[0:1])
    svec_o[...] = svec_s[...]

    for x in fetch:
        x.wait()
    top = lax.broadcasted_iota(jnp.int32, (16, 1), 0) == 0
    for s in range(segs):
        line = pl.ds(meta[4] + s, 1)
        gr1_o[s] = gr1_s[line, :]
        patch[s] = jnp.where(top, cls_s[line, :], patch[s].astype(f32)).astype(bf16)
    store = [pltpu.make_async_copy(patch.at[s], mixed_o.at[pl.ds(s * L, 16), :], psems.at[s]) for s in range(segs)]
    for x in store:
        x.start()

    member = meta[0]
    pick = onehot(r, D, member * r)
    window = 256

    def own(x, count):
        width = x.shape[1]
        at_col = jnp.minimum(lax.div(member * count, 128) * 128, width - window)
        near = x[:, pl.ds(pl.multiple_of(at_col, 128), window)]
        return nt(onehot(count, window, member * count - at_col), near).astype(bf16)

    hb_s[...] = hb
    z1_s[...] = z1b
    y1_s[...] = y1b
    hbt = own(hb_s, r)
    for m, g in enumerate((gq_s, gk_s, gv_s)):
        gqkv_o[m] = nn(hbt, g[...])
    go_o[...] = nn(own(o_s, r), xga)
    gd_o[...] = nn(own(xgb, r * n), xgm)
    sgd_o[...] = nn(own(sgb, r * n), sgm)
    z1t, y1t = own(z1_s, r), own(y1_s, r)
    for c in cs:
        gu_o[:, c] = nn(z1t, xgu[:, c])
        sgu_o[:, c] = nn(y1t, sgu[:, c])
    bias, gains, shifts = own_vectors(vec_s[...], member, r, n * D)
    gbias_o[...] = bias
    ggains_o[...] = gains
    gshifts_o[...] = shifts
    gown = nt_exact(gcls, pick)
    high = gown.astype(bf16)
    gpos_o[...] = tn(placed, high) + tn(placed, (gown - high.astype(f32)).astype(bf16))
    for x in store:
        x.wait()


def cross(meta, rows_in, mixed, seg_params, cross_params, pos, segs, r):
    swu, swd, sbias, sgains, sshifts = seg_params
    xqkv, xo, xu, xd, xbias, xgains, xshifts = cross_params
    R = rows_in.shape[0]
    D, F = swu.shape
    n = F // CHUNK
    outs = [S(mixed.shape, bf16), S((segs, 1, D), f32), S((SMALL_ROWS, D), f32), S((3, r, D), f32), S((r, D), f32), S((r, F), f32),
            S((r * n, D), f32), S((1, r * n), f32), S((2, r), f32), S((6, r), f32), S((pos.shape[0], r), f32), S((r, F), f32), S((r * n, D), f32)]
    up, down, row = V((n, D, CHUNK), bf16), V((n, CHUNK, D), bf16), V((R, D), bf16)
    return pl.pallas_call(
        functools.partial(cross_kernel, r),
        in_specs=[SM, VM] + [ANY] * 7 + [VM] * 7,
        out_specs=[ANY] + [VM] * (len(outs) - 1),
        out_shape=outs,
        scratch_shapes=[up, down, V(xqkv.shape, bf16), V(xo.shape, bf16), up, down] + [V((R, F), bf16)] * 6 + [row] * 3
        + [V((D // HD, R, R), bf16)] + [row] * 8 + [V((R, D), f32)] * 2 + [V((SMALL_ROWS, D), f32)] * 2
        + [V((segs, 16, D), bf16), pltpu.SemaphoreType.DMA((4 * n + 4,)), pltpu.SemaphoreType.DMA((segs,))],
        input_output_aliases={2: 0},
        compiler_params=PARAMS,
        name="cross_block", cost_estimate=cost(28),
    )(meta, rows_in, mixed, swu, swd, xqkv, xo, xu, xd, sbias, sgains, sshifts, xbias, xgains, xshifts, pos)


def finish_kernel(r, F, routed, meta, *rest):
    ins, (w_o, o_o, bias_o, gains_o, shifts_o) = rest[:-5], rest[-5:]
    if routed:
        lower = meta[1] == 0
        totals = []
        for x, other in (ins[0:2], ins[2:4]):
            a, b = x[...].astype(f32), other[...].astype(f32)
            totals.append(jnp.concatenate([jnp.where(lower, a, b), jnp.where(lower, b, a)], axis=0))
    else:
        totals = [ins[0][...], ins[1][...]]
    a, b = totals
    H = a.shape[1] // 2
    for m in range(2):
        w_o[m] = jnp.concatenate([a[:r, m * H:(m + 1) * H], b[:r, m * H:(m + 1) * H]], axis=1)
    w_o[2] = b[r:2 * r]
    o_o[...] = a[r:2 * r]
    bias, gains, shifts = own_vectors(b[2 * r:] + ins[-1][...], meta[0], r, F)
    bias_o[...] = bias
    gains_o[...] = gains
    shifts_o[...] = shifts


def finish(meta, parts, vec_c, r, F, routed):
    D = vec_c.shape[1]
    outs = [S((3, r, D), f32), S((r, D), f32), S((1, r * (F // D)), f32), S((2, r), f32), S((6, r), f32)]
    return pl.pallas_call(
        functools.partial(finish_kernel, r, F, routed), in_specs=[SM] + [VM] * (len(parts) + 1), out_specs=[VM] * len(outs), out_shape=outs,
        compiler_params=PARAMS, name="finish", cost_estimate=cost(2),
    )(meta, *parts, vec_c)


def add_up(a, b):
    return (a.astype(f32) + b.astype(f32)).astype(bf16)


def at(x, i, axis):
    return lax.dynamic_index_in_dim(x, i, axis, keepdims=False)


def fold(pieces, members, member):
    bits = members.bit_length() - 1
    x = pieces.reshape((2,) * bits + pieces.shape[1:])
    for bit in range(bits):
        axis = bits - 1 - bit
        mine = (member >> bit) & 1
        got = lax.ppermute(at(x, 1 - mine, axis), "seg", [(m, m ^ (1 << bit)) for m in range(members)])
        x = add_up(at(x, mine, axis), got)
    return x


def over_docs(x):
    docs = lax.axis_size("doc")
    total, part = x.astype(f32), x
    for _ in range(docs - 1):
        part = lax.ppermute(part, "doc", [(d, (d + 1) % docs) for d in range(docs)])
        total = total + part.astype(f32)
    return total


class Routed:
    def __init__(self, send, keep):
        self.members, member = lax.axis_size("seg"), lax.axis_index("seg")
        self.core, self.number = member & 1, lax.axis_index("doc") * self.members + member
        self.step, self.out = 0, [send]
        self.shape = (2, 2, 2, 2, send.shape[1] // 2, send.shape[2])
        self.terms, self.fresh = [(keep, ())], 0

    def bit(self, first, second):
        return jnp.where(self.core == 0, (self.number & first) != 0, (self.number & second) != 0).astype(jnp.int32)

    def sum(self, *choices):
        total = 0.0
        for x, path in self.terms:
            for axis, i in path + choices:
                x = at(x, i, axis)
            total = total + x.astype(f32)
        return total.astype(bf16)

    def ready(self):
        X, Z0, Z1, Y = 2, 4, 8, self.members
        if self.step == 1:
            self.terms = [(x.reshape(self.shape), path) for x, path in self.terms]
            b = self.bit(X, Z0)
            self.masks, self.out, self.choice = [(X, Z0)], [self.sum((0, 1 - b))], ((0, b),)
        elif self.step == 2:
            b, y = self.bit(Z0, X), self.bit(Y, Y)
            self.masks = [(Z0, X), (Y, Y), (Z0 + Y, X + Y)]
            self.out = [self.sum((1, i), (1, h)) for i, h in ((1 - b, y), (b, 1 - y), (1 - b, 1 - y))]
            self.choice = ((1, b), (1, y))
        elif self.step == 3:
            b = self.bit(Z1, Z1)
            self.terms, self.fresh = [(lax.optimization_barrier(self.sum()), ())], 0
            self.masks, self.out, self.choice = [(Z1, Z1)], [self.sum((0, 1 - b))], ((0, b),)
        else:
            self.masks, self.out = [(Y, Y)], [self.sum()]
        return self

    def go(self):
        masks = self.masks if self.step else [(1, 1)]
        got = [lax.ppermute(x, ("doc", "seg"), [(m, m ^ by[m & 1]) for m in range(2 * self.members)]) for x, by in zip(self.out, masks)]
        if self.step == 4:
            self.x = (self.out[0], got[0])
        elif self.step:
            self.terms = [(x, path + self.choice) for x, path in self.terms] + [(x, ()) for x in got]
        else:
            self.terms.append((got[0], ()))
        self.fresh = len(got)
        self.step += 1
        return self

    def hold(self, *arrays):
        old = self.terms[:len(self.terms) - self.fresh]
        vals = lax.optimization_barrier(tuple(x for x, _ in old) + arrays)
        self.terms = [(v, path) for v, (_, path) in zip(vals, old)] + self.terms[len(old):]
        return self

    def after(self, *others):
        return self.hold(*(x for f in others for x in f.out))


def before(x, *others):
    vals = [v for f in others for v in (f.out if isinstance(f, Routed) else [f])]
    res = lax.optimization_barrier((x, *vals))
    rest = list(res[1:])
    for f in others:
        if isinstance(f, Routed):
            f.out = [rest.pop(0) for _ in f.out]
        else:
            rest.pop(0)
    return res[0]


def join(x, other):
    a, b = x.astype(f32), other.astype(f32)
    lower = lax.axis_index("doc") == 0
    return jnp.concatenate([jnp.where(lower, a, b), jnp.where(lower, b, a)], axis=0)


def trade(x, mask):
    members = lax.axis_size("seg")
    return lax.ppermute(x, ("doc", "seg"), [(m, m ^ mask) for m in range(2 * members)])


def gather_start(x):
    Z1, Y = 8, lax.axis_size("seg")
    near, far, both = trade(x, Z1), trade(x, Y), trade(x, Y + Z1)
    mine, theirs = jnp.stack([x, near]), jnp.stack([far, both])
    lower = lax.axis_index("doc") == 0
    return jnp.stack([jnp.where(lower, mine, theirs), jnp.where(lower, theirs, mine)])


def gather_middle(x):
    X, Z0 = 2, 4
    return jnp.concatenate([x, trade(x, X), trade(x, Z0), trade(x, X + Z0)], axis=1)


def gather_end(x):
    return jnp.concatenate([x, trade(x, 1)], axis=1)


def shards(tokens, token_mask, doc_lengths, seg_qkv, seg_proj, seg_up, seg_down, seg_bias, seg_gains, seg_shifts,
           cross_qkv, cross_proj, cross_up, cross_down, cross_bias, cross_gains, cross_shifts, positions, cotangent):
    segs, L, D = tokens.shape
    F = seg_up.shape[1]
    members, member = lax.axis_size("seg"), lax.axis_index("seg")
    docs, doc = lax.axis_size("doc"), lax.axis_index("doc")
    r, wide, T = D // members, F // D, segs * L
    all_groups = docs * members * segs <= 256
    few = members == 16 and docs == 2
    place = (doc * members if few else doc * members + member if all_groups else member) * segs
    meta = jnp.stack([member, doc, jnp.int32(members), member & 1, place]).astype(jnp.int32)
    tok, cot = tokens.reshape(T, D), cotangent.reshape(T, D)
    bias, xbias = seg_bias.reshape(-1, 128), cross_bias.reshape(-1, 128)

    q, k, v, p, ob, n1, inv1, dg, gr2, mixed, pack, small_f, *gw_d = forward(
        meta, doc_lengths, tok, cot, token_mask, seg_qkv, seg_proj, seg_up, seg_down, bias, seg_gains, seg_shifts, members)
    routed = few and len(gw_d) == 2
    pack = pack.reshape(segs, -1)
    if few:
        pack = gather_start(pack)
    if routed:
        fold_d = Routed(*gw_d).go()
        inv1 = before(inv1, pack)
    gr1, gbias, small_b, *gw_u = ffn_back(meta, n1, inv1, dg, gr2, seg_up, seg_down, seg_gains, seg_shifts, members)
    if few:
        rows = gather_middle(pack)
    if routed:
        gw_u[0] = before(gw_u[0], fold_d.ready(), rows)
        fold_u = Routed(*gw_u).go()
    if few:
        rows = gather_end(rows).reshape(docs * members * segs, -1)
    else:
        rows = lax.all_gather(pack, ("doc", "seg") if all_groups else ("seg",), axis=0, tiled=True)
    if routed:
        rows = before(rows, fold_d)
        fold_d.go()
    mixed, gr1c, svec, *sums = cross(
        meta, rows, mixed, (seg_up, seg_down, bias, seg_gains, seg_shifts),
        (cross_qkv, cross_proj, cross_up, cross_down, xbias, cross_gains, cross_shifts), positions, segs, r)
    if routed:
        gr1c = before(gr1c, fold_d.ready(), fold_u.ready())
        fold_d.go()
        fold_u.go()
    qk0, ga, first_v, sums_a, *gw_a = attn_back(meta, (gr1, gr1c, ob), p, q, k, v, tok, seg_proj, members, False)
    if routed:
        gw_a[0] = before(gw_a[0], fold_d.ready(), fold_u.ready())
        ga = before(ga, fold_d, fold_u)
        fold_a = Routed(*gw_a).go()
        fold_d.go()
        fold_u.go()
    qk1, vv, vec, *gw_b = attn_back(meta, (first_v, small_f, small_b, sums_a, gbias, ga), p, q, k, v, tok, seg_proj, members, True)
    if routed:
        gw_b[0] = before(gw_b[0], fold_a.ready(), fold_d.ready(), fold_u.ready())
        fold_b = Routed(*gw_b).go()
        for f in (fold_a, fold_d, fold_u):
            f.go()

    if not all_groups:
        sums, svec = [over_docs(s.astype(bf16)) for s in sums], over_docs(svec.astype(bf16))
    gxqkv, gxo, gxu, gxd, gxbias, gxgains, gxshifts, gpos, gsu, gsd = sums

    if routed:
        gh = input_grad(gr1, gr1c, qk0, qk1, vv, seg_qkv)
        fold_b.hold(gh)
        for m in range(3):
            fold_b.ready()
            fold_a.after(fold_b)
            fold_b.go()
            fold_a.ready()
            fold_b.after(fold_a)
            fold_a.go()
        fold_b.ready().go()
        fold_u.ready().go()
        sum_d, sum_u = join(*fold_d.x), join(*fold_u.x)
        parts = fold_a.x + fold_b.x
    else:
        def whole_pieces(g, tall=False):
            if len(g) == 1:
                return g[0].reshape(members, -1, D) if tall else g[0].reshape(-1, members, r, D).swapaxes(0, 1).reshape(members, -1, D)
            send, keep = g
            c = member & 1
            first, second = jnp.where(c == 0, keep, send), jnp.where(c == 0, send, keep)
            if members > 4:
                apart = lambda x: x.reshape((2, -1, 2) + x.shape[1:])
                first = jnp.moveaxis(apart(first), 0, 2).reshape(first.shape)
                second = apart(second).swapaxes(0, 1).reshape(second.shape)
            both = jnp.stack([first, second], axis=1)
            return both.reshape(members, -1, D)

        pieces = [whole_pieces(gw_d, True)] + [whole_pieces(g) for g in (gw_u, gw_a, gw_b)]
        if len(gw_b) == 1:
            tail = jnp.broadcast_to(vec.astype(bf16)[None], (members, SMALL_ROWS, D))
            pieces[3] = jnp.concatenate([pieces[3], tail], axis=1)
        sum_d, sum_u, *parts = [over_docs(fold(x, members, member)) for x in pieces]
    if not routed:
        gh = input_grad(gr1, gr1c, qk0, qk1, vv, seg_qkv)
    gqkv, go, gb, gg, gs = finish(meta, parts, svec, r, F, routed)
    up = sum_u.reshape(wide, r, D).swapaxes(0, 1).reshape(r, F) + gsu
    return (
        mixed.reshape(segs, L, D), gh.reshape(segs, L, D),
        gqkv, go, up, sum_d + gsd, gb.reshape(-1), gg, gs,
        gxqkv, gxo, gxu, gxd, gxbias.reshape(-1), gxgains, gxshifts, gpos,
    )


def solution(mesh):
    rows, seg, copied = P("doc", "seg", None), P("seg", None), P()
    grads = (P(None, "seg", None), seg, seg, seg, P("seg"), P(None, "seg"), P(None, "seg"))
    return jax.shard_map(
        shards,
        mesh=mesh,
        in_specs=(rows, P("doc", "seg"), P("doc", None)) + (copied,) * 15 + (rows,),
        out_specs=(rows, rows) + grads + grads + (P(None, "seg"),),
        check_vma=False,
    )
```
